32 devices in a mesh: parts: 2 (over x), row: 16 (over z, y, core).
Axes of the slice: x: 2, y: 2, z: 4, core: 2. Of those that a mesh axis runs over, the one named last changes fastest.
Arguments:
- features: bfloat16 [16384, 128], P(('parts', 'row')), parts along dimension 0, may hold values from -6 to 6
- tiles: bfloat16 [1920, 128, 128], P(('parts', 'row')), parts along dimension 0, as said below
- tile_row: int32 [1920], P(('parts', 'row')), parts along dimension 0, may hold values from 0 to 63, as said below
- tile_col: int32 [1920], P(('parts', 'row')), parts along dimension 0, may hold values from -1 to 63, as said below
- degree: int32 [16384], P(('parts', 'row')), parts along dimension 0, may hold values from 16 to 64
- train_mask: int32 [16384], P(('parts', 'row')), parts along dimension 0, may hold values 0 or 1
- w_self: bfloat16 [128, 256], replicated, may hold values from -0.5 to 0.5
- w_neigh: bfloat16 [128, 256], replicated, may hold values from -0.5 to 0.5
- cotangent: bfloat16 [16384, 256], P(('parts', 'row')), parts along dimension 0, may hold values from -6 to 6
Outputs:
- embedded: bfloat16 [16384, 256], P(('parts', 'row')), parts along dimension 0
- grad_input: bfloat16 [16384, 128], P(('parts', 'row')), parts along dimension 0
- grad_self: float32 [256, 256], P('parts'), parts along dimension 0
- grad_neigh: float32 [256, 256], P('parts'), parts along dimension 0
The draws below stay inside these ranges and needn't reach their ends.
There are 2 independent parts, one for each index of `parts`. The reference program is written for one: setup_inputs(seed, part) draws one part's arguments, and reference() takes and returns one part's arrays. A program takes and returns all parts, laid end to end along the dimension named above; an argument that names none is the same for every part. Nothing has to cross between parts.
Inputs may be any that keep to these rules, and one draw needn't show every extreme that they name: `tile_row`: the tile slots of the device that holds nodes 128 b to 128 b + 127 name only row blocks of that device's 512 // 128 blocks. `tile_col`: -1 marks an empty slot; empty slots stand after the live ones of a device; every device has 30 live slots or more, and in every draw some device has all its slots live. The live slots of one device name column blocks held by any one other device at most 4 times, and in every draw some device does so exactly 4 times. A pair of blocks may appear in several slots. `tiles`: nonnegative edge weights.
All inputs are finite; a program needn't handle non-finite values. No bound on the sum of `train_mask` on one device may be relied on, other than what follows from the above.
Results may differ from the reference program's by a relative error of at most 0.0029.
Values may be sent and summed in bfloat16 or wider, within the bound.
No kernel may reach another device: no remote copies, remote signals or barrier semaphores. Data moves between devices by JAX's collectives and lax.ppermute only.
A program may use at most 128 MiB of HBM per device.

```python
import jax
import jax.numpy as jnp
from jax import lax

F_IN = 128
F = 256
NODE_DEV = 512
TILES_DEV = 60
NODES = 8192
TILES = 960
CAP = 4


def tile_layout(key):
    block_local = NODE_DEV // 128
    device_total = TILES // TILES_DEV
    keys = jax.random.split(key, 8)
    device = jnp.arange(TILES, dtype=jnp.int32) // TILES_DEV
    slot_index = jnp.arange(TILES, dtype=jnp.int32) % TILES_DEV
    row_block = device * block_local + jax.random.randint(keys[0], (TILES,), 0, block_local)
    live_count = jax.random.randint(keys[1], (device_total,), TILES_DEV // 2, TILES_DEV + 1)
    busiest = jax.random.randint(keys[2], (), 0, device_total)
    is_busy = device == busiest
    live_count = jnp.where(jnp.arange(device_total) == busiest, TILES_DEV, live_count)
    is_live = slot_index < live_count[device]
    remote = (jax.random.randint(keys[3], (TILES,), 0, 8) != 0) | is_busy & (slot_index < CAP)
    spots = CAP * (device_total - 1)
    order = jax.vmap(lambda sub: jax.random.permutation(sub, spots))(jax.random.split(keys[4], device_total))
    offset = (order[:, :TILES_DEV] // CAP).reshape(TILES).astype(jnp.int32)
    turn = jax.random.randint(keys[5], (), 0, device_total - 1)
    offset = jnp.where(is_busy, (slot_index // CAP + turn) % (device_total - 1), offset)
    owner = (device + 1 + offset) % device_total
    home_col = device * block_local + jax.random.randint(keys[6], (TILES,), 0, block_local)
    far_col = owner * block_local + jax.random.randint(keys[7], (TILES,), 0, block_local)
    col_block = jnp.where(remote, far_col, home_col)
    col_block = jnp.where(is_live, col_block, -1)
    return (row_block.astype(jnp.int32), col_block.astype(jnp.int32))


def draw_tile_row(key, part):
    return tile_layout(key)[0]


def draw_tile_col(key, part):
    return tile_layout(key)[1]


def draw_tiles(key, part):
    key = jax.random.fold_in(key, 11)
    key_mask, key_value = jax.random.split(key)
    present = jax.random.uniform(key_mask, (TILES, 128, 128)) < 0.03125
    value = jax.random.uniform(key_value, (TILES, 128, 128), minval=1.0, maxval=3.0)
    return jnp.where(present, value, 0.0).astype(jnp.float32).astype(jnp.bfloat16)


def touch_ends(result, key, low, largest):
    spot = [jax.random.randint(jax.random.fold_in(key, axis), (), 0, length) for axis, length in enumerate(result.shape)]
    longest = result.shape.index(max(result.shape))
    next_to = spot[:longest] + [(spot[longest] + 1) % result.shape[longest]] + spot[longest + 1:]
    return result.at[tuple(spot)].set(low).at[tuple(next_to)].set(largest)


def level_of(rng, dims, cuts, low, top_value):
    def one(position, blocks):
        steps = jax.random.uniform(jax.random.fold_in(jax.random.fold_in(rng, 6), position), (blocks,), jnp.float32, low / len(cuts), top_value / len(cuts))
        return jnp.repeat(jnp.exp(steps), dims[position] // blocks).reshape((-1,) + (1,) * (len(dims) - position - 1))

    loudness = one(*cuts[0])
    for cut in cuts[1:]:
        loudness = loudness * one(*cut)
    return loudness


def gaussian(key, extent, deviation, limit, cuts=(), kind=jnp.bfloat16):
    level = level_of(key, extent, cuts, -0.22, 0.18) if cuts else 1.0
    drawn = jax.random.normal(key, extent, jnp.float32) * deviation * level
    return jnp.minimum(jnp.maximum(drawn, -limit), limit).astype(kind)


def setup_inputs(seed: int = 0, part: int = 0) -> dict:
    seeds = jax.random.split(jax.random.key(seed), 10)
    part_keys = jax.random.split(jax.random.fold_in(seeds[9], part), 10)
    return {
        "features": gaussian(part_keys[0], (NODES, F_IN), 1.0, 6.0, ((0, 16),)),
        "tiles": draw_tiles(jax.random.fold_in(jax.random.fold_in(seeds[9], part), 71), part),
        "tile_row": draw_tile_row(jax.random.fold_in(jax.random.fold_in(seeds[9], part), 71), part),
        "tile_col": draw_tile_col(jax.random.fold_in(jax.random.fold_in(seeds[9], part), 71), part),
        "degree": touch_ends(jax.random.randint(part_keys[4], (NODES,), 16, 65), jax.random.fold_in(part_keys[4], 1), 16, 64).astype(jnp.int32),
        "train_mask": touch_ends((jax.random.randint(part_keys[5], (NODES,), 0, 2) < 1).astype(jnp.int32), jax.random.fold_in(part_keys[5], 1), 0, 1),
        "w_self": gaussian(seeds[6], (F_IN, F), F_IN ** -0.5, 0.5),
        "w_neigh": gaussian(seeds[7], (F_IN, F), F_IN ** -0.5, 0.5),
        "cotangent": gaussian(part_keys[8], (NODES, F), 1.0, 6.0, ((0, 16),)),
    }


def reference(features, tiles, tile_row, tile_col, degree, train_mask, w_self, w_neigh, cotangent):
    block_total = NODES // 128
    device_total = TILES // TILES_DEV
    is_live = tile_col >= 0
    col_block = jnp.where(is_live, tile_col, 0).astype(jnp.int32).reshape(device_total, TILES_DEV)
    row_block = tile_row.astype(jnp.int32).reshape(device_total, TILES_DEV)
    live_weight = jnp.where(is_live, 1.0, 0.0).astype(jnp.float32).reshape(device_total, TILES_DEV)
    grouped = tiles.reshape(device_total, TILES_DEV, 128, 128)
    feature_blocks = features.astype(jnp.float32).reshape(block_total, 128, F_IN)

    def forward_step(carry, item):
        slab, rblk, cblk, weight = item
        slab = slab.astype(jnp.float32) * weight[:, None, None]
        picked = feature_blocks[cblk]
        contrib = jnp.einsum("tij,tjf->tif", slab, picked, precision=lax.Precision.HIGHEST)
        return carry.at[rblk].add(contrib), None

    raw, _ = lax.scan(forward_step, jnp.zeros((block_total, 128, F_IN), jnp.float32),
                      (grouped, row_block, col_block, live_weight))
    raw = raw.reshape(NODES, F_IN)
    scaled_degree = degree.astype(jnp.float32)[:, None]
    neighbour_mean = raw / scaled_degree
    pre_act = jnp.dot(features, w_self, preferred_element_type=jnp.float32) + jnp.dot(
        neighbour_mean, w_neigh.astype(jnp.float32), precision=lax.Precision.HIGHEST)
    sigmoid_val = jax.nn.sigmoid(pre_act)
    embedded = (pre_act * sigmoid_val).astype(jnp.bfloat16)
    upstream = cotangent.astype(jnp.float32) * train_mask.astype(jnp.float32)[:, None]
    grad_pre = upstream * sigmoid_val * (1.0 + pre_act * (1.0 - sigmoid_val))
    scaled_grad = (grad_pre / scaled_degree).astype(jnp.bfloat16)
    grad_blocks = scaled_grad.astype(jnp.float32).reshape(block_total, 128, F)

    def backward_step(carry, item):
        slab, rblk, cblk, weight = item
        slab = slab.astype(jnp.float32) * weight[:, None, None]
        picked = grad_blocks[rblk]
        contrib = jnp.einsum("tji,tjf->tif", slab, picked, precision=lax.Precision.HIGHEST)
        return carry.at[cblk].add(contrib), None

    spread, _ = lax.scan(backward_step, jnp.zeros((block_total, 128, F), jnp.float32),
                         (grouped, row_block, col_block, live_weight))
    spread = spread.reshape(NODES, F)
    feat_wide = features.astype(jnp.float32)
    grad_self = jnp.dot(feat_wide.T, grad_pre, precision=lax.Precision.HIGHEST)
    grad_neigh = jnp.dot(feat_wide.T, spread, precision=lax.Precision.HIGHEST)
    grad_input = (jnp.dot(grad_pre, w_self.astype(jnp.float32).T, precision=lax.Precision.HIGHEST)
                  + jnp.dot(spread, w_neigh.astype(jnp.float32).T, precision=lax.Precision.HIGHEST)).astype(jnp.bfloat16)
    return embedded, grad_input, grad_self, grad_neigh
```

```python
import functools

import jax
import jax.numpy as jnp
from jax import lax
from jax.experimental import pallas as pl
from jax.experimental.pallas import tpu as pltpu
from jax.sharding import PartitionSpec as P

BLOCK = 128
F32, BF16 = jnp.float32, jnp.bfloat16
VMEM = pl.BlockSpec(memory_space=pltpu.VMEM)
SMEM = pl.BlockSpec(memory_space=pltpu.SMEM)
ANY = pl.BlockSpec(memory_space=pl.ANY)
VMEM_LIMIT = 56 * 1024 * 1024


def swap(x, n, offset):
    return lax.ppermute(x, "row", [(i, i ^ offset) for i in range(n)])


def gather_by_xor(x, n):
    blocks = {0: x}
    bits = [1 << b for b in range(n.bit_length() - 2, -1, -1)]
    while bits:
        if len(bits) >= 4:
            hi, lo, bits = bits[0], bits[1], bits[2:]
            offsets = (hi, lo, hi | lo)
        else:
            offsets, bits = (bits[0],), bits[1:]
        blocks |= {k ^ o: swap(v, n, o) for o in offsets for k, v in blocks.items()}
    return [blocks[k] for k in range(n)]


def split_bf16(x):
    high = x.astype(BF16)
    return high, (x - high.astype(F32)).astype(BF16)


def dot(a, b, dims=((1,), (0,))):
    return lax.dot_general(a, b, (dims, ((), ())), preferred_element_type=F32)


def dot_wide(a, b, dims=((1,), (0,))):
    high, low = split_bf16(a)
    return dot(high, b, dims) + dot(low, b, dims)


def rows_to_lanes(row):
    return jnp.transpose(jnp.broadcast_to(row, (BLOCK, BLOCK)))


def local_kernel(n, group, me_ref, trow_ref, tcol_ref, tiles_ref, deg_ref, mask_ref, ws_ref,
                 wn_ref, cot_ref, own_ref, *refs):
    feat_refs, refs = refs[:n], refs[n:]
    (emb_ref, base_ref, wkeep_ref, wsend_ref, keep_ref, send_ref,
     feats, raw, gt, acc, wsum, sem) = refs
    block_local = own_ref.shape[0] // BLOCK
    tile_count = tiles_ref.shape[0]
    me = me_ref[0]

    copies = [
        pltpu.make_async_copy(feat_refs[k], feats.at[pl.ds(k * block_local, block_local)],
                              sem.at[k])
        for k in range(n)
    ]
    for copy in copies:
        copy.start()
    raw[...] = jnp.zeros_like(raw)
    acc[...] = jnp.zeros_like(acc)
    for copy in copies:
        copy.wait()

    def place(t):
        col = tcol_ref[t]
        live = col >= 0
        col = jnp.maximum(col, 0)
        position = ((col // block_local) ^ me) * block_local + col % block_local
        row = jnp.clip(trow_ref[t] - me * block_local, 0, block_local - 1)
        return live, row, position

    def forward(step, carry):
        rows, products = [], []
        for u in range(group):
            t = step * group + u
            live, row, position = place(t)
            rows.append(jnp.where(live, row, block_local))
            products.append(dot(tiles_ref[t], feats[position]))
        for row, product in zip(rows, products):
            raw[row] += product
        return carry

    lax.fori_loop(0, tile_count // group, forward, 0)

    wn = wn_ref[...]
    ws = ws_ref[...]
    for b in range(block_local):
        span = pl.ds(b * BLOCK, BLOCK)
        degree = rows_to_lanes(deg_ref[pl.ds(b, 1), :].astype(F32))
        mask = rows_to_lanes(mask_ref[pl.ds(b, 1), :].astype(F32))
        degree2 = jnp.concatenate([degree, degree], axis=1)
        mask2 = jnp.concatenate([mask, mask], axis=1)
        feat = own_ref[span, :]
        raw_b = raw[b]
        pre = dot(feat, ws) + dot_wide(raw_b / degree, wn)
        sig = jax.nn.sigmoid(pre)
        emb_ref[span, :] = (pre * sig).astype(BF16)
        upstream = cot_ref[span, :].astype(F32) * mask2
        grad_pre = upstream * sig * (1.0 + pre * (1.0 - sig))
        scaled = (grad_pre / degree2).astype(BF16)
        gp_high, gp_low = split_bf16(grad_pre)
        feat_t = jnp.transpose(feat.astype(F32)).astype(BF16)
        grad_self = dot(feat_t, gp_high) + dot(feat_t, gp_low)
        grad_neigh = dot_wide(jnp.transpose(raw_b), scaled)
        if b == 0:
            wsum[0], wsum[1] = grad_self, grad_neigh
        else:
            wsum[0] += grad_self
            wsum[1] += grad_neigh
        last = ((1,), (1,))
        base_ref[span, :] = dot(gp_high, ws, last) + dot(gp_low, ws, last)
        high, low = split_bf16(dot(wn, scaled, last))
        gt[b, :BLOCK, :] = high
        gt[b, BLOCK:, :] = low

    core = me % 2
    wkeep_ref[...] = wsum[core]
    wsend_ref[...] = wsum[1 - core]

    def backward(step, carry):
        places, products = [], []
        for u in range(group):
            t = step * group + u
            live, row, position = place(t)
            places.append(jnp.where(live, position, n * block_local))
            both = dot(gt[row], tiles_ref[t])
            products.append(both[:BLOCK] + both[BLOCK:])
        for position, product in zip(places, products):
            acc[position] += product
        return carry

    lax.fori_loop(0, tile_count // group, backward, 0)

    for k in range(n):
        for b in range(block_local):
            target = send_ref if k % 2 else keep_ref
            target[k // 2, pl.ds(b * BLOCK, BLOCK), :] = acc[k * block_local + b]


def pair_kernel(chips, keep_ref, got_ref, own_ref, *out_refs):
    own_ref[...] = keep_ref[0] + got_ref[0]
    for j in range(1, chips):
        out_refs[j - 1][...] = (keep_ref[j] + got_ref[j]).astype(BF16)


def last_kernel(chips, base_ref, own_ref, *refs):
    got_refs, out_ref = refs[:chips - 1], refs[chips - 1]
    for b in range(base_ref.shape[0] // BLOCK):
        span = pl.ds(b * BLOCK, BLOCK)
        total = own_ref[span, :]
        for got in got_refs:
            total = total + got[span, :].astype(F32)
        out_ref[span, :] = (base_ref[span, :] + jnp.transpose(total)).astype(BF16)


def body(features, tiles, tile_row, tile_col, degree, train_mask, w_self, w_neigh, cotangent):
    n = lax.axis_size("row")
    me = lax.axis_index("row")
    chips = n // 2
    nodes, feat_in = features.shape
    hidden = w_self.shape[1]
    block_local = nodes // BLOCK
    tile_count = tiles.shape[0]
    group = max(g for g in range(1, 7) if tile_count % g == 0)
    params = pltpu.CompilerParams(vmem_limit_bytes=VMEM_LIMIT)

    gathered = gather_by_xor(features, n)
    half = jax.ShapeDtypeStruct((chips, nodes, feat_in), F32)
    weight = jax.ShapeDtypeStruct((feat_in, hidden), F32)
    embedded, base, wkeep, wsend, keep, send = pl.pallas_call(
        functools.partial(local_kernel, n, group),
        out_shape=(
            jax.ShapeDtypeStruct((nodes, hidden), BF16),
            jax.ShapeDtypeStruct((nodes, feat_in), F32),
            weight, weight, half, half,
        ),
        in_specs=[SMEM] * 3 + [VMEM] * 7 + [ANY] * n,
        out_specs=(VMEM,) * 6,
        scratch_shapes=[
            pltpu.VMEM((n * block_local, BLOCK, feat_in), BF16),
            pltpu.VMEM((block_local + 1, BLOCK, feat_in), F32),
            pltpu.VMEM((block_local, 2 * feat_in, BLOCK), BF16),
            pltpu.VMEM((n * block_local + 1, feat_in, BLOCK), F32),
            pltpu.VMEM((2, feat_in, hidden), F32),
            pltpu.SemaphoreType.DMA((n,)),
        ],
        compiler_params=params,
        name="local_layer",
    )(
        me.astype(jnp.int32).reshape(1), tile_row, tile_col, tiles,
        degree.reshape(block_local, BLOCK), train_mask.reshape(block_local, BLOCK),
        w_self, w_neigh, cotangent, features,
        *[g.reshape(block_local, BLOCK, feat_in) for g in gathered],
    )

    got = swap(send, n, 1)
    own, *outgoing = pl.pallas_call(
        functools.partial(pair_kernel, chips),
        out_shape=[jax.ShapeDtypeStruct((nodes, feat_in), F32)]
        + [jax.ShapeDtypeStruct((nodes, feat_in), BF16)] * (chips - 1),
        in_specs=[VMEM] * 2,
        out_specs=[VMEM] * chips,
        compiler_params=params,
        name="pair_sum",
    )(keep, got)
    arrived = [swap(x, n, 2 * (j + 1)) for j, x in enumerate(outgoing)]

    groups = [[2 * i + c for i in range(chips)] for c in range(2)]

    def exchange(x):
        return lax.all_to_all(x, "row", 0, 0, axis_index_groups=groups, tiled=True)

    pair = (wkeep + swap(wsend, n, 1)).reshape(chips, feat_in // chips, hidden)
    chunk = jnp.sum(exchange(pair), axis=0)
    mine = exchange(jnp.broadcast_to(chunk[None], pair.shape)).reshape(feat_in, hidden)
    other = swap(mine, n, 1)
    first = me % 2 == 0
    grad_self = jnp.where(first, mine, other)
    grad_neigh = jnp.where(first, other, mine)

    grad_input = pl.pallas_call(
        functools.partial(last_kernel, chips),
        out_shape=jax.ShapeDtypeStruct((nodes, feat_in), BF16),
        in_specs=[VMEM] * (chips + 1),
        out_specs=VMEM,
        compiler_params=params,
        name="grad_input_sum",
    )(base, own, *arrived)
    return (embedded, grad_input, grad_self, grad_neigh)


def solution(mesh):
    placed = (
        P(("parts", "row"), None),
        P(("parts", "row"), None, None),
        P(("parts", "row")),
        P(("parts", "row")),
        P(("parts", "row")),
        P(("parts", "row")),
        P(),
        P(),
        P(("parts", "row"), None),
    )
    return jax.shard_map(
        body,
        mesh=mesh,
        in_specs=placed,
        out_specs=(
            P(("parts", "row"), None),
            P(("parts", "row"), None),
            P("parts", None),
            P("parts", None),
        ),
        check_vma=False,
    )
```

```python
import functools

import jax
import jax.numpy as jnp
from jax import lax
from jax.experimental import pallas as pl
from jax.experimental.pallas import tpu as pltpu
from jax.sharding import PartitionSpec as P

BLOCK = 128
F32, BF16 = jnp.float32, jnp.bfloat16
VMEM = pl.BlockSpec(memory_space=pltpu.VMEM)
SMEM = pl.BlockSpec(memory_space=pltpu.SMEM)
MIB = 1024 * 1024


def swap(x, n, offset):
    return lax.ppermute(x, "row", [(i, i ^ offset) for i in range(n)])


def gather_by_xor(x, n):
    blocks = {0: x}
    for bit in range(n.bit_length() - 2, -1, -1):
        blocks |= {k ^ (1 << bit): swap(v, n, 1 << bit) for k, v in blocks.items()}
    return [blocks[k] for k in range(n)]


def split_bf16(x):
    high = x.astype(BF16)
    return high, (x - high.astype(F32)).astype(BF16)


def dot(a, b, dims=((1,), (0,))):
    return lax.dot_general(a, b, (dims, ((), ())), preferred_element_type=F32)


def dot_wide(a, b, dims=((1,), (0,))):
    high, low = split_bf16(a)
    return dot(high, b, dims) + dot(low, b, dims)


def rows_to_lanes(row):
    return jnp.transpose(jnp.broadcast_to(row, (BLOCK, BLOCK)))


def place(t, n, block_local, me, trow_ref, tcol_ref):
    col = tcol_ref[t]
    live = col >= 0
    col = jnp.maximum(col, 0)
    position = ((col // block_local) ^ me) * block_local + col % block_local
    row = jnp.clip(trow_ref[t] - me * block_local, 0, block_local - 1)
    return live, row, position


def forward_kernel(n, group, me_ref, trow_ref, tcol_ref, tiles_ref, deg_ref, mask_ref, ws_ref,
                   wn_ref, cot_ref, *refs):
    feat_refs, refs = refs[:n], refs[n:]
    emb_ref, base_ref, wkeep_ref, wsend_ref, gt_ref, feats, raw, wsum = refs
    own_ref = feat_refs[0]
    block_local = own_ref.shape[0] // BLOCK
    tile_count = tiles_ref.shape[0]
    me = me_ref[0]

    raw[...] = jnp.zeros_like(raw)
    for k in range(n):
        for b in range(block_local):
            feats[k * block_local + b] = feat_refs[k][pl.ds(b * BLOCK, BLOCK), :]

    def forward(step, carry):
        rows, products = [], []
        for u in range(group):
            t = step * group + u
            live, row, position = place(t, n, block_local, me, trow_ref, tcol_ref)
            rows.append(jnp.where(live, row, block_local))
            products.append(dot(tiles_ref[t], feats[position]))
        for row, product in zip(rows, products):
            raw[row] += product
        return carry

    lax.fori_loop(0, tile_count // group, forward, 0)

    wn = wn_ref[...]
    ws = ws_ref[...]
    for b in range(block_local):
        span = pl.ds(b * BLOCK, BLOCK)
        degree = rows_to_lanes(deg_ref[pl.ds(b, 1), :].astype(F32))
        mask = rows_to_lanes(mask_ref[pl.ds(b, 1), :].astype(F32))
        degree2 = jnp.concatenate([degree, degree], axis=1)
        mask2 = jnp.concatenate([mask, mask], axis=1)
        feat = own_ref[span, :]
        raw_b = raw[b]
        pre = dot(feat, ws) + dot_wide(raw_b / degree, wn)
        sig = jax.nn.sigmoid(pre)
        emb_ref[span, :] = (pre * sig).astype(BF16)
        upstream = cot_ref[span, :].astype(F32) * mask2
        grad_pre = upstream * sig * (1.0 + pre * (1.0 - sig))
        scaled = (grad_pre / degree2).astype(BF16)
        gp_high, gp_low = split_bf16(grad_pre)
        feat_t = jnp.transpose(feat.astype(F32)).astype(BF16)
        grad_self = dot(feat_t, gp_high) + dot(feat_t, gp_low)
        grad_neigh = dot_wide(jnp.transpose(raw_b), scaled)
        if b == 0:
            wsum[0], wsum[1] = grad_self, grad_neigh
        else:
            wsum[0] += grad_self
            wsum[1] += grad_neigh
        last = ((1,), (1,))
        base_ref[span, :] = dot(gp_high, ws, last) + dot(gp_low, ws, last)
        high, low = split_bf16(dot(wn, scaled, last))
        gt_ref[b, :BLOCK, :] = high
        gt_ref[b, BLOCK:, :] = low

    core = me % 2
    wkeep_ref[...] = wsum[core]
    wsend_ref[...] = wsum[1 - core]


def backward_kernel(n, group, me_ref, trow_ref, tcol_ref, tiles_ref, gt_ref,
                    send_odd_ref, send_even_ref, keep_odd_ref, keep_even_ref, acc):
    block_local = gt_ref.shape[0]
    tile_count = tiles_ref.shape[0]
    me = me_ref[0]
    acc[...] = jnp.zeros_like(acc)

    def backward(step, carry):
        places, products = [], []
        for u in range(group):
            t = step * group + u
            live, row, position = place(t, n, block_local, me, trow_ref, tcol_ref)
            places.append(jnp.where(live, position, n * block_local))
            both = dot(gt_ref[row], tiles_ref[t])
            products.append(both[:BLOCK] + both[BLOCK:])
        for position, product in zip(places, products):
            acc[position] += product
        return carry

    lax.fori_loop(0, tile_count // group, backward, 0)

    targets = ((keep_even_ref, keep_odd_ref), (send_even_ref, send_odd_ref))
    for k in range(n):
        j = k // 2
        for b in range(block_local):
            targets[k % 2][j % 2][j // 2, pl.ds(b * BLOCK, BLOCK), :] = acc[k * block_local + b]


def odd_kernel(count, keep_ref, got_ref, *out_refs):
    for j in range(count):
        out_refs[j][...] = (keep_ref[j] + got_ref[j]).astype(BF16)


def even_kernel(count, keep_ref, got_ref, *out_refs):
    for j in range(count):
        out_refs[j][...] = keep_ref[j] + got_ref[j]


def add_kernel(own_ref, got_ref, out_ref):
    out_ref[...] = (own_ref[...] + got_ref[...].astype(F32)).astype(BF16)


def last_kernel(count, base_ref, own_ref, *refs):
    got_refs, out_ref = refs[:count], refs[count]
    for b in range(base_ref.shape[0] // BLOCK):
        span = pl.ds(b * BLOCK, BLOCK)
        total = own_ref[span, :]
        for got in got_refs:
            total = total + got[span, :].astype(F32)
        out_ref[span, :] = (base_ref[span, :] + jnp.transpose(total)).astype(BF16)


def body(features, tiles, tile_row, tile_col, degree, train_mask, w_self, w_neigh, cotangent):
    n = lax.axis_size("row")
    me = lax.axis_index("row")
    lines = n // 4
    nodes, feat_in = features.shape
    hidden = w_self.shape[1]
    block_local = nodes // BLOCK
    tile_count = tiles.shape[0]
    group = max(g for g in range(1, 7) if tile_count % g == 0)
    small = n * nodes * feat_in * 4 <= 4 * MIB
    limit = (24 if small else 56) * MIB

    def near(x):
        return pltpu.with_memory_space_constraint(x, pltpu.VMEM) if small else x

    def result(shape, dtype, stays=True):
        kind = pltpu.VMEM if small and stays else jax.ShapeDtypeStruct
        return kind(shape, dtype)

    def call(kernel, name, out_shape, scalars, arrays, scratch=()):
        return pl.pallas_call(
            kernel,
            out_shape=out_shape,
            in_specs=[SMEM] * len(scalars) + [VMEM] * len(arrays),
            out_specs=jax.tree.map(lambda _: VMEM, out_shape),
            scratch_shapes=list(scratch),
            compiler_params=pltpu.CompilerParams(vmem_limit_bytes=limit),
            name=name,
        )(*scalars, *[near(x) for x in arrays])

    scalars = (me.astype(jnp.int32).reshape(1), tile_row, tile_col)
    gathered = gather_by_xor(features, n)
    embedded, base, wkeep, wsend, gt = call(
        functools.partial(forward_kernel, n, group),
        "forward_layer",
        (
            result((nodes, hidden), BF16, False),
            result((nodes, feat_in), F32),
            result((feat_in, hidden), F32),
            result((feat_in, hidden), F32),
            result((block_local, 2 * feat_in, BLOCK), BF16),
        ),
        scalars,
        (
            tiles, degree.reshape(block_local, BLOCK), train_mask.reshape(block_local, BLOCK),
            w_self, w_neigh, cotangent, *gathered,
        ),
        [
            pltpu.VMEM((n * block_local, BLOCK, feat_in), BF16),
            pltpu.VMEM((block_local + 1, BLOCK, feat_in), F32),
            pltpu.VMEM((2, feat_in, hidden), F32),
        ],
    )

    quarter = result((lines, nodes, feat_in), F32)
    send_odd, send_even, keep_odd, keep_even = call(
        functools.partial(backward_kernel, n, group),
        "backward_tiles",
        (quarter,) * 4,
        scalars,
        (tiles, gt),
        [pltpu.VMEM((n * block_local + 1, feat_in, BLOCK), F32)],
    )

    piece = result((nodes, feat_in), BF16)
    wide = result((nodes, feat_in), F32)
    to_y = call(
        functools.partial(odd_kernel, lines), "pair_sum_y", (piece,) * lines, (),
        (keep_odd, swap(send_odd, n, 1)),
    )
    from_y = [swap(x, n, 2) for x in to_y]
    here = call(
        functools.partial(even_kernel, lines), "pair_sum_z", (wide,) * lines, (),
        (keep_even, swap(send_even, n, 1)),
    )
    from_z = []
    for line in range(lines - 1, 0, -1):
        total = call(add_kernel, "line_sum", piece, (), (here[line], from_y[line]))
        from_z.append(swap(total, n, 4 * line))

    mine = wkeep + swap(wsend, n, 1)
    for bit in range(1, n.bit_length() - 1):
        mine = mine + swap(mine, n, 1 << bit)
    other = swap(mine, n, 1)
    first = me % 2 == 0
    grad_self = jnp.where(first, mine, other)
    grad_neigh = jnp.where(first, other, mine)

    grad_input = call(
        functools.partial(last_kernel, lines), "grad_input_sum",
        result((nodes, feat_in), BF16, False), (),
        (base, here[0], from_y[0], *from_z),
    )
    return (embedded, grad_input, grad_self, grad_neigh)


def solution(mesh):
    placed = (
        P(("parts", "row"), None),
        P(("parts", "row"), None, None),
        P(("parts", "row")),
        P(("parts", "row")),
        P(("parts", "row")),
        P(("parts", "row")),
        P(),
        P(),
        P(("parts", "row"), None),
    )
    return jax.shard_map(
        body,
        mesh=mesh,
        in_specs=placed,
        out_specs=(
            P(("parts", "row"), None),
            P(("parts", "row"), None),
            P("parts", None),
            P("parts", None),
        ),
        check_vma=False,
    )
```

```python
import functools

import jax
import jax.numpy as jnp
from jax import lax
from jax.experimental import pallas as pl
from jax.experimental.pallas import tpu as pltpu
from jax.sharding import PartitionSpec as P

BLOCK = 128
F32, BF16 = jnp.float32, jnp.bfloat16
VMEM = pl.BlockSpec(memory_space=pltpu.VMEM)
SMEM = pl.BlockSpec(memory_space=pltpu.SMEM)
ANY = pl.BlockSpec(memory_space=pl.ANY)
MIB = 1024 * 1024
LAST = ((1,), (1,))


def swap(x, n, offset):
    return lax.ppermute(x, "row", [(i, i ^ offset) for i in range(n)])


def gather_by_xor(x, n, call, pack):
    blocks = [x]
    bit = n // 2
    while bit >= 8:
        blocks = blocks + [swap(v, n, bit) for v in blocks]
        bit //= 2
    offsets = [0]
    bit = n // 2
    while bit >= 8:
        offsets = offsets + [o ^ bit for o in offsets]
        bit //= 2
    blocks = [v for _, v in sorted(zip(offsets, blocks), key=lambda pair: pair[0])]
    same = []
    for v in blocks:
        square = (v, *[swap(v, n, offset) for offset in (2, 4, 6)])
        same.append(call(pack_kernel, "pack_square", pack, square))
    return same, [swap(v, n, 1) for v in same]


def split_bf16(x):
    high = x.astype(BF16)
    return high, (x - high.astype(F32)).astype(BF16)


def dot(a, b, dims=((1,), (0,))):
    return lax.dot_general(a, b, (dims, ((), ())), preferred_element_type=F32)


def dot_wide(a, b, dims=((1,), (0,))):
    high, low = split_bf16(a)
    return dot(high, b, dims) + dot(low, b, dims)


def rows_to_lanes(row):
    return jnp.transpose(jnp.broadcast_to(row, (BLOCK, BLOCK)))


def rows_of(b):
    return pl.ds(b * BLOCK, BLOCK)


def pack_kernel(*refs):
    for i, ref in enumerate(refs[:-1]):
        refs[-1][i] = ref[...]


def stage_kernel(me_ref, trow_ref, tcol_ref, deg_ref, mask_ref, ws_ref, wn_ref, feat_ref, cot_ref,
                 tiles_ref, tiles_out, ws_out, wn_out, deg_out, up_out, pre_out, featt_out,
                 index_out, sem):
    copy = pltpu.make_async_copy(tiles_ref, tiles_out, sem)
    copy.start()
    block_local = feat_ref.shape[0] // BLOCK
    tile_count = trow_ref.shape[0]
    me = me_ref[0]
    index_out[2 * tile_count] = me

    def place(t, carry):
        col = tcol_ref[t]
        live = col >= 0
        col = jnp.maximum(col, 0)
        position = ((col // block_local) ^ me) * block_local + col % block_local
        row = jnp.clip(trow_ref[t] - me * block_local, 0, block_local - 1)
        index_out[t] = jnp.where(live, row, block_local)
        index_out[tile_count + t] = position
        return carry

    lax.fori_loop(0, tile_count, place, 0)
    ws_out[...] = ws_ref[...]
    wn_out[...] = wn_ref[...]
    ws = ws_ref[...]
    for b in range(block_local):
        degree = rows_to_lanes(deg_ref[pl.ds(b, 1), :].astype(F32))
        mask = rows_to_lanes(mask_ref[pl.ds(b, 1), :].astype(F32))
        deg_out[b] = degree
        feat = feat_ref[rows_of(b), :]
        featt_out[b] = jnp.transpose(feat.astype(F32)).astype(BF16)
        pre_out[rows_of(b), :] = dot(feat, ws)
        up_out[rows_of(b), :] = cot_ref[rows_of(b), :].astype(F32) * jnp.concatenate(
            [mask, mask], axis=1)
    copy.wait()


def forward_kernel(n, group, index_ref, tiles_ref, ws_ref, wn_ref, deg_ref, up_ref, pre_ref,
                   featt_ref, *refs):
    squares = n // 8
    feat_refs, refs = refs[:2 * squares], refs[2 * squares:]
    emb_ref, base_ref, wkeep_ref, wsend_ref, gt_ref, feats, raw, wsum = refs
    block_local = deg_ref.shape[0]
    tile_count = tiles_ref.shape[0]

    raw[...] = jnp.zeros_like(raw)
    for s in range(squares):
        for q in range(4):
            for core in range(2):
                for b in range(block_local):
                    spot = (8 * s + 2 * q + core) * block_local + b
                    feats[spot] = feat_refs[core * squares + s][q, rows_of(b), :]

    def forward(step, carry):
        rows, products = [], []
        for u in range(group):
            t = step * group + u
            rows.append(index_ref[t])
            products.append(dot(tiles_ref[t], feats[index_ref[tile_count + t]]))
        for row, product in zip(rows, products):
            raw[row] += product
        return carry

    lax.fori_loop(0, tile_count // group, forward, 0)

    wn = wn_ref[...]
    ws = ws_ref[...]
    for b in range(block_local):
        degree = deg_ref[b]
        raw_b = raw[b]
        pre = pre_ref[rows_of(b), :] + dot_wide(raw_b / degree, wn)
        sig = jax.nn.sigmoid(pre)
        emb_ref[rows_of(b), :] = (pre * sig).astype(BF16)
        grad_pre = up_ref[rows_of(b), :] * sig * (1.0 + pre * (1.0 - sig))
        scaled = (grad_pre / jnp.concatenate([degree, degree], axis=1)).astype(BF16)
        gp_high, gp_low = split_bf16(grad_pre)
        feat_t = featt_ref[b]
        grad_self = dot(feat_t, gp_high) + dot(feat_t, gp_low)
        grad_neigh = dot_wide(jnp.transpose(raw_b), scaled)
        if b == 0:
            wsum[0], wsum[1] = grad_self, grad_neigh
        else:
            wsum[0] += grad_self
            wsum[1] += grad_neigh
        base_ref[rows_of(b), :] = dot(gp_high, ws, LAST) + dot(gp_low, ws, LAST)
        high, low = split_bf16(dot(wn, scaled, LAST))
        gt_ref[b, :BLOCK, :] = high
        gt_ref[b, BLOCK:, :] = low

    core = index_ref[2 * tile_count] % 2
    wkeep_ref[...] = wsum[core]
    wsend_ref[...] = wsum[1 - core]


def add_tiles(first, last, group, index_ref, tiles_ref, gt_ref, acc):
    block_local = gt_ref.shape[0]
    tile_count = tiles_ref.shape[0]
    dump = acc.shape[0] - 1

    def backward(step, carry):
        places, products = [], []
        for u in range(group):
            t = first + step * group + u
            row = index_ref[t]
            places.append(jnp.where(row < block_local, index_ref[tile_count + t], dump))
            both = dot(gt_ref[jnp.minimum(row, block_local - 1)], tiles_ref[t])
            products.append(both[:BLOCK] + both[BLOCK:])
        for position, product in zip(places, products):
            acc[position] += product
        return carry

    lax.fori_loop(0, (last - first) // group, backward, 0)


def backward_first_kernel(last, group, index_ref, tiles_ref, gt_ref, acc_ref):
    acc_ref[...] = jnp.zeros_like(acc_ref)
    add_tiles(0, last, group, index_ref, tiles_ref, gt_ref, acc_ref)


def backward_second_kernel(n, first, group, index_ref, tiles_ref, gt_ref, wkeep_ref, wgot_ref,
                           before_ref, *refs):
    far_send, near_send, far_keep, near_keep, w0, w1, w2, w3, acc = refs
    block_local = gt_ref.shape[0]
    tile_count = tiles_ref.shape[0]
    rows = w0.shape[0]
    chip = index_ref[2 * tile_count] // 2 % 4
    for p, ref in enumerate((w0, w1, w2, w3)):
        span = pl.ds(pl.multiple_of((chip ^ p) * rows, rows), rows)
        ref[...] = wkeep_ref[span, :] + wgot_ref[span, :]
    acc[...] = jnp.zeros_like(acc)
    add_tiles(first, tile_count, group, index_ref, tiles_ref, gt_ref, acc)
    for k in range(n):
        square, q = k // 8, k // 2 % 4
        near, far = (near_send, far_send) if k % 2 else (near_keep, far_keep)
        for b in range(block_local):
            spot = k * block_local + b
            total = acc[spot] + before_ref[spot]
            if square:
                far[square - 1, q, rows_of(b), :] = total
            else:
                near[0, q, rows_of(b), :] = total


def pair_kernel(squares, keep_ref, got_ref, *refs):
    for s in range(squares):
        refs[4 * s][...] = keep_ref[s, 0] + got_ref[s, 0]
        for q in range(1, 4):
            refs[4 * s + q][...] = (keep_ref[s, q] + got_ref[s, q]).astype(BF16)


def pair_far_kernel(squares, w0, w1, w2, w3, *refs):
    refs[-1][...] = (w0[...] + w1[...]) + (w2[...] + w3[...])
    pair_kernel(squares, *refs[:-1])


def add_kernel(own_ref, *refs):
    total = own_ref[...]
    for got_ref in refs[:-1]:
        total = total + got_ref[...].astype(F32)
    refs[-1][...] = total.astype(BF16)


def add_both_kernel(weight_ref, wgot_ref, own_ref, *refs):
    refs[-1][...] = weight_ref[...] + wgot_ref[...]
    add_kernel(own_ref, *refs[:-1])


def last_kernel(index_ref, weight_ref, other_ref, base_ref, own_ref, *refs):
    got_refs, (out_ref, self_ref, neigh_ref) = refs[:-3], refs[-3:]
    for b in range(base_ref.shape[0] // BLOCK):
        total = own_ref[rows_of(b), :]
        for got_ref in got_refs:
            total = total + got_ref[rows_of(b), :].astype(F32)
        out_ref[rows_of(b), :] = (base_ref[rows_of(b), :] + jnp.transpose(total)).astype(BF16)
    me = index_ref[index_ref.shape[0] - 1]
    first = me % 2 == 0
    chip = me // 2 % 4
    rows = weight_ref.shape[1]
    for p in range(4):
        span = pl.ds(pl.multiple_of((chip ^ p) * rows, rows), rows)
        mine, other = weight_ref[p], other_ref[p]
        self_ref[span, :] = jnp.where(first, mine, other)
        neigh_ref[span, :] = jnp.where(first, other, mine)


def body(features, tiles, tile_row, tile_col, degree, train_mask, w_self, w_neigh, cotangent):
    n = lax.axis_size("row")
    me = lax.axis_index("row").astype(jnp.int32).reshape(1)
    squares = n // 8
    nodes, feat_in = features.shape
    hidden = w_self.shape[1]
    block_local = nodes // BLOCK
    tile_count = tiles.shape[0]
    half = tile_count // 2
    group = max(g for g in range(1, 7) if half % g == 0)
    small = n * nodes * feat_in * 4 <= 4 * MIB
    limit = (24 if small else 56) * MIB

    def result(shape, dtype, stays=True):
        kind = pltpu.VMEM if small and stays else jax.ShapeDtypeStruct
        return kind(shape, dtype)

    def placed(x, spec):
        if spec is SMEM or not small:
            return x
        return pltpu.with_memory_space_constraint(x, pltpu.HBM if spec is ANY else pltpu.VMEM)

    def call(kernel, name, out_shape, operands, in_specs=None, out_specs=None, cost_us=0.2, **more):
        specs = in_specs or [VMEM] * len(operands)
        return pl.pallas_call(
            kernel,
            out_shape=out_shape,
            in_specs=specs,
            out_specs=out_specs or jax.tree.map(lambda _: VMEM, out_shape),
            compiler_params=pltpu.CompilerParams(vmem_limit_bytes=limit),
            cost_estimate=pl.CostEstimate(
                flops=0, bytes_accessed=int(cost_us * 3.6e6), transcendentals=0),
            name=name,
            **more,
        )(*[placed(x, spec) for x, spec in zip(operands, specs)])

    wide, piece = result((nodes, feat_in), F32), result((nodes, feat_in), BF16)
    weight = result((feat_in, hidden), F32)
    chunk = result((feat_in // 4, hidden), F32)
    by_block = (block_local, BLOCK, feat_in)

    own_arguments = (
        degree.reshape(block_local, BLOCK), train_mask.reshape(block_local, BLOCK),
        w_self, w_neigh, features, cotangent,
    )
    if small:
        own_arguments = [pltpu.with_memory_space_constraint(x, pltpu.HBM) for x in own_arguments]
    tiles_near, ws, wn, degree_wide, upstream, pre_self, feat_t, index = pl.pallas_call(
        stage_kernel,
        out_shape=(
            result(tiles.shape, BF16),
            result(w_self.shape, BF16),
            result(w_neigh.shape, BF16),
            result(by_block, F32),
            result((nodes, hidden), F32),
            result((nodes, hidden), F32),
            result(by_block, BF16),
            jax.ShapeDtypeStruct((2 * tile_count + 1,), jnp.int32),
        ),
        in_specs=[SMEM] * 3 + [VMEM] * 6 + [ANY],
        out_specs=(VMEM,) * 7 + (SMEM,),
        scratch_shapes=[pltpu.SemaphoreType.DMA],
        compiler_params=pltpu.CompilerParams(vmem_limit_bytes=limit),
        cost_estimate=pl.CostEstimate(flops=0, bytes_accessed=int(3 * 3.6e6), transcendentals=0),
        name="stage_arguments",
    )(me, tile_row, tile_col, *own_arguments, placed(tiles, ANY))

    same, other = gather_by_xor(features, n, call, result((4, nodes, feat_in), BF16))
    operands = (index, tiles_near, ws, wn, degree_wide, upstream, pre_self, feat_t, *same, *other)
    embedded, base, wkeep, wsend, gt = call(
        functools.partial(forward_kernel, n, group),
        "forward_layer",
        (
            result((nodes, hidden), BF16, False), wide, weight, weight,
            result((block_local, 2 * feat_in, BLOCK), BF16),
        ),
        operands,
        [SMEM] + [VMEM] * (len(operands) - 1),
        cost_us=5,
        scratch_shapes=[
            pltpu.VMEM((n * block_local, BLOCK, feat_in), BF16),
            pltpu.VMEM((block_local + 1, BLOCK, feat_in), F32),
            pltpu.VMEM((2, feat_in, hidden), F32),
        ],
    )

    wgot = swap(wsend, n, 1)
    acc_shape = (n * block_local + 1, feat_in, BLOCK)
    acc = call(
        functools.partial(backward_first_kernel, half, group),
        "backward_first", result(acc_shape, F32), (index, tiles_near, gt), [SMEM, VMEM, VMEM],
        cost_us=2.5,
    )
    far = result((max(squares - 1, 1), 4, nodes, feat_in), F32)
    near = result((1, 4, nodes, feat_in), F32)
    far_send, near_send, far_keep, near_keep, *w = call(
        functools.partial(backward_second_kernel, n, half, group),
        "backward_second", (far, near, far, near) + (chunk,) * 4,
        (index, tiles_near, gt, wkeep, wgot, acc), [SMEM] + [VMEM] * 5, cost_us=2.5,
        scratch_shapes=[pltpu.VMEM(acc_shape, F32)],
    )

    count = squares - 1
    *far_sums, wsum = call(
        functools.partial(pair_far_kernel, count), "pair_sum_far",
        (wide, piece, piece, piece) * count + (chunk,),
        (w[0], *[swap(w[p], n, 2 * p) for p in (1, 2, 3)], far_keep, swap(far_send, n, 1)),
    )
    near_sums = call(
        functools.partial(pair_kernel, 1), "pair_sum_near", (wide, piece, piece, piece),
        (near_keep, swap(near_send, n, 1)),
    )
    sums = [*near_sums, *far_sums]
    terms = [
        [sums[4 * s], *[swap(sums[4 * s + q], n, 2 * q) for q in (1, 2, 3)]]
        for s in range(squares)
    ]
    distance = 1
    while distance < squares:
        wgot = swap(wsum, n, 8 * distance)
        for s in range(squares - distance, 0, -2 * distance):
            if s == squares - distance:
                total, wsum = call(
                    add_both_kernel, "square_sum", (piece, chunk), (wsum, wgot, *terms[s]))
            else:
                total = call(add_kernel, "square_sum", piece, terms[s])
            terms[s - distance].append(swap(total, n, 8 * distance))
        distance *= 2

    mine = call(
        pack_kernel, "pack_weights", result((4, feat_in // 4, hidden), F32),
        (wsum, *[swap(wsum, n, 2 * p) for p in (1, 2, 3)]),
    )
    grad_input, grad_self, grad_neigh = call(
        last_kernel, "grad_input_sum",
        (
            result((nodes, feat_in), BF16, False), result((feat_in, hidden), F32, False),
            result((feat_in, hidden), F32, False),
        ),
        (index, mine, swap(mine, n, 1), base, *terms[0]),
        [SMEM] + [VMEM] * (3 + len(terms[0])),
    )
    return (embedded, grad_input, grad_self, grad_neigh)


def solution(mesh):
    placed = (
        P(("parts", "row"), None),
        P(("parts", "row"), None, None),
        P(("parts", "row")),
        P(("parts", "row")),
        P(("parts", "row")),
        P(("parts", "row")),
        P(),
        P(),
        P(("parts", "row"), None),
    )
    return jax.shard_map(
        body,
        mesh=mesh,
        in_specs=placed,
        out_specs=(
            P(("parts", "row"), None),
            P(("parts", "row"), None),
            P("parts", None),
            P("parts", None),
        ),
        check_vma=False,
    )
```

```python
import functools

import jax
import jax.numpy as jnp
from jax import lax
from jax.experimental import pallas as pl
from jax.experimental.pallas import tpu as pltpu
from jax.sharding import PartitionSpec as P

BLOCK = 128
F32, BF16 = jnp.float32, jnp.bfloat16
VMEM = pl.BlockSpec(memory_space=pltpu.VMEM)
SMEM = pl.BlockSpec(memory_space=pltpu.SMEM)
ANY = pl.BlockSpec(memory_space=pl.ANY)
MIB = 1024 * 1024
LAST = ((1,), (1,))
NEAR_COST, SQUARE_COST, WEIGHT_COST = 1, 4, 8


def swap(x, n, offset):
    return lax.ppermute(x, "row", [(i, i ^ offset) for i in range(n)])


def gather_by_xor(x, own, n, call, pack):
    blocks = [x]
    bit = n // 2
    while bit >= 8:
        blocks = blocks + [swap(v, n, bit) for v in blocks]
        bit //= 2
    offsets = [0]
    bit = n // 2
    while bit >= 8:
        offsets = offsets + [o ^ bit for o in offsets]
        bit //= 2
    blocks = [v for _, v in sorted(zip(offsets, blocks), key=lambda pair: pair[0])]
    same = []
    for v in blocks:
        square = (own if v is x else v, *[swap(v, n, offset) for offset in (2, 4, 6)])
        same.append(call(pack_kernel, "pack_square", pack, square))
    return same, [swap(v, n, 1) for v in same]


def split_bf16(x):
    high = x.astype(BF16)
    return high, (x - high.astype(F32)).astype(BF16)


def dot(a, b, dims=((1,), (0,))):
    return lax.dot_general(a, b, (dims, ((), ())), preferred_element_type=F32)


def dot_wide(a, b, dims=((1,), (0,))):
    high, low = split_bf16(a)
    return dot(high, b, dims) + dot(low, b, dims)


def rows_to_lanes(row):
    return jnp.transpose(jnp.broadcast_to(row, (BLOCK, BLOCK)))


def rows_of(b):
    return pl.ds(b * BLOCK, BLOCK)


def pack_kernel(*refs):
    for i, ref in enumerate(refs[:-1]):
        refs[-1][i] = ref[...]


def stage_kernel(me_ref, trow_ref, tcol_ref, deg_ref, mask_ref, ws_ref, wn_ref, feat_ref, cot_ref,
                 tiles_ref, tiles_out, ws_out, wn_out, deg_out, up_out, pre_out, featt_out,
                 own_out, index_out, sem):
    copy = pltpu.make_async_copy(tiles_ref, tiles_out, sem)
    copy.start()
    block_local = feat_ref.shape[0] // BLOCK
    tile_count = trow_ref.shape[0]
    me = me_ref[0]
    index_out[2 * tile_count] = me

    def place(t, carry):
        col = tcol_ref[t]
        live = col >= 0
        col = jnp.maximum(col, 0)
        position = ((col // block_local) ^ me) * block_local + col % block_local
        row = jnp.clip(trow_ref[t] - me * block_local, 0, block_local - 1)
        index_out[t] = jnp.where(live, row, block_local)
        index_out[tile_count + t] = position
        return carry

    lax.fori_loop(0, tile_count, place, 0)
    own_out[...] = feat_ref[...]
    ws_out[...] = ws_ref[...]
    wn_out[...] = wn_ref[...]
    ws = ws_ref[...]
    for b in range(block_local):
        degree = rows_to_lanes(deg_ref[pl.ds(b, 1), :].astype(F32))
        mask = rows_to_lanes(mask_ref[pl.ds(b, 1), :].astype(F32))
        deg_out[b] = degree
        feat = feat_ref[rows_of(b), :]
        featt_out[b] = jnp.transpose(feat.astype(F32)).astype(BF16)
        pre_out[rows_of(b), :] = dot(feat, ws)
        up_out[rows_of(b), :] = cot_ref[rows_of(b), :].astype(F32) * jnp.concatenate(
            [mask, mask], axis=1)
    copy.wait()


def forward_kernel(n, group, index_ref, tiles_ref, ws_ref, wn_ref, deg_ref, up_ref, pre_ref,
                   featt_ref, *refs):
    squares = n // 8
    feat_refs, refs = refs[:2 * squares], refs[2 * squares:]
    emb_ref, base_ref, wkeep_ref, wsend_ref, gt_ref, feats, raw, wsum = refs
    block_local = deg_ref.shape[0]
    tile_count = tiles_ref.shape[0]

    raw[...] = jnp.zeros_like(raw)
    for s in range(squares):
        for q in range(4):
            for core in range(2):
                for b in range(block_local):
                    spot = (8 * s + 2 * q + core) * block_local + b
                    feats[spot] = feat_refs[core * squares + s][q, rows_of(b), :]

    def forward(step, carry):
        rows, products = [], []
        for u in range(group):
            t = step * group + u
            rows.append(index_ref[t])
            products.append(dot(tiles_ref[t], feats[index_ref[tile_count + t]]))
        for row, product in zip(rows, products):
            raw[row] += product
        return carry

    lax.fori_loop(0, tile_count // group, forward, 0)

    wn = wn_ref[...]
    ws = ws_ref[...]
    for b in range(block_local):
        degree = deg_ref[b]
        raw_b = raw[b]
        pre = pre_ref[rows_of(b), :] + dot_wide(raw_b / degree, wn)
        sig = jax.nn.sigmoid(pre)
        emb_ref[rows_of(b), :] = (pre * sig).astype(BF16)
        grad_pre = up_ref[rows_of(b), :] * sig * (1.0 + pre * (1.0 - sig))
        scaled = (grad_pre / jnp.concatenate([degree, degree], axis=1)).astype(BF16)
        gp_high, gp_low = split_bf16(grad_pre)
        feat_t = featt_ref[b]
        grad_self = dot(feat_t, gp_high) + dot(feat_t, gp_low)
        grad_neigh = dot_wide(jnp.transpose(raw_b), scaled)
        if b == 0:
            wsum[0], wsum[1] = grad_self, grad_neigh
        else:
            wsum[0] += grad_self
            wsum[1] += grad_neigh
        base_ref[rows_of(b), :] = dot(gp_high, ws, LAST) + dot(gp_low, ws, LAST)
        high, low = split_bf16(dot(wn, scaled, LAST))
        gt_ref[b, :BLOCK, :] = high
        gt_ref[b, BLOCK:, :] = low

    core = index_ref[2 * tile_count] % 2
    wkeep_ref[...] = wsum[core]
    wsend_ref[...] = wsum[1 - core]


def backward_kernel(group, index_ref, tiles_ref, gt_ref, acc_ref):
    block_local = gt_ref.shape[0]
    tile_count = tiles_ref.shape[0]
    dump = acc_ref.shape[0] - 1
    acc_ref[...] = jnp.zeros_like(acc_ref)

    def backward(step, carry):
        places, products = [], []
        for u in range(group):
            t = step * group + u
            row = index_ref[t]
            places.append(jnp.where(row < block_local, index_ref[tile_count + t], dump))
            both = dot(gt_ref[jnp.minimum(row, block_local - 1)], tiles_ref[t])
            products.append(both[:BLOCK] + both[BLOCK:])
        for position, product in zip(places, products):
            acc_ref[position] += product
        return carry

    lax.fori_loop(0, tile_count // group, backward, 0)


def split_kernel(n, block_local, index_ref, acc_ref, wkeep_ref, wgot_ref, far_send, near_send,
                 far_keep, near_keep, *parts):
    rows = parts[0].shape[0]
    chip = index_ref[index_ref.shape[0] - 1] // 2 % 4
    for p, ref in enumerate(parts):
        span = pl.ds(pl.multiple_of((chip ^ p) * rows, rows), rows)
        ref[...] = wkeep_ref[span, :] + wgot_ref[span, :]
    for k in range(n):
        square, q = k // 8, k // 2 % 4
        near, far = (near_send, far_send) if k % 2 else (near_keep, far_keep)
        for b in range(block_local):
            total = acc_ref[k * block_local + b]
            if square:
                far[square - 1, q, rows_of(b), :] = total
            else:
                near[0, q, rows_of(b), :] = total


def pair_far_kernel(squares, keep_ref, got_ref, *refs):
    for s in range(squares):
        refs[4 * s][...] = keep_ref[s, 0] + got_ref[s, 0]
        for q in range(1, 4):
            refs[4 * s + q][...] = (keep_ref[s, q] + got_ref[s, q]).astype(BF16)


def pair_near_kernel(keep_ref, got_ref, weight_ref, wgot_ref, own_ref, weight_out, *pieces):
    nodes, lanes = own_ref.shape
    weight = weight_ref[...] + wgot_ref[...]
    rows = weight.shape[0]
    high, low = split_bf16(weight)
    weight_out[...] = high.astype(F32) + low.astype(F32)
    own_ref[...] = keep_ref[0, 0] + got_ref[0, 0]
    for q, ref in enumerate(pieces):
        ref[pl.ds(0, nodes), :] = (keep_ref[0, q + 1] + got_ref[0, q + 1]).astype(BF16)
        start = nodes
        for part in (high, low):
            for column in range(0, weight.shape[1], lanes):
                ref[pl.ds(start, rows), :] = part[:, column:column + lanes]
                start += rows


def add_four_kernel(w0, w1, w2, w3, after_ref, out_ref):
    del after_ref
    out_ref[...] = (w0[...] + w1[...]) + (w2[...] + w3[...])


def add_two_kernel(own_ref, got_ref, out_ref):
    out_ref[...] = own_ref[...] + got_ref[...]


def add_kernel(own_ref, *refs):
    total = own_ref[...]
    for got_ref in refs[:-1]:
        total = total + got_ref[...].astype(F32)
    refs[-1][...] = total.astype(BF16)


def near_kernel(base_ref, own_ref, weight_ref, g1, g2, g3, out_ref, weights_out):
    nodes, lanes = own_ref.shape
    for b in range(nodes // BLOCK):
        total = own_ref[rows_of(b), :]
        for got_ref in (g1, g2, g3):
            total = total + got_ref[rows_of(b), :].astype(F32)
        out_ref[rows_of(b), :] = base_ref[rows_of(b), :] + jnp.transpose(total)
    rows, columns = weight_ref.shape
    cuts = columns // lanes
    weights_out[0] = weight_ref[...]
    for q, ref in enumerate((g1, g2, g3)):
        for cut in range(cuts):
            high = ref[pl.ds(nodes + cut * rows, rows), :]
            low = ref[pl.ds(nodes + (cuts + cut) * rows, rows), :]
            weights_out[q + 1, :, pl.ds(cut * lanes, lanes)] = (
                high.astype(F32) + low.astype(F32))


def last_kernel(index_ref, weight_ref, other_ref, near_ref, *refs):
    got_refs, (out_ref, self_ref, neigh_ref) = refs[:-3], refs[-3:]
    for b in range(near_ref.shape[0] // BLOCK):
        total = got_refs[0][rows_of(b), :].astype(F32)
        for got_ref in got_refs[1:]:
            total = total + got_ref[rows_of(b), :].astype(F32)
        out_ref[rows_of(b), :] = (near_ref[rows_of(b), :] + jnp.transpose(total)).astype(BF16)
    me = index_ref[index_ref.shape[0] - 1]
    first = me % 2 == 0
    chip = me // 2 % 4
    rows = weight_ref.shape[1]
    for p in range(4):
        span = pl.ds(pl.multiple_of((chip ^ p) * rows, rows), rows)
        mine, other = weight_ref[p], other_ref[p]
        self_ref[span, :] = jnp.where(first, mine, other)
        neigh_ref[span, :] = jnp.where(first, other, mine)


def body(features, tiles, tile_row, tile_col, degree, train_mask, w_self, w_neigh, cotangent):
    n = lax.axis_size("row")
    me = lax.axis_index("row").astype(jnp.int32).reshape(1)
    squares = n // 8
    nodes, feat_in = features.shape
    hidden = w_self.shape[1]
    block_local = nodes // BLOCK
    tile_count = tiles.shape[0]
    group = max(g for g in range(1, 7) if tile_count % g == 0)
    small = n * nodes * feat_in * 4 <= 4 * MIB
    limit = (24 if small else 56) * MIB

    def result(shape, dtype, stays=True):
        kind = pltpu.VMEM if small and stays else jax.ShapeDtypeStruct
        return kind(shape, dtype)

    def placed(x, spec):
        if spec is SMEM or not small:
            return x
        return pltpu.with_memory_space_constraint(x, pltpu.HBM if spec is ANY else pltpu.VMEM)

    def call(kernel, name, out_shape, operands, in_specs=None, out_specs=None, cost_us=0.2, **more):
        specs = in_specs or [VMEM] * len(operands)
        return pl.pallas_call(
            kernel,
            out_shape=out_shape,
            in_specs=specs,
            out_specs=out_specs or jax.tree.map(lambda _: VMEM, out_shape),
            compiler_params=pltpu.CompilerParams(vmem_limit_bytes=limit),
            cost_estimate=pl.CostEstimate(
                flops=int(cost_us * 1.1e9), bytes_accessed=int(cost_us * 3.6e6), transcendentals=0),
            name=name,
            **more,
        )(*[placed(x, spec) for x, spec in zip(operands, specs)])

    wide, piece = result((nodes, feat_in), F32), result((nodes, feat_in), BF16)
    weight = result((feat_in, hidden), F32)
    chunk = result((feat_in // 4, hidden), F32)
    by_block = (block_local, BLOCK, feat_in)

    own_arguments = (
        degree.reshape(block_local, BLOCK), train_mask.reshape(block_local, BLOCK),
        w_self, w_neigh, features, cotangent,
    )
    if small:
        own_arguments = [pltpu.with_memory_space_constraint(x, pltpu.HBM) for x in own_arguments]
    tiles_near, ws, wn, degree_wide, upstream, pre_self, feat_t, own, index = pl.pallas_call(
        stage_kernel,
        out_shape=(
            result(tiles.shape, BF16),
            result(w_self.shape, BF16),
            result(w_neigh.shape, BF16),
            result(by_block, F32),
            result((nodes, hidden), F32),
            result((nodes, hidden), F32),
            result(by_block, BF16),
            piece,
            jax.ShapeDtypeStruct((2 * tile_count + 1,), jnp.int32),
        ),
        in_specs=[SMEM] * 3 + [VMEM] * 6 + [ANY],
        out_specs=(VMEM,) * 8 + (SMEM,),
        scratch_shapes=[pltpu.SemaphoreType.DMA],
        compiler_params=pltpu.CompilerParams(vmem_limit_bytes=limit),
        cost_estimate=pl.CostEstimate(flops=int(3 * 1.1e9), bytes_accessed=int(3 * 3.6e6), transcendentals=0),
        name="stage_arguments",
    )(me, tile_row, tile_col, *own_arguments, placed(tiles, ANY))

    same, other = gather_by_xor(features, own, n, call, result((4, nodes, feat_in), BF16))
    operands = (index, tiles_near, ws, wn, degree_wide, upstream, pre_self, feat_t, *same, *other)
    embedded, base, wkeep, wsend, gt = call(
        functools.partial(forward_kernel, n, group),
        "forward_layer",
        (
            result((nodes, hidden), BF16, False), wide, weight, weight,
            result((block_local, 2 * feat_in, BLOCK), BF16),
        ),
        operands,
        [SMEM] + [VMEM] * (len(operands) - 1),
        cost_us=5,
        scratch_shapes=[
            pltpu.VMEM((n * block_local, BLOCK, feat_in), BF16),
            pltpu.VMEM((block_local + 1, BLOCK, feat_in), F32),
            pltpu.VMEM((2, feat_in, hidden), F32),
        ],
    )

    acc_shape = result((n * block_local + 1, feat_in, BLOCK), F32)
    acc = call(
        functools.partial(backward_kernel, group), "backward_tiles", acc_shape,
        (index, tiles_near, gt), [SMEM, VMEM, VMEM], cost_us=3.5,
    )
    far = result((squares - 1, 4, nodes, feat_in), F32)
    near = result((1, 4, nodes, feat_in), F32)
    far_send, near_send, far_keep, near_keep, *parts = call(
        functools.partial(split_kernel, n, block_local), "split_sums",
        (far, near, far, near) + (chunk,) * 4,
        (index, acc, wkeep, swap(wsend, n, 1)), [SMEM] + [VMEM] * 3, cost_us=0.8,
    )

    far_sums = call(
        functools.partial(pair_far_kernel, squares - 1), "pair_sum_far",
        (wide, piece, piece, piece) * (squares - 1), (far_keep, swap(far_send, n, 1)),
    )
    wsum = call(
        add_four_kernel, "weight_square_sum", chunk,
        (parts[0], *[swap(parts[p], n, 2 * p) for p in (1, 2, 3)], far_sums[0]),
        cost_us=WEIGHT_COST,
    )
    bit = 8
    while 2 * bit < n:
        wsum = call(add_two_kernel, "weight_sum", chunk, (wsum, swap(wsum, n, bit)))
        bit *= 2
    extra = result((nodes + 2 * chunk.shape[0] * (hidden // feat_in), feat_in), BF16)
    near_own, wsum, *near_pieces = call(
        pair_near_kernel, "pair_sum_near", (wide, chunk, extra, extra, extra),
        (near_keep, swap(near_send, n, 1), wsum, swap(wsum, n, bit)),
    )
    near_sum, mine = call(
        near_kernel, "near_sum", (wide, result((4,) + chunk.shape, F32)),
        (base, near_own, wsum, *[swap(x, n, 2 * q + 2) for q, x in enumerate(near_pieces)]),
        cost_us=NEAR_COST,
    )
    terms = [[near_sum]] + [
        [far_sums[4 * s], *[swap(far_sums[4 * s + q], n, 2 * q) for q in (1, 2, 3)]]
        for s in range(squares - 1)
    ]
    distance = 1
    while distance < squares:
        for s in range(squares - distance, 0, -2 * distance):
            total = call(add_kernel, "square_sum", piece, terms[s], cost_us=SQUARE_COST)
            terms[s - distance].append(swap(total, n, 8 * distance))
        distance *= 2

    grad_input, grad_self, grad_neigh = call(
        last_kernel, "grad_input_sum",
        (
            result((nodes, feat_in), BF16, False), result((feat_in, hidden), F32, False),
            result((feat_in, hidden), F32, False),
        ),
        (index, mine, swap(mine, n, 1), *terms[0]),
        [SMEM] + [VMEM] * (2 + len(terms[0])),
    )
    return (embedded, grad_input, grad_self, grad_neigh)


def solution(mesh):
    placed = (
        P(("parts", "row"), None),
        P(("parts", "row"), None, None),
        P(("parts", "row")),
        P(("parts", "row")),
        P(("parts", "row")),
        P(("parts", "row")),
        P(),
        P(),
        P(("parts", "row"), None),
    )
    return jax.shard_map(
        body,
        mesh=mesh,
        in_specs=placed,
        out_specs=(
            P(("parts", "row"), None),
            P(("parts", "row"), None),
            P("parts", None),
            P("parts", None),
        ),
        check_vma=False,
    )
```

```python
import functools

import jax
import jax.numpy as jnp
from jax import lax
from jax.experimental import pallas as pl
from jax.experimental.pallas import tpu as pltpu
from jax.sharding import PartitionSpec as P

BLOCK = 128
F32, BF16 = jnp.float32, jnp.bfloat16
VMEM = pl.BlockSpec(memory_space=pltpu.VMEM)
SMEM = pl.BlockSpec(memory_space=pltpu.SMEM)
ANY = pl.BlockSpec(memory_space=pl.ANY)
MIB = 1024 * 1024
LAST = ((1,), (1,))
NEAR_COST, SQUARE_COST, MAIN_COST = 8, 4, 10


def swap(x, n, offset):
    return lax.ppermute(x, "row", [(i, i ^ offset) for i in range(n)])


def gather_by_xor(x, own, n, call, pack):
    blocks = [x]
    bit = n // 2
    while bit >= 8:
        blocks = blocks + [swap(v, n, bit) for v in blocks]
        bit //= 2
    offsets = [0]
    bit = n // 2
    while bit >= 8:
        offsets = offsets + [o ^ bit for o in offsets]
        bit //= 2
    blocks = [v for _, v in sorted(zip(offsets, blocks), key=lambda pair: pair[0])]
    same = []
    for v in blocks:
        order = (2, 6, 4) if v is x else (6, 2, 4)
        square = (own if v is x else v, *[swap(v, n, offset) for offset in order])
        slots = (0, *[offset // 2 for offset in order])
        same.append(call(functools.partial(pack_kernel, slots), "pack_square", pack, square))
    return same, [swap(v, n, 1) for v in same]


def split_bf16(x):
    high = x.astype(BF16)
    return high, (x - high.astype(F32)).astype(BF16)


def dot(a, b, dims=((1,), (0,))):
    return lax.dot_general(a, b, (dims, ((), ())), preferred_element_type=F32)


def dot_wide(a, b, dims=((1,), (0,))):
    high, low = split_bf16(a)
    return dot(high, b, dims) + dot(low, b, dims)


def rows_to_lanes(row):
    return jnp.transpose(jnp.broadcast_to(row, (BLOCK, BLOCK)))


def rows_of(b):
    return pl.ds(b * BLOCK, BLOCK)


def pack_kernel(slots, *refs):
    for slot, ref in zip(slots, refs[:-1]):
        refs[-1][slot] = ref[...]


def stage_kernel(me_ref, trow_ref, tcol_ref, deg_ref, mask_ref, ws_ref, wn_ref, feat_ref, cot_ref,
                 tiles_ref, tiles_out, ws_out, wn_out, deg_out, up_out, pre_out, featt_out,
                 own_out, index_out, sem):
    copy = pltpu.make_async_copy(tiles_ref, tiles_out, sem)
    copy.start()
    block_local = feat_ref.shape[0] // BLOCK
    tile_count = trow_ref.shape[0]
    me = me_ref[0]
    index_out[2 * tile_count] = me

    def place(t, carry):
        col = tcol_ref[t]
        live = col >= 0
        col = jnp.maximum(col, 0)
        position = ((col // block_local) ^ me) * block_local + col % block_local
        row = jnp.clip(trow_ref[t] - me * block_local, 0, block_local - 1)
        index_out[t] = jnp.where(live, row, block_local)
        index_out[tile_count + t] = position
        return carry

    lax.fori_loop(0, tile_count, place, 0)
    own_out[...] = feat_ref[...]
    ws_out[...] = ws_ref[...]
    wn_out[...] = wn_ref[...]
    ws = ws_ref[...]
    for b in range(block_local):
        degree = rows_to_lanes(deg_ref[pl.ds(b, 1), :].astype(F32))
        mask = rows_to_lanes(mask_ref[pl.ds(b, 1), :].astype(F32))
        deg_out[b] = degree
        feat = feat_ref[rows_of(b), :]
        featt_out[b] = jnp.transpose(feat.astype(F32)).astype(BF16)
        pre_out[rows_of(b), :] = dot(feat, ws)
        up_out[rows_of(b), :] = cot_ref[rows_of(b), :].astype(F32) * jnp.concatenate(
            [mask, mask], axis=1)
    copy.wait()


def forward_kernel(n, group, index_ref, tiles_ref, ws_ref, wn_ref, deg_ref, up_ref, pre_ref,
                   featt_ref, *refs):
    squares = n // 8
    feat_refs, refs = refs[:2 * squares], refs[2 * squares:]
    emb_ref, base_ref, wkeep_ref, wsend_ref, gt_ref, feats, raw, wsum = refs
    block_local = deg_ref.shape[0]
    tile_count = tiles_ref.shape[0]

    raw[...] = jnp.zeros_like(raw)
    for s in range(squares):
        for q in range(4):
            for core in range(2):
                for b in range(block_local):
                    spot = (8 * s + 2 * q + core) * block_local + b
                    feats[spot] = feat_refs[core * squares + s][q, rows_of(b), :]

    def forward(step, carry):
        rows, products = [], []
        for u in range(group):
            t = step * group + u
            rows.append(index_ref[t])
            products.append(dot(tiles_ref[t], feats[index_ref[tile_count + t]]))
        for row, product in zip(rows, products):
            raw[row] += product
        return carry

    lax.fori_loop(0, tile_count // group, forward, 0)

    wn = wn_ref[...]
    ws = ws_ref[...]
    for b in range(block_local):
        degree = deg_ref[b]
        raw_b = raw[b]
        pre = pre_ref[rows_of(b), :] + dot_wide(raw_b / degree, wn)
        sig = jax.nn.sigmoid(pre)
        emb_ref[rows_of(b), :] = (pre * sig).astype(BF16)
        grad_pre = up_ref[rows_of(b), :] * sig * (1.0 + pre * (1.0 - sig))
        scaled = (grad_pre / jnp.concatenate([degree, degree], axis=1)).astype(BF16)
        gp_high, gp_low = split_bf16(grad_pre)
        feat_t = featt_ref[b]
        grad_self = dot(feat_t, gp_high) + dot(feat_t, gp_low)
        grad_neigh = dot_wide(jnp.transpose(raw_b), scaled)
        if b == 0:
            wsum[0], wsum[1] = grad_self, grad_neigh
        else:
            wsum[0] += grad_self
            wsum[1] += grad_neigh
        base_ref[rows_of(b), :] = dot(gp_high, ws, LAST) + dot(gp_low, ws, LAST)
        high, low = split_bf16(dot(wn, scaled, LAST))
        gt_ref[b, :BLOCK, :] = high
        gt_ref[b, BLOCK:, :] = low

    core = index_ref[2 * tile_count] % 2
    wkeep_ref[...] = wsum[core]
    wsend_ref[...] = wsum[1 - core]


def backward_kernel(group, index_ref, tiles_ref, gt_ref, acc_ref):
    block_local = gt_ref.shape[0]
    tile_count = tiles_ref.shape[0]
    dump = acc_ref.shape[0] - 1
    acc_ref[...] = jnp.zeros_like(acc_ref)

    def backward(step, carry):
        places, products = [], []
        for u in range(group):
            t = step * group + u
            row = index_ref[t]
            places.append(jnp.where(row < block_local, index_ref[tile_count + t], dump))
            both = dot(gt_ref[jnp.minimum(row, block_local - 1)], tiles_ref[t])
            products.append(both[:BLOCK] + both[BLOCK:])
        for position, product in zip(places, products):
            acc_ref[position] += product
        return carry

    lax.fori_loop(0, tile_count // group, backward, 0)


def send_kernel(square, block_local, acc_ref, send_ref):
    for q in range(4):
        for b in range(block_local):
            send_ref[q, rows_of(b), :] = acc_ref[(8 * square + 2 * q + 1) * block_local + b]


def send_weights_kernel(square, block_local, index_ref, acc_ref, wkeep_ref, wgot_ref, send_ref,
                        *parts):
    send_kernel(square, block_local, acc_ref, send_ref)
    rows = parts[0].shape[0]
    chip = index_ref[index_ref.shape[0] - 1] // 2 % 4
    for p, ref in enumerate(parts):
        span = pl.ds(pl.multiple_of((chip ^ p) * rows, rows), rows)
        ref[...] = wkeep_ref[span, :] + wgot_ref[span, :]


def pair_kernel(square, acc_ref, got_ref, own_ref, *pieces):
    block_local = own_ref.shape[0] // BLOCK
    for q, ref in enumerate((own_ref, *pieces)):
        for b in range(block_local):
            kept = acc_ref[(8 * square + 2 * q) * block_local + b]
            ref[rows_of(b), :] = (kept + got_ref[q, rows_of(b), :]).astype(ref.dtype)


def pair_weights_kernel(square, acc_ref, got_ref, w1, w2, w3, own_ref, *pieces):
    pair_kernel(square, acc_ref, got_ref, own_ref, *pieces)
    nodes, lanes = own_ref.shape
    for weight_ref, ref in zip((w1, w2, w3), pieces):
        rows, columns = weight_ref.shape
        start = nodes
        for part in split_bf16(weight_ref[...]):
            for column in range(0, columns, lanes):
                ref[pl.ds(start, rows), :] = part[:, column:column + lanes]
                start += rows


def add_two_kernel(own_ref, got_ref, out_ref):
    out_ref[...] = own_ref[...] + got_ref[...]


def add_kernel(own_ref, *refs):
    total = own_ref[...]
    for got_ref in refs[:-1]:
        total = total + got_ref[...].astype(F32)
    refs[-1][...] = total.astype(BF16)


def add_weights_kernel(weight_ref, own_ref, *refs):
    got_refs, (out_ref, weight_out) = refs[:-2], refs[-2:]
    nodes, lanes = own_ref.shape
    add_kernel(own_ref, *[ref.at[pl.ds(0, nodes), :] for ref in got_refs], out_ref)
    rows, columns = weight_ref.shape
    cuts = columns // lanes
    for cut in range(cuts):
        span = pl.ds(cut * lanes, lanes)
        total = weight_ref[:, span]
        for ref in got_refs[:3]:
            high = ref[pl.ds(nodes + cut * rows, rows), :]
            low = ref[pl.ds(nodes + (cuts + cut) * rows, rows), :]
            total = total + (high.astype(F32) + low.astype(F32))
        weight_out[:, span] = total


def near_kernel(base_ref, own_ref, *refs):
    for b in range(own_ref.shape[0] // BLOCK):
        total = own_ref[rows_of(b), :]
        for got_ref in refs[:-1]:
            total = total + got_ref[rows_of(b), :].astype(F32)
        refs[-1][rows_of(b), :] = base_ref[rows_of(b), :] + jnp.transpose(total)


def main_kernel(near_ref, *refs):
    for b in range(near_ref.shape[0] // BLOCK):
        total = refs[0][rows_of(b), :].astype(F32)
        for got_ref in refs[1:-1]:
            total = total + got_ref[rows_of(b), :].astype(F32)
        refs[-1][rows_of(b), :] = (near_ref[rows_of(b), :] + jnp.transpose(total)).astype(BF16)


def last_kernel(index_ref, weight_ref, other_ref, main_ref, out_ref, self_ref, neigh_ref):
    out_ref[...] = main_ref[...]
    me = index_ref[index_ref.shape[0] - 1]
    first = me % 2 == 0
    chip = me // 2 % 4
    rows = weight_ref.shape[2]
    for p in range(4):
        span = pl.ds(pl.multiple_of((chip ^ p) * rows, rows), rows)
        mine, other = weight_ref[p // 2, p % 2], other_ref[p // 2, p % 2]
        self_ref[span, :] = jnp.where(first, mine, other)
        neigh_ref[span, :] = jnp.where(first, other, mine)


def body(features, tiles, tile_row, tile_col, degree, train_mask, w_self, w_neigh, cotangent):
    n = lax.axis_size("row")
    me = lax.axis_index("row").astype(jnp.int32).reshape(1)
    squares = n // 8
    nodes, feat_in = features.shape
    hidden = w_self.shape[1]
    block_local = nodes // BLOCK
    tile_count = tiles.shape[0]
    group = max(g for g in range(1, 7) if tile_count % g == 0)
    small = n * nodes * feat_in * 4 <= 4 * MIB
    limit = (24 if small else 56) * MIB

    def result(shape, dtype, stays=True):
        kind = pltpu.VMEM if small and stays else jax.ShapeDtypeStruct
        return kind(shape, dtype)

    def placed(x, spec):
        if spec is SMEM or not small:
            return x
        return pltpu.with_memory_space_constraint(x, pltpu.HBM if spec is ANY else pltpu.VMEM)

    def call(kernel, name, out_shape, operands, in_specs=None, out_specs=None, cost_us=0.2, **more):
        specs = in_specs or [VMEM] * len(operands)
        return pl.pallas_call(
            kernel,
            out_shape=out_shape,
            in_specs=specs,
            out_specs=out_specs or jax.tree.map(lambda _: VMEM, out_shape),
            compiler_params=pltpu.CompilerParams(vmem_limit_bytes=limit),
            cost_estimate=pl.CostEstimate(
                flops=int(cost_us * 1.1e9), bytes_accessed=int(cost_us * 3.6e6), transcendentals=0),
            name=name,
            **more,
        )(*[placed(x, spec) for x, spec in zip(operands, specs)])

    wide, piece = result((nodes, feat_in), F32), result((nodes, feat_in), BF16)
    weight = result((feat_in, hidden), F32)
    chunk = result((feat_in // 4, hidden), F32)
    by_block = (block_local, BLOCK, feat_in)

    own_arguments = (
        degree.reshape(block_local, BLOCK), train_mask.reshape(block_local, BLOCK),
        w_self, w_neigh, features, cotangent,
    )
    if small:
        own_arguments = [pltpu.with_memory_space_constraint(x, pltpu.HBM) for x in own_arguments]
    tiles_near, ws, wn, degree_wide, upstream, pre_self, feat_t, own, index = pl.pallas_call(
        stage_kernel,
        out_shape=(
            result(tiles.shape, BF16),
            result(w_self.shape, BF16),
            result(w_neigh.shape, BF16),
            result(by_block, F32),
            result((nodes, hidden), F32),
            result((nodes, hidden), F32),
            result(by_block, BF16),
            piece,
            pltpu.SMEM((2 * tile_count + 1,), jnp.int32),
        ),
        in_specs=[SMEM] * 3 + [VMEM] * 6 + [ANY],
        out_specs=(VMEM,) * 8 + (SMEM,),
        scratch_shapes=[pltpu.SemaphoreType.DMA],
        compiler_params=pltpu.CompilerParams(vmem_limit_bytes=limit),
        cost_estimate=pl.CostEstimate(flops=int(3 * 1.1e9), bytes_accessed=int(3 * 3.6e6), transcendentals=0),
        name="stage_arguments",
    )(me, tile_row, tile_col, *own_arguments, placed(tiles, ANY))

    same, other = gather_by_xor(features, own, n, call, result((4, nodes, feat_in), BF16))
    operands = (index, tiles_near, ws, wn, degree_wide, upstream, pre_self, feat_t, *same, *other)
    embedded, base, wkeep, wsend, gt = call(
        functools.partial(forward_kernel, n, group),
        "forward_layer",
        (
            result((nodes, hidden), BF16, False), wide, weight, weight,
            result((block_local, 2 * feat_in, BLOCK), BF16),
        ),
        operands,
        [SMEM] + [VMEM] * (len(operands) - 1),
        cost_us=5,
        scratch_shapes=[
            pltpu.VMEM((n * block_local, BLOCK, feat_in), BF16),
            pltpu.VMEM((block_local + 1, BLOCK, feat_in), F32),
            pltpu.VMEM((2, feat_in, hidden), F32),
        ],
    )

    acc_shape = result((n * block_local + 1, feat_in, BLOCK), F32)
    acc = call(
        functools.partial(backward_kernel, group), "backward_tiles", acc_shape,
        (index, tiles_near, gt), [SMEM, VMEM, VMEM], cost_us=3.5,
    )
    send_shape = result((4, nodes, feat_in), F32)
    send = [None] * squares
    for s in range(squares - 1, -1, -1):
        if s == squares - 1:
            send[s], w0, w1, w2, w3 = call(
                functools.partial(send_weights_kernel, s, block_local), "send_weights",
                (send_shape,) + (chunk,) * 4, (index, acc, wkeep, swap(wsend, n, 1)),
                [SMEM] + [VMEM] * 3)
        else:
            send[s] = call(
                functools.partial(send_kernel, s, block_local), "send", send_shape, (acc,))

    extra = result((nodes + 2 * chunk.shape[0] * (hidden // feat_in), feat_in), BF16)
    terms = [None] * squares
    for s in range(squares - 1, -1, -1):
        operands = (acc, swap(send[s], n, 1))
        if s == squares - 1:
            own, *pieces = call(
                functools.partial(pair_weights_kernel, s), "pair_sum_weights", (wide, extra, extra, extra),
                operands + (w1, w2, w3))
        else:
            own, *pieces = call(
                functools.partial(pair_kernel, s), "pair_sum", (wide, piece, piece, piece), operands)
        terms[s] = [own, *[swap(x, n, 2 * q + 2) for q, x in enumerate(pieces)]]
    near_total = call(near_kernel, "near_sum", wide, (base, *terms[0]), cost_us=NEAR_COST)
    terms[0] = [near_total]
    distance = 1
    while distance < squares:
        for s in range(squares - distance, 0, -2 * distance):
            if s == squares - 1:
                total, wsum = call(
                    add_weights_kernel, "square_sum_weights", (piece, chunk), (w0, *terms[s]),
                    cost_us=SQUARE_COST)
            else:
                total = call(add_kernel, "square_sum", piece, terms[s], cost_us=SQUARE_COST)
            terms[s - distance].append(swap(total, n, 8 * distance))
        distance *= 2
    bit = 8
    while bit < n:
        wsum = call(add_two_kernel, "weight_sum", chunk, (wsum, swap(wsum, n, bit)))
        bit *= 2
    rows = chunk.shape[0]
    two = call(functools.partial(pack_kernel, (0, 1)), "pack_weights", result((2, rows, hidden), F32), (wsum, swap(wsum, n, 2)))
    mine = call(
        functools.partial(pack_kernel, (0, 1)), "pack_weights", result((2, 2, rows, hidden), F32), (two, swap(two, n, 4), near_total))
    main = call(main_kernel, "main_sum", piece, terms[0], cost_us=MAIN_COST)
    grad_input, grad_self, grad_neigh = call(
        last_kernel, "write_gradients",
        (
            result((nodes, feat_in), BF16, False), result((feat_in, hidden), F32, False),
            result((feat_in, hidden), F32, False),
        ),
        (index, mine, swap(mine, n, 1), main), [SMEM] + [VMEM] * 3,
    )
    return (embedded, grad_input, grad_self, grad_neigh)


def solution(mesh):
    placed = (
        P(("parts", "row"), None),
        P(("parts", "row"), None, None),
        P(("parts", "row")),
        P(("parts", "row")),
        P(("parts", "row")),
        P(("parts", "row")),
        P(),
        P(),
        P(("parts", "row"), None),
    )
    return jax.shard_map(
        body,
        mesh=mesh,
        in_specs=placed,
        out_specs=(
            P(("parts", "row"), None),
            P(("parts", "row"), None),
            P("parts", None),
            P("parts", None),
        ),
        check_vma=False,
    )
```

```python
import functools

import jax
import jax.numpy as jnp
from jax import lax
from jax.experimental import pallas as pl
from jax.experimental.pallas import tpu as pltpu
from jax.sharding import PartitionSpec as P

BLOCK = 128
F32, BF16 = jnp.float32, jnp.bfloat16
VMEM = pl.BlockSpec(memory_space=pltpu.VMEM)
SMEM = pl.BlockSpec(memory_space=pltpu.SMEM)
ANY = pl.BlockSpec(memory_space=pl.ANY)
MIB = 1024 * 1024
LAST = ((1,), (1,))
NEAR_COST, SQUARE_COST, MAIN_COST = 0.2, 0.2, 4


def swap(x, n, offset):
    return lax.ppermute(x, "row", [(i, i ^ offset) for i in range(n)])


def gather_by_xor(x, own, n, call, pack):
    blocks = [x]
    bit = n // 2
    while bit >= 8:
        blocks = blocks + [swap(v, n, bit) for v in blocks]
        bit //= 2
    offsets = [0]
    bit = n // 2
    while bit >= 8:
        offsets = offsets + [o ^ bit for o in offsets]
        bit //= 2
    blocks = [v for _, v in sorted(zip(offsets, blocks), key=lambda pair: pair[0])]
    same = []
    for v in blocks:
        order = (2, 6, 4) if v is x else (6, 2, 4)
        square = (own if v is x else v, *[swap(v, n, offset) for offset in order])
        slots = (0, *[offset // 2 for offset in order])
        same.append(call(functools.partial(pack_kernel, slots), "pack_square", pack, square))
    return same, [swap(v, n, 1) for v in same]


def split_bf16(x):
    high = x.astype(BF16)
    return high, (x - high.astype(F32)).astype(BF16)


def dot(a, b, dims=((1,), (0,))):
    return lax.dot_general(a, b, (dims, ((), ())), preferred_element_type=F32)


def dot_wide(a, b, dims=((1,), (0,))):
    high, low = split_bf16(a)
    return dot(high, b, dims) + dot(low, b, dims)


def rows_to_lanes(row):
    return jnp.transpose(jnp.broadcast_to(row, (BLOCK, BLOCK)))


def rows_of(b):
    return pl.ds(b * BLOCK, BLOCK)


def pack_kernel(slots, *refs):
    for slot, ref in zip(slots, refs[:-1]):
        refs[-1][slot] = ref[...]


def stage_kernel(me_ref, trow_ref, tcol_ref, deg_ref, mask_ref, ws_ref, wn_ref, feat_ref, cot_ref,
                 tiles_ref, tiles_out, ws_out, wn_out, deg_out, up_out, pre_out, featt_out,
                 own_out, index_out, sem):
    copy = pltpu.make_async_copy(tiles_ref, tiles_out, sem)
    copy.start()
    block_local = feat_ref.shape[0] // BLOCK
    tile_count = trow_ref.shape[0]
    me = me_ref[0]
    index_out[2 * tile_count] = me

    def place(t, carry):
        col = tcol_ref[t]
        live = col >= 0
        col = jnp.maximum(col, 0)
        position = ((col // block_local) ^ me) * block_local + col % block_local
        row = jnp.clip(trow_ref[t] - me * block_local, 0, block_local - 1)
        index_out[t] = jnp.where(live, row, block_local)
        index_out[tile_count + t] = position
        return carry

    lax.fori_loop(0, tile_count, place, 0)
    own_out[...] = feat_ref[...]
    ws_out[...] = ws_ref[...]
    wn_out[...] = wn_ref[...]
    ws = ws_ref[...]
    for b in range(block_local):
        degree = rows_to_lanes(deg_ref[pl.ds(b, 1), :].astype(F32))
        mask = rows_to_lanes(mask_ref[pl.ds(b, 1), :].astype(F32))
        deg_out[b] = degree
        feat = feat_ref[rows_of(b), :]
        featt_out[b] = jnp.transpose(feat.astype(F32)).astype(BF16)
        pre_out[rows_of(b), :] = dot(feat, ws)
        up_out[rows_of(b), :] = cot_ref[rows_of(b), :].astype(F32) * jnp.concatenate(
            [mask, mask], axis=1)
    copy.wait()


def forward_kernel(n, group, index_ref, tiles_ref, ws_ref, wn_ref, deg_ref, up_ref, pre_ref,
                   featt_ref, *refs):
    squares = n // 8
    feat_refs, refs = refs[:2 * squares], refs[2 * squares:]
    emb_ref, base_ref, wkeep_ref, wsend_ref, gt_ref, feats, raw, wsum = refs
    block_local = deg_ref.shape[0]
    tile_count = tiles_ref.shape[0]

    raw[...] = jnp.zeros_like(raw)
    for s in range(squares):
        for q in range(4):
            for core in range(2):
                for b in range(block_local):
                    spot = (8 * s + 2 * q + core) * block_local + b
                    feats[spot] = feat_refs[core * squares + s][q, rows_of(b), :]

    def forward(step, carry):
        rows, products = [], []
        for u in range(group):
            t = step * group + u
            rows.append(index_ref[t])
            products.append(dot(tiles_ref[t], feats[index_ref[tile_count + t]]))
        for row, product in zip(rows, products):
            raw[row] += product
        return carry

    lax.fori_loop(0, tile_count // group, forward, 0)

    wn = wn_ref[...]
    ws = ws_ref[...]
    for b in range(block_local):
        degree = deg_ref[b]
        raw_b = raw[b]
        pre = pre_ref[rows_of(b), :] + dot_wide(raw_b / degree, wn)
        sig = jax.nn.sigmoid(pre)
        emb_ref[rows_of(b), :] = (pre * sig).astype(BF16)
        grad_pre = up_ref[rows_of(b), :] * sig * (1.0 + pre * (1.0 - sig))
        scaled = (grad_pre / jnp.concatenate([degree, degree], axis=1)).astype(BF16)
        gp_high, gp_low = split_bf16(grad_pre)
        feat_t = featt_ref[b]
        grad_self = dot(feat_t, gp_high) + dot(feat_t, gp_low)
        grad_neigh = dot_wide(jnp.transpose(raw_b), scaled)
        if b == 0:
            wsum[0], wsum[1] = grad_self, grad_neigh
        else:
            wsum[0] += grad_self
            wsum[1] += grad_neigh
        base_ref[rows_of(b), :] = dot(gp_high, ws, LAST) + dot(gp_low, ws, LAST)
        high, low = split_bf16(dot(wn, scaled, LAST))
        gt_ref[b, :BLOCK, :] = high
        gt_ref[b, BLOCK:, :] = low

    core = index_ref[2 * tile_count] % 2
    wkeep_ref[...] = wsum[core]
    wsend_ref[...] = wsum[1 - core]


def backward_kernel(group, index_ref, tiles_ref, gt_ref, acc_ref):
    block_local = gt_ref.shape[0]
    tile_count = tiles_ref.shape[0]
    dump = acc_ref.shape[0] - 1
    acc_ref[...] = jnp.zeros_like(acc_ref)

    def backward(step, carry):
        places, products = [], []
        for u in range(group):
            t = step * group + u
            row = index_ref[t]
            places.append(jnp.where(row < block_local, index_ref[tile_count + t], dump))
            both = dot(gt_ref[jnp.minimum(row, block_local - 1)], tiles_ref[t])
            products.append(both[:BLOCK] + both[BLOCK:])
        for position, product in zip(places, products):
            acc_ref[position] += product
        return carry

    lax.fori_loop(0, tile_count // group, backward, 0)


def send_kernel(square, block_local, acc_ref, send_ref):
    for q in range(4):
        for b in range(block_local):
            send_ref[q, rows_of(b), :] = acc_ref[(8 * square + 2 * q + 1) * block_local + b]


def send_weights_kernel(square, block_local, index_ref, acc_ref, wkeep_ref, wgot_ref, send_ref,
                        *parts):
    send_kernel(square, block_local, acc_ref, send_ref)
    rows = parts[0].shape[0]
    chip = index_ref[index_ref.shape[0] - 1] // 2 % 4
    for p, ref in enumerate(parts):
        span = pl.ds(pl.multiple_of((chip ^ p) * rows, rows), rows)
        ref[...] = wkeep_ref[span, :] + wgot_ref[span, :]


def pair_kernel(square, acc_ref, got_ref, *refs):
    own_ref, *pieces = refs[-4:]
    block_local = own_ref.shape[0] // BLOCK
    for q, ref in enumerate((own_ref, *pieces)):
        for b in range(block_local):
            kept = acc_ref[(8 * square + 2 * q) * block_local + b]
            ref[rows_of(b), :] = (kept + got_ref[q, rows_of(b), :]).astype(ref.dtype)


def pair_weights_kernel(square, acc_ref, got_ref, w1, w2, w3, own_ref, *pieces):
    pair_kernel(square, acc_ref, got_ref, own_ref, *pieces)
    nodes, lanes = own_ref.shape
    for weight_ref, ref in zip((w1, w2, w3), pieces):
        rows, columns = weight_ref.shape
        start = nodes
        for part in split_bf16(weight_ref[...]):
            for column in range(0, columns, lanes):
                ref[pl.ds(start, rows), :] = part[:, column:column + lanes]
                start += rows


def add_two_kernel(own_ref, got_ref, out_ref):
    out_ref[...] = own_ref[...] + got_ref[...]


def add_kernel(own_ref, *refs):
    total = own_ref[...].astype(F32)
    for got_ref in refs[:-1]:
        total = total + got_ref[...].astype(F32)
    refs[-1][...] = total.astype(refs[-1].dtype)


def add_weights_kernel(weight_ref, own_ref, *refs):
    got_refs, (out_ref, weight_out) = refs[:-2], refs[-2:]
    nodes, lanes = own_ref.shape
    add_kernel(own_ref, *[ref.at[pl.ds(0, nodes), :] for ref in got_refs], out_ref)
    rows, columns = weight_ref.shape
    cuts = columns // lanes
    for cut in range(cuts):
        span = pl.ds(cut * lanes, lanes)
        total = weight_ref[:, span]
        for ref in got_refs[:3]:
            high = ref[pl.ds(nodes + cut * rows, rows), :]
            low = ref[pl.ds(nodes + (cuts + cut) * rows, rows), :]
            total = total + (high.astype(F32) + low.astype(F32))
        weight_out[:, span] = total


def near_kernel(base_ref, own_ref, *refs):
    for b in range(own_ref.shape[0] // BLOCK):
        total = own_ref[rows_of(b), :]
        for got_ref in refs[:-1]:
            total = total + got_ref[rows_of(b), :].astype(F32)
        refs[-1][rows_of(b), :] = base_ref[rows_of(b), :] + jnp.transpose(total)


def main_kernel(near_ref, *refs):
    for b in range(near_ref.shape[0] // BLOCK):
        total = refs[0][rows_of(b), :].astype(F32)
        for got_ref in refs[1:-1]:
            total = total + got_ref[rows_of(b), :].astype(F32)
        refs[-1][rows_of(b), :] = (near_ref[rows_of(b), :] + jnp.transpose(total)).astype(BF16)


def last_kernel(index_ref, weight_ref, other_ref, main_ref, out_ref, self_ref, neigh_ref):
    out_ref[...] = main_ref[...]
    me = index_ref[index_ref.shape[0] - 1]
    first = me % 2 == 0
    chip = me // 2 % 4
    rows = weight_ref.shape[2]
    for p in range(4):
        span = pl.ds(pl.multiple_of((chip ^ p) * rows, rows), rows)
        mine, other = weight_ref[p // 2, p % 2], other_ref[p // 2, p % 2]
        self_ref[span, :] = jnp.where(first, mine, other)
        neigh_ref[span, :] = jnp.where(first, other, mine)


def body(features, tiles, tile_row, tile_col, degree, train_mask, w_self, w_neigh, cotangent):
    n = lax.axis_size("row")
    me = lax.axis_index("row").astype(jnp.int32).reshape(1)
    squares = n // 8
    nodes, feat_in = features.shape
    hidden = w_self.shape[1]
    block_local = nodes // BLOCK
    tile_count = tiles.shape[0]
    group = max(g for g in range(1, 7) if tile_count % g == 0)
    small = n * nodes * feat_in * 4 <= 4 * MIB
    limit = (24 if small else 56) * MIB

    def result(shape, dtype, stays=True):
        kind = pltpu.VMEM if small and stays else jax.ShapeDtypeStruct
        return kind(shape, dtype)

    def placed(x, spec):
        if spec is SMEM or not small:
            return x
        return pltpu.with_memory_space_constraint(x, pltpu.HBM if spec is ANY else pltpu.VMEM)

    def call(kernel, name, out_shape, operands, in_specs=None, out_specs=None, cost_us=0.2, **more):
        specs = in_specs or [VMEM] * len(operands)
        return pl.pallas_call(
            kernel,
            out_shape=out_shape,
            in_specs=specs,
            out_specs=out_specs or jax.tree.map(lambda _: VMEM, out_shape),
            compiler_params=pltpu.CompilerParams(vmem_limit_bytes=limit),
            cost_estimate=pl.CostEstimate(
                flops=int(cost_us * 1.1e9), bytes_accessed=int(cost_us * 3.6e6), transcendentals=0),
            name=name,
            **more,
        )(*[placed(x, spec) for x, spec in zip(operands, specs)])

    wide, piece = result((nodes, feat_in), F32), result((nodes, feat_in), BF16)
    weight = result((feat_in, hidden), F32)
    chunk = result((feat_in // 4, hidden), F32)
    by_block = (block_local, BLOCK, feat_in)

    own_arguments = (
        degree.reshape(block_local, BLOCK), train_mask.reshape(block_local, BLOCK),
        w_self, w_neigh, features, cotangent,
    )
    if small:
        own_arguments = [pltpu.with_memory_space_constraint(x, pltpu.HBM) for x in own_arguments]
    tiles_near, ws, wn, degree_wide, upstream, pre_self, feat_t, own, index = pl.pallas_call(
        stage_kernel,
        out_shape=(
            result(tiles.shape, BF16),
            result(w_self.shape, BF16),
            result(w_neigh.shape, BF16),
            result(by_block, F32),
            result((nodes, hidden), F32),
            result((nodes, hidden), F32),
            result(by_block, BF16),
            piece,
            pltpu.SMEM((2 * tile_count + 1,), jnp.int32),
        ),
        in_specs=[SMEM] * 3 + [VMEM] * 6 + [ANY],
        out_specs=(VMEM,) * 8 + (SMEM,),
        scratch_shapes=[pltpu.SemaphoreType.DMA],
        compiler_params=pltpu.CompilerParams(vmem_limit_bytes=limit),
        cost_estimate=pl.CostEstimate(flops=int(3 * 1.1e9), bytes_accessed=int(3 * 3.6e6), transcendentals=0),
        name="stage_arguments",
    )(me, tile_row, tile_col, *own_arguments, placed(tiles, ANY))

    same, other = gather_by_xor(features, own, n, call, result((4, nodes, feat_in), BF16))
    operands = (index, tiles_near, ws, wn, degree_wide, upstream, pre_self, feat_t, *same, *other)
    embedded, base, wkeep, wsend, gt = call(
        functools.partial(forward_kernel, n, group),
        "forward_layer",
        (
            result((nodes, hidden), BF16, False), wide, weight, weight,
            result((block_local, 2 * feat_in, BLOCK), BF16),
        ),
        operands,
        [SMEM] + [VMEM] * (len(operands) - 1),
        cost_us=5,
        scratch_shapes=[
            pltpu.VMEM((n * block_local, BLOCK, feat_in), BF16),
            pltpu.VMEM((block_local + 1, BLOCK, feat_in), F32),
            pltpu.VMEM((2, feat_in, hidden), F32),
        ],
    )

    acc_shape = result((n * block_local + 1, feat_in, BLOCK), F32)
    acc = call(
        functools.partial(backward_kernel, group), "backward_tiles", acc_shape,
        (index, tiles_near, gt), [SMEM, VMEM, VMEM], cost_us=3.5,
    )
    send_shape = result((4, nodes, feat_in), F32)
    send = [None] * squares
    for s in range(squares - 1, -1, -1):
        if s == squares - 1:
            send[s], w0, w1, w2, w3 = call(
                functools.partial(send_weights_kernel, s, block_local), "send_weights",
                (send_shape,) + (chunk,) * 4, (index, acc, wkeep, swap(wsend, n, 1)),
                [SMEM] + [VMEM] * 3)
        else:
            send[s] = call(
                functools.partial(send_kernel, s, block_local), "send", send_shape, (acc,))

    extra = result((nodes + 2 * chunk.shape[0] * (hidden // feat_in), feat_in), BF16)
    terms = [None] * squares
    for s in range(squares - 1, 0, -1):
        operands = (acc, swap(send[s], n, 1))
        if s == squares - 1:
            own, *pieces = call(
                functools.partial(pair_weights_kernel, s), "pair_sum_weights",
                (wide, extra, extra, extra), operands + (w1, w2, w3))
        else:
            own, *pieces = call(
                functools.partial(pair_kernel, s), "pair_sum", (wide, piece, piece, piece), operands)
        terms[s] = [own, *[swap(x, n, 2 * q + 2) for q, x in enumerate(pieces)]]
    from_squares = []
    distance = 1
    while distance < squares:
        for s in range(squares - distance, 0, -2 * distance):
            if s == squares - 1:
                total, wsum = call(
                    add_weights_kernel, "square_sum_weights", (piece, chunk), (w0, *terms[s]),
                    cost_us=SQUARE_COST)
            else:
                total = call(add_kernel, "square_sum", piece, terms[s], cost_us=SQUARE_COST)
            target = from_squares if s == distance else terms[s - distance]
            target.append(swap(total, n, 8 * distance))
        distance *= 2
    bit = 8
    while bit < n:
        wsum = call(add_two_kernel, "weight_sum", chunk, (wsum, swap(wsum, n, bit)))
        bit *= 2
    own, *pieces = call(
        functools.partial(pair_kernel, 0), "pair_sum", (wide, piece, piece, piece),
        (acc, swap(send[0], n, 1), wsum))
    near = [swap(x, n, 2 * q + 2) for q, x in enumerate(pieces)]
    near_total = call(near_kernel, "near_sum", wide, (base, own, *near), cost_us=NEAR_COST)
    rows = chunk.shape[0]
    two = call(functools.partial(pack_kernel, (0, 1)), "pack_weights", result((2, rows, hidden), F32), (wsum, swap(wsum, n, 2)))
    mine = call(
        functools.partial(pack_kernel, (0, 1)), "pack_weights", result((2, 2, rows, hidden), F32), (two, swap(two, n, 4), near_total))
    main = call(main_kernel, "main_sum", piece, (near_total, *[call(add_kernel, "far_sum", wide, (x,), cost_us=10) for x in from_squares]), cost_us=MAIN_COST)
    grad_input, grad_self, grad_neigh = call(
        last_kernel, "write_gradients",
        (
            result((nodes, feat_in), BF16, False), result((feat_in, hidden), F32, False),
            result((feat_in, hidden), F32, False),
        ),
        (index, mine, swap(mine, n, 1), main), [SMEM] + [VMEM] * 3,
    )
    return (embedded, grad_input, grad_self, grad_neigh)


def solution(mesh):
    placed = (
        P(("parts", "row"), None),
        P(("parts", "row"), None, None),
        P(("parts", "row")),
        P(("parts", "row")),
        P(("parts", "row")),
        P(("parts", "row")),
        P(),
        P(),
        P(("parts", "row"), None),
    )
    return jax.shard_map(
        body,
        mesh=mesh,
        in_specs=placed,
        out_specs=(
            P(("parts", "row"), None),
            P(("parts", "row"), None),
            P("parts", None),
            P("parts", None),
        ),
        check_vma=False,
    )
```

```python
import functools

import jax
import jax.numpy as jnp
from jax import lax
from jax.experimental import pallas as pl
from jax.experimental.pallas import tpu as pltpu
from jax.sharding import PartitionSpec as P

BLOCK = 128
F32, BF16 = jnp.float32, jnp.bfloat16
VMEM = pl.BlockSpec(memory_space=pltpu.VMEM)
SMEM = pl.BlockSpec(memory_space=pltpu.SMEM)
ANY = pl.BlockSpec(memory_space=pl.ANY)
MIB = 1024 * 1024
LAST = ((1,), (1,))
NEAR_COST, SQUARE_COST, MAIN_COST, FAR_COST = 4, 0.2, 0.2, 10


def swap(x, n, offset):
    return lax.ppermute(x, "row", [(i, i ^ offset) for i in range(n)])


def gather_by_xor(x, own, n, call, pack):
    blocks = [x]
    bit = n // 2
    while bit >= 8:
        blocks = blocks + [swap(v, n, bit) for v in blocks]
        bit //= 2
    offsets = [0]
    bit = n // 2
    while bit >= 8:
        offsets = offsets + [o ^ bit for o in offsets]
        bit //= 2
    blocks = [v for _, v in sorted(zip(offsets, blocks), key=lambda pair: pair[0])]
    same = []
    for v in blocks:
        order = (2, 6, 4) if v is x else (6, 2, 4)
        square = (own if v is x else v, *[swap(v, n, offset) for offset in order])
        slots = (0, *[offset // 2 for offset in order])
        same.append(call(functools.partial(pack_kernel, slots), "pack_square", pack, square))
    return same, [swap(v, n, 1) for v in same]


def split_bf16(x):
    high = x.astype(BF16)
    return high, (x - high.astype(F32)).astype(BF16)


def dot(a, b, dims=((1,), (0,))):
    return lax.dot_general(a, b, (dims, ((), ())), preferred_element_type=F32)


def dot_wide(a, b, dims=((1,), (0,))):
    high, low = split_bf16(a)
    return dot(high, b, dims) + dot(low, b, dims)


def rows_to_lanes(row):
    return jnp.transpose(jnp.broadcast_to(row, (BLOCK, BLOCK)))


def rows_of(b):
    return pl.ds(b * BLOCK, BLOCK)


def pack_kernel(slots, *refs):
    for slot, ref in zip(slots, refs[:-1]):
        refs[-1][slot] = ref[...]


def stage_kernel(me_ref, trow_ref, tcol_ref, deg_ref, mask_ref, ws_ref, wn_ref, feat_ref, cot_ref,
                 tiles_ref, tiles_out, ws_out, wn_out, deg_out, up_out, pre_out, featt_out,
                 own_out, index_out, sem):
    copy = pltpu.make_async_copy(tiles_ref, tiles_out, sem)
    copy.start()
    block_local = feat_ref.shape[0] // BLOCK
    tile_count = trow_ref.shape[0]
    me = me_ref[0]
    index_out[2 * tile_count] = me

    def place(t, carry):
        col = tcol_ref[t]
        live = col >= 0
        col = jnp.maximum(col, 0)
        position = ((col // block_local) ^ me) * block_local + col % block_local
        row = jnp.clip(trow_ref[t] - me * block_local, 0, block_local - 1)
        index_out[t] = jnp.where(live, row, block_local)
        index_out[tile_count + t] = position
        return carry

    lax.fori_loop(0, tile_count, place, 0)
    own_out[...] = feat_ref[...]
    ws_out[...] = ws_ref[...]
    wn_out[...] = wn_ref[...]
    ws = ws_ref[...]
    for b in range(block_local):
        degree = rows_to_lanes(deg_ref[pl.ds(b, 1), :].astype(F32))
        mask = rows_to_lanes(mask_ref[pl.ds(b, 1), :].astype(F32))
        deg_out[b] = degree
        feat = feat_ref[rows_of(b), :]
        featt_out[b] = jnp.transpose(feat.astype(F32)).astype(BF16)
        pre_out[rows_of(b), :] = dot(feat, ws)
        up_out[rows_of(b), :] = cot_ref[rows_of(b), :].astype(F32) * jnp.concatenate(
            [mask, mask], axis=1)
    copy.wait()


def forward_kernel(n, group, index_ref, tiles_ref, ws_ref, wn_ref, deg_ref, up_ref, pre_ref,
                   featt_ref, *refs):
    squares = n // 8
    feat_refs, refs = refs[:2 * squares], refs[2 * squares:]
    emb_ref, base_ref, wkeep_ref, wsend_ref, gt_ref, feats, raw, wsum = refs
    block_local = deg_ref.shape[0]
    tile_count = tiles_ref.shape[0]

    raw[...] = jnp.zeros_like(raw)
    for s in range(squares):
        for q in range(4):
            for core in range(2):
                for b in range(block_local):
                    spot = (8 * s + 2 * q + core) * block_local + b
                    feats[spot] = feat_refs[core * squares + s][q, rows_of(b), :]

    def forward(step, carry):
        rows, products = [], []
        for u in range(group):
            t = step * group + u
            rows.append(index_ref[t])
            products.append(dot(tiles_ref[t], feats[index_ref[tile_count + t]]))
        for row, product in zip(rows, products):
            raw[row] += product
        return carry

    lax.fori_loop(0, tile_count // group, forward, 0)

    wn = wn_ref[...]
    ws = ws_ref[...]
    for b in range(block_local):
        degree = deg_ref[b]
        raw_b = raw[b]
        pre = pre_ref[rows_of(b), :] + dot_wide(raw_b / degree, wn)
        sig = jax.nn.sigmoid(pre)
        emb_ref[rows_of(b), :] = (pre * sig).astype(BF16)
        grad_pre = up_ref[rows_of(b), :] * sig * (1.0 + pre * (1.0 - sig))
        scaled = (grad_pre / jnp.concatenate([degree, degree], axis=1)).astype(BF16)
        gp_high, gp_low = split_bf16(grad_pre)
        feat_t = featt_ref[b]
        grad_self = dot(feat_t, gp_high) + dot(feat_t, gp_low)
        grad_neigh = dot_wide(jnp.transpose(raw_b), scaled)
        if b == 0:
            wsum[0], wsum[1] = grad_self, grad_neigh
        else:
            wsum[0] += grad_self
            wsum[1] += grad_neigh
        base_ref[rows_of(b), :] = dot(gp_high, ws, LAST) + dot(gp_low, ws, LAST)
        high, low = split_bf16(dot(wn, scaled, LAST))
        gt_ref[b, :BLOCK, :] = high
        gt_ref[b, BLOCK:, :] = low

    core = index_ref[2 * tile_count] % 2
    wkeep_ref[...] = wsum[core]
    wsend_ref[...] = wsum[1 - core]


def backward_kernel(group, index_ref, tiles_ref, gt_ref, acc_ref):
    block_local = gt_ref.shape[0]
    tile_count = tiles_ref.shape[0]
    dump = acc_ref.shape[0] - 1
    acc_ref[...] = jnp.zeros_like(acc_ref)

    def backward(step, carry):
        places, products = [], []
        for u in range(group):
            t = step * group + u
            row = index_ref[t]
            places.append(jnp.where(row < block_local, index_ref[tile_count + t], dump))
            both = dot(gt_ref[jnp.minimum(row, block_local - 1)], tiles_ref[t])
            products.append(both[:BLOCK] + both[BLOCK:])
        for position, product in zip(places, products):
            acc_ref[position] += product
        return carry

    lax.fori_loop(0, tile_count // group, backward, 0)


def send_kernel(square, block_local, acc_ref, send_ref):
    for q in range(4):
        for b in range(block_local):
            send_ref[q, rows_of(b), :] = acc_ref[(8 * square + 2 * q + 1) * block_local + b]


def send_weights_kernel(square, block_local, index_ref, acc_ref, wkeep_ref, wgot_ref, send_ref,
                        *parts):
    send_kernel(square, block_local, acc_ref, send_ref)
    rows = parts[0].shape[0]
    chip = index_ref[index_ref.shape[0] - 1] // 2 % 4
    for p, ref in enumerate(parts):
        span = pl.ds(pl.multiple_of((chip ^ p) * rows, rows), rows)
        ref[...] = wkeep_ref[span, :] + wgot_ref[span, :]


def put_weights(refs, ref, start):
    lanes = ref.shape[1]
    for weight in refs:
        rows, columns = weight.shape
        for part in split_bf16(weight):
            for column in range(0, columns, lanes):
                ref[pl.ds(start, rows), :] = part[:, column:column + lanes]
                start += rows


def add_weights(weight_ref, ref, start, out_ref):
    lanes = ref.shape[1]
    rows, columns = weight_ref.shape
    for column in range(0, columns, lanes):
        high = ref[pl.ds(start + column // lanes * rows, rows), :]
        low = ref[pl.ds(start + (columns + column) // lanes * rows, rows), :]
        span = pl.ds(column, lanes)
        out_ref[:, span] = weight_ref[:, span] + (high.astype(F32) + low.astype(F32))


def pair_kernel(square, kept, sent, acc_ref, got_ref, *refs):
    weights, refs = refs[:-3], refs[-3:]
    nodes = refs[0].shape[0]
    block_local = nodes // BLOCK
    places = [(refs[0], 0), (refs[1], 0), (refs[2], 0), (refs[2], nodes)]
    for q, (ref, start) in zip((*kept, *sent), places):
        for b in range(block_local):
            total = acc_ref[(8 * square + 2 * q) * block_local + b] + got_ref[q, rows_of(b), :]
            ref[pl.ds(start + b * BLOCK, BLOCK), :] = total.astype(ref.dtype)
    put_weights([ref[...] for ref in weights], refs[2], 2 * nodes)


def middle_kernel(first_ref, second_ref, got_ref, *refs):
    nodes = first_ref.shape[0]
    if len(refs) == 2:
        first_out, second_out = refs
    else:
        weight_ref, weight_send_ref, first_out, second_out, weight_out, scratch = refs
        rows = 2 * weight_ref.shape[0] * weight_ref.shape[1] // first_ref.shape[1]
        add_weights(weight_ref, got_ref, 2 * nodes, weight_out)
        add_weights(weight_send_ref, got_ref, 2 * nodes + rows, scratch)
        put_weights([scratch[...]], second_out, nodes)
    for ref, start, out in ((first_ref, 0, first_out), (second_ref, nodes, second_out)):
        total = ref[...] + got_ref[pl.ds(start, nodes), :].astype(F32)
        out[pl.ds(0, nodes), :] = total.astype(out.dtype)


def add_two_kernel(own_ref, got_ref, out_ref):
    out_ref[...] = own_ref[...] + got_ref[...]


def add_kernel(own_ref, *refs):
    total = own_ref[...].astype(F32)
    for got_ref in refs[:-1]:
        total = total + got_ref[...].astype(F32)
    refs[-1][...] = total.astype(refs[-1].dtype)


def add_weights_kernel(weight_ref, own_ref, *refs):
    got_refs, (out_ref, weight_out) = refs[:-2], refs[-2:]
    nodes = own_ref.shape[0]
    add_kernel(own_ref, *[ref.at[pl.ds(0, nodes), :] for ref in got_refs], out_ref)
    add_weights(weight_ref, got_refs[0], nodes, weight_out)


def near_kernel(base_ref, own_ref, *refs):
    for b in range(own_ref.shape[0] // BLOCK):
        total = own_ref[rows_of(b), :]
        for got_ref in refs[:-1]:
            total = total + got_ref[rows_of(b), :].astype(F32)
        refs[-1][rows_of(b), :] = base_ref[rows_of(b), :] + jnp.transpose(total)


def main_kernel(near_ref, *refs):
    for b in range(near_ref.shape[0] // BLOCK):
        total = refs[0][rows_of(b), :].astype(F32)
        for got_ref in refs[1:-1]:
            total = total + got_ref[rows_of(b), :].astype(F32)
        refs[-1][rows_of(b), :] = (near_ref[rows_of(b), :] + jnp.transpose(total)).astype(BF16)


def last_kernel(index_ref, weight_ref, other_ref, main_ref, out_ref, self_ref, neigh_ref):
    out_ref[...] = main_ref[...]
    me = index_ref[index_ref.shape[0] - 1]
    first = me % 2 == 0
    chip = me // 2 % 4
    rows = weight_ref.shape[2]
    for p in range(4):
        span = pl.ds(pl.multiple_of((chip ^ p) * rows, rows), rows)
        mine, other = weight_ref[p // 2, p % 2], other_ref[p // 2, p % 2]
        self_ref[span, :] = jnp.where(first, mine, other)
        neigh_ref[span, :] = jnp.where(first, other, mine)


def body(features, tiles, tile_row, tile_col, degree, train_mask, w_self, w_neigh, cotangent):
    n = lax.axis_size("row")
    me = lax.axis_index("row").astype(jnp.int32).reshape(1)
    squares = n // 8
    nodes, feat_in = features.shape
    hidden = w_self.shape[1]
    block_local = nodes // BLOCK
    tile_count = tiles.shape[0]
    group = max(g for g in range(1, 7) if tile_count % g == 0)
    small = n * nodes * feat_in * 4 <= 4 * MIB
    limit = (24 if small else 56) * MIB

    def result(shape, dtype, stays=True):
        kind = pltpu.VMEM if small and stays else jax.ShapeDtypeStruct
        return kind(shape, dtype)

    def placed(x, spec):
        if spec is SMEM or not small:
            return x
        return pltpu.with_memory_space_constraint(x, pltpu.HBM if spec is ANY else pltpu.VMEM)

    def call(kernel, name, out_shape, operands, in_specs=None, out_specs=None, cost_us=0.2, **more):
        specs = in_specs or [VMEM] * len(operands)
        return pl.pallas_call(
            kernel,
            out_shape=out_shape,
            in_specs=specs,
            out_specs=out_specs or jax.tree.map(lambda _: VMEM, out_shape),
            compiler_params=pltpu.CompilerParams(vmem_limit_bytes=limit),
            cost_estimate=pl.CostEstimate(
                flops=int(cost_us * 1.1e9), bytes_accessed=int(cost_us * 3.6e6), transcendentals=0),
            name=name,
            **more,
        )(*[placed(x, spec) for x, spec in zip(operands, specs)])

    wide, piece = result((nodes, feat_in), F32), result((nodes, feat_in), BF16)
    weight = result((feat_in, hidden), F32)
    chunk = result((feat_in // 4, hidden), F32)
    by_block = (block_local, BLOCK, feat_in)

    own_arguments = (
        degree.reshape(block_local, BLOCK), train_mask.reshape(block_local, BLOCK),
        w_self, w_neigh, features, cotangent,
    )
    if small:
        own_arguments = [pltpu.with_memory_space_constraint(x, pltpu.HBM) for x in own_arguments]
    tiles_near, ws, wn, degree_wide, upstream, pre_self, feat_t, own, index = pl.pallas_call(
        stage_kernel,
        out_shape=(
            result(tiles.shape, BF16),
            result(w_self.shape, BF16),
            result(w_neigh.shape, BF16),
            result(by_block, F32),
            result((nodes, hidden), F32),
            result((nodes, hidden), F32),
            result(by_block, BF16),
            piece,
            pltpu.SMEM((2 * tile_count + 1,), jnp.int32),
        ),
        in_specs=[SMEM] * 3 + [VMEM] * 6 + [ANY],
        out_specs=(VMEM,) * 8 + (SMEM,),
        scratch_shapes=[pltpu.SemaphoreType.DMA],
        compiler_params=pltpu.CompilerParams(vmem_limit_bytes=limit),
        cost_estimate=pl.CostEstimate(flops=int(3 * 1.1e9), bytes_accessed=int(3 * 3.6e6), transcendentals=0),
        name="stage_arguments",
    )(me, tile_row, tile_col, *own_arguments, placed(tiles, ANY))

    same, other = gather_by_xor(features, own, n, call, result((4, nodes, feat_in), BF16))
    operands = (index, tiles_near, ws, wn, degree_wide, upstream, pre_self, feat_t, *same, *other)
    embedded, base, wkeep, wsend, gt = call(
        functools.partial(forward_kernel, n, group),
        "forward_layer",
        (
            result((nodes, hidden), BF16, False), wide, weight, weight,
            result((block_local, 2 * feat_in, BLOCK), BF16),
        ),
        operands,
        [SMEM] + [VMEM] * (len(operands) - 1),
        cost_us=5,
        scratch_shapes=[
            pltpu.VMEM((n * block_local, BLOCK, feat_in), BF16),
            pltpu.VMEM((block_local + 1, BLOCK, feat_in), F32),
            pltpu.VMEM((2, feat_in, hidden), F32),
        ],
    )

    acc_shape = result((n * block_local + 1, feat_in, BLOCK), F32)
    acc = call(
        functools.partial(backward_kernel, group), "backward_tiles", acc_shape,
        (index, tiles_near, gt), [SMEM, VMEM, VMEM], cost_us=3.5,
    )
    send_shape = result((4, nodes, feat_in), F32)
    send = [None] * squares
    for s in range(squares - 1, -1, -1):
        if s == squares - 1:
            send[s], w0, w1, w2, w3 = call(
                functools.partial(send_weights_kernel, s, block_local), "send_weights",
                (send_shape,) + (chunk,) * 4, (index, acc, wkeep, swap(wsend, n, 1)),
                [SMEM] + [VMEM] * 3)
        else:
            send[s] = call(
                functools.partial(send_kernel, s, block_local), "send", send_shape, (acc,))

    rows = chunk.shape[0]
    more = 2 * rows * hidden // feat_in
    terms = [None] * squares
    for s in range(squares - 1, -1, -1):
        heavy = s == squares - 1
        along, across = (2, 4) if s else (4, 2)
        kept, sent = ((0, 2), (1, 3)) if s else ((0, 1), (2, 3))
        first, second, piece_out = call(
            functools.partial(pair_kernel, s, kept, sent), "pair_sum",
            (wide, wide, result((2 * nodes + 2 * more * heavy, feat_in), BF16)),
            (acc, swap(send[s], n, 1)) + ((w1, w3) if heavy else ()))
        out_shape = (wide, result((nodes + more * heavy, feat_in), BF16))
        got = swap(piece_out, n, along)
        if heavy:
            first, piece_out, wsum = call(
                middle_kernel, "middle_sum_weights", out_shape + (chunk,),
                (first, second, got, w0, w2), scratch_shapes=[pltpu.VMEM((rows, hidden), F32)])
        else:
            first, piece_out = call(middle_kernel, "middle_sum", out_shape, (first, second, got))
        terms[s] = [first, swap(piece_out, n, across)]
    near_total = call(near_kernel, "near_sum", wide, (base, *terms[0]), cost_us=NEAR_COST)
    terms[0] = [near_total]
    distance = 1
    while distance < squares:
        for s in range(squares - distance, 0, -2 * distance):
            if s == squares - 1:
                total, wsum = call(
                    add_weights_kernel, "square_sum_weights", (piece, chunk), (wsum, *terms[s]),
                    cost_us=SQUARE_COST)
            else:
                total = call(add_kernel, "square_sum", piece, terms[s], cost_us=SQUARE_COST)
            if s == distance:
                total = swap(total, n, 8 * distance)
                terms[0].append(call(add_kernel, "far_sum", wide, (total,), cost_us=FAR_COST))
            else:
                terms[s - distance].append(swap(total, n, 8 * distance))
        distance *= 2
    bit = 8
    while bit < n:
        wsum = call(add_two_kernel, "weight_sum", chunk, (wsum, swap(wsum, n, bit)))
        bit *= 2
    two = call(
        functools.partial(pack_kernel, (0, 1)), "pack_weights", result((2, rows, hidden), F32),
        (wsum, swap(wsum, n, 2), near_total))
    mine = call(
        functools.partial(pack_kernel, (0, 1)), "pack_weights", result((2, 2, rows, hidden), F32),
        (two, swap(two, n, 4)))
    main = call(main_kernel, "main_sum", piece, terms[0], cost_us=MAIN_COST)
    grad_input, grad_self, grad_neigh = call(
        last_kernel, "write_gradients",
        (
            result((nodes, feat_in), BF16, False), result((feat_in, hidden), F32, False),
            result((feat_in, hidden), F32, False),
        ),
        (index, mine, swap(mine, n, 1), main), [SMEM] + [VMEM] * 3,
    )
    return (embedded, grad_input, grad_self, grad_neigh)


def solution(mesh):
    placed = (
        P(("parts", "row"), None),
        P(("parts", "row"), None, None),
        P(("parts", "row")),
        P(("parts", "row")),
        P(("parts", "row")),
        P(("parts", "row")),
        P(),
        P(),
        P(("parts", "row"), None),
    )
    return jax.shard_map(
        body,
        mesh=mesh,
        in_specs=placed,
        out_specs=(
            P(("parts", "row"), None),
            P(("parts", "row"), None),
            P("parts", None),
            P("parts", None),
        ),
        check_vma=False,
    )
```

```python
import functools

import jax
import jax.numpy as jnp
from jax import lax
from jax.experimental import pallas as pl
from jax.experimental.pallas import tpu as pltpu
from jax.sharding import PartitionSpec as P

BLOCK = 128
F32, BF16 = jnp.float32, jnp.bfloat16
VMEM = pl.BlockSpec(memory_space=pltpu.VMEM)
SMEM = pl.BlockSpec(memory_space=pltpu.SMEM)
ANY = pl.BlockSpec(memory_space=pl.ANY)
MIB = 1024 * 1024
LAST = ((1,), (1,))
NEAR_COST, SQUARE_COST, MAIN_COST, FAR_COST, WEIGHT_COST = 1, 4, 0.2, 10, 8


def swap(x, n, offset):
    return lax.ppermute(x, "row", [(i, i ^ offset) for i in range(n)])


def gather_by_xor(x, own, n, call, pack):
    blocks = [x]
    bit = n // 2
    while bit >= 8:
        blocks = blocks + [swap(v, n, bit) for v in blocks]
        bit //= 2
    offsets = [0]
    bit = n // 2
    while bit >= 8:
        offsets = offsets + [o ^ bit for o in offsets]
        bit //= 2
    blocks = [v for _, v in sorted(zip(offsets, blocks), key=lambda pair: pair[0])]
    same = []
    for v in blocks:
        order = (2, 6, 4) if v is x else (6, 2, 4)
        square = (own if v is x else v, *[swap(v, n, offset) for offset in order])
        slots = (0, *[offset // 2 for offset in order])
        same.append(call(functools.partial(pack_kernel, slots), "pack_square", pack, square))
    return same, [swap(v, n, 1) for v in same]


def split_bf16(x):
    high = x.astype(BF16)
    return high, (x - high.astype(F32)).astype(BF16)


def dot(a, b, dims=((1,), (0,))):
    return lax.dot_general(a, b, (dims, ((), ())), preferred_element_type=F32)


def dot_wide(a, b, dims=((1,), (0,))):
    high, low = split_bf16(a)
    return dot(high, b, dims) + dot(low, b, dims)


def rows_to_lanes(row):
    return jnp.transpose(jnp.broadcast_to(row, (BLOCK, BLOCK)))


def rows_of(b):
    return pl.ds(b * BLOCK, BLOCK)


def pack_kernel(slots, *refs):
    for slot, ref in zip(slots, refs[:-1]):
        refs[-1][slot] = ref[...]


def stage_kernel(me_ref, trow_ref, tcol_ref, deg_ref, mask_ref, ws_ref, wn_ref, feat_ref, cot_ref,
                 tiles_ref, tiles_out, ws_out, wn_out, deg_out, up_out, pre_out, featt_out,
                 own_out, index_out, sem):
    copy = pltpu.make_async_copy(tiles_ref, tiles_out, sem)
    copy.start()
    block_local = feat_ref.shape[0] // BLOCK
    tile_count = trow_ref.shape[0]
    me = me_ref[0]
    index_out[2 * tile_count] = me

    def place(t, carry):
        col = tcol_ref[t]
        live = col >= 0
        col = jnp.maximum(col, 0)
        position = ((col // block_local) ^ me) * block_local + col % block_local
        row = jnp.clip(trow_ref[t] - me * block_local, 0, block_local - 1)
        index_out[t] = jnp.where(live, row, block_local)
        index_out[tile_count + t] = position
        return carry

    lax.fori_loop(0, tile_count, place, 0)
    own_out[...] = feat_ref[...]
    ws_out[...] = ws_ref[...]
    wn_out[...] = wn_ref[...]
    ws = ws_ref[...]
    for b in range(block_local):
        degree = rows_to_lanes(deg_ref[pl.ds(b, 1), :].astype(F32))
        mask = rows_to_lanes(mask_ref[pl.ds(b, 1), :].astype(F32))
        deg_out[b] = degree
        feat = feat_ref[rows_of(b), :]
        featt_out[b] = jnp.transpose(feat.astype(F32)).astype(BF16)
        pre_out[rows_of(b), :] = dot(feat, ws)
        up_out[rows_of(b), :] = cot_ref[rows_of(b), :].astype(F32) * jnp.concatenate(
            [mask, mask], axis=1)
    copy.wait()


def forward_kernel(n, group, index_ref, tiles_ref, ws_ref, wn_ref, deg_ref, up_ref, pre_ref,
                   featt_ref, *refs):
    squares = n // 8
    feat_refs, refs = refs[:2 * squares], refs[2 * squares:]
    emb_ref, base_ref, wkeep_ref, wsend_ref, gt_ref, feats, raw, wsum = refs
    block_local = deg_ref.shape[0]
    tile_count = tiles_ref.shape[0]

    raw[...] = jnp.zeros_like(raw)
    for s in range(squares):
        for q in range(4):
            for core in range(2):
                for b in range(block_local):
                    spot = (8 * s + 2 * q + core) * block_local + b
                    feats[spot] = feat_refs[core * squares + s][q, rows_of(b), :]

    def forward(step, carry):
        rows, products = [], []
        for u in range(group):
            t = step * group + u
            rows.append(index_ref[t])
            products.append(dot(tiles_ref[t], feats[index_ref[tile_count + t]]))
        for row, product in zip(rows, products):
            raw[row] += product
        return carry

    lax.fori_loop(0, tile_count // group, forward, 0)

    wn = wn_ref[...]
    ws = ws_ref[...]
    for b in range(block_local):
        degree = deg_ref[b]
        raw_b = raw[b]
        pre = pre_ref[rows_of(b), :] + dot_wide(raw_b / degree, wn)
        sig = jax.nn.sigmoid(pre)
        emb_ref[rows_of(b), :] = (pre * sig).astype(BF16)
        grad_pre = up_ref[rows_of(b), :] * sig * (1.0 + pre * (1.0 - sig))
        scaled = (grad_pre / jnp.concatenate([degree, degree], axis=1)).astype(BF16)
        gp_high, gp_low = split_bf16(grad_pre)
        feat_t = featt_ref[b]
        grad_self = dot(feat_t, gp_high) + dot(feat_t, gp_low)
        grad_neigh = dot_wide(jnp.transpose(raw_b), scaled)
        if b == 0:
            wsum[0], wsum[1] = grad_self, grad_neigh
        else:
            wsum[0] += grad_self
            wsum[1] += grad_neigh
        base_ref[rows_of(b), :] = dot(gp_high, ws, LAST) + dot(gp_low, ws, LAST)
        high, low = split_bf16(dot(wn, scaled, LAST))
        gt_ref[b, :BLOCK, :] = high
        gt_ref[b, BLOCK:, :] = low

    core = index_ref[2 * tile_count] % 2
    wkeep_ref[...] = wsum[core]
    wsend_ref[...] = wsum[1 - core]


def backward_kernel(group, index_ref, tiles_ref, gt_ref, acc_ref):
    block_local = gt_ref.shape[0]
    tile_count = tiles_ref.shape[0]
    dump = acc_ref.shape[0] - 1
    acc_ref[...] = jnp.zeros_like(acc_ref)

    def backward(step, carry):
        places, products = [], []
        for u in range(group):
            t = step * group + u
            row = index_ref[t]
            places.append(jnp.where(row < block_local, index_ref[tile_count + t], dump))
            both = dot(gt_ref[jnp.minimum(row, block_local - 1)], tiles_ref[t])
            products.append(both[:BLOCK] + both[BLOCK:])
        for position, product in zip(places, products):
            acc_ref[position] += product
        return carry

    lax.fori_loop(0, tile_count // group, backward, 0)


def send_kernel(square, block_local, acc_ref, send_ref):
    for q in range(4):
        for b in range(block_local):
            send_ref[q, rows_of(b), :] = acc_ref[(8 * square + 2 * q + 1) * block_local + b]


def cut_kernel(index_ref, wkeep_ref, wgot_ref, keep_ref, send_ref):
    rows = keep_ref.shape[0]
    square = index_ref[index_ref.shape[0] - 1] // 8 % 2
    for p, ref in enumerate((keep_ref, send_ref)):
        span = pl.ds(pl.multiple_of((square ^ p) * rows, rows), rows)
        ref[...] = wkeep_ref[span, :] + wgot_ref[span, :]


def send_weights_kernel(square, block_local, index_ref, acc_ref, wkeep_ref, wgot_ref, send_ref,
                        *halves):
    cut_kernel(index_ref, wkeep_ref, wgot_ref, *halves)
    send_kernel(square, block_local, acc_ref, send_ref)


def pair_kernel(square, acc_ref, got_ref, own_ref, *pieces):
    nodes = own_ref.shape[0]
    for q, ref in enumerate((own_ref, *pieces)):
        for b in range(nodes // BLOCK):
            kept = acc_ref[(8 * square + 2 * q) * (nodes // BLOCK) + b]
            ref[rows_of(b), :] = (kept + got_ref[q, rows_of(b), :]).astype(ref.dtype)


def pair_weights_kernel(square, acc_ref, got_ref, weight_ref, own_ref, *pieces):
    pair_kernel(square, acc_ref, got_ref, own_ref, *pieces)
    nodes, lanes = own_ref.shape
    rows, columns = weight_ref.shape
    parts = split_bf16(weight_ref[...])
    for ref in pieces:
        start = nodes
        for part in parts:
            for column in range(0, columns, lanes):
                ref[pl.ds(start, rows), :] = part[:, column:column + lanes]
                start += rows


def add_two_kernel(own_ref, got_ref, out_ref):
    out_ref[...] = own_ref[...] + got_ref[...]


def add_kernel(own_ref, *refs):
    total = own_ref[...].astype(F32)
    for got_ref in refs[:-1]:
        total = total + got_ref[...].astype(F32)
    refs[-1][...] = total.astype(refs[-1].dtype)


def near_kernel(base_ref, own_ref, weight_ref, g1, g2, g3, out_ref, weight_out):
    nodes, lanes = own_ref.shape
    for b in range(nodes // BLOCK):
        total = own_ref[rows_of(b), :]
        for got_ref in (g1, g2, g3):
            total = total + got_ref[rows_of(b), :].astype(F32)
        out_ref[rows_of(b), :] = base_ref[rows_of(b), :] + jnp.transpose(total)
    rows, columns = weight_ref.shape
    for cut in range(columns // lanes):
        span = pl.ds(cut * lanes, lanes)
        high, low = split_bf16(weight_ref[:, span])
        terms = [high.astype(F32) + low.astype(F32)]
        for ref in (g1, g2, g3):
            high = ref[pl.ds(nodes + cut * rows, rows), :]
            low = ref[pl.ds(nodes + (columns // lanes + cut) * rows, rows), :]
            terms.append(high.astype(F32) + low.astype(F32))
        weight_out[:, span] = (terms[0] + terms[1]) + (terms[2] + terms[3])


def main_kernel(near_ref, *refs):
    for b in range(near_ref.shape[0] // BLOCK):
        total = refs[0][rows_of(b), :].astype(F32)
        for got_ref in refs[1:-1]:
            total = total + got_ref[rows_of(b), :].astype(F32)
        refs[-1][rows_of(b), :] = (near_ref[rows_of(b), :] + jnp.transpose(total)).astype(BF16)


def last_kernel(index_ref, weight_ref, other_ref, main_ref, out_ref, self_ref, neigh_ref):
    out_ref[...] = main_ref[...]
    me = index_ref[index_ref.shape[0] - 1]
    first = me % 2 == 0
    square = me // 8 % 2
    rows = weight_ref.shape[1]
    for p in range(2):
        span = pl.ds(pl.multiple_of((square ^ p) * rows, rows), rows)
        mine, other = weight_ref[p], other_ref[p]
        self_ref[span, :] = jnp.where(first, mine, other)
        neigh_ref[span, :] = jnp.where(first, other, mine)


def body(features, tiles, tile_row, tile_col, degree, train_mask, w_self, w_neigh, cotangent):
    n = lax.axis_size("row")
    me = lax.axis_index("row").astype(jnp.int32).reshape(1)
    squares = n // 8
    nodes, feat_in = features.shape
    hidden = w_self.shape[1]
    block_local = nodes // BLOCK
    tile_count = tiles.shape[0]
    group = max(g for g in range(1, 7) if tile_count % g == 0)
    small = n * nodes * feat_in * 4 <= 4 * MIB
    limit = (24 if small else 56) * MIB

    def result(shape, dtype, stays=True):
        kind = pltpu.VMEM if small and stays else jax.ShapeDtypeStruct
        return kind(shape, dtype)

    def placed(x, spec):
        if spec is SMEM or not small:
            return x
        return pltpu.with_memory_space_constraint(x, pltpu.HBM if spec is ANY else pltpu.VMEM)

    def call(kernel, name, out_shape, operands, in_specs=None, out_specs=None, cost_us=0.2, **more):
        specs = in_specs or [VMEM] * len(operands)
        return pl.pallas_call(
            kernel,
            out_shape=out_shape,
            in_specs=specs,
            out_specs=out_specs or jax.tree.map(lambda _: VMEM, out_shape),
            compiler_params=pltpu.CompilerParams(vmem_limit_bytes=limit),
            cost_estimate=pl.CostEstimate(
                flops=int(cost_us * 1.1e9), bytes_accessed=int(cost_us * 3.6e6), transcendentals=0),
            name=name,
            **more,
        )(*[placed(x, spec) for x, spec in zip(operands, specs)])

    wide, piece = result((nodes, feat_in), F32), result((nodes, feat_in), BF16)
    weight = result((feat_in, hidden), F32)
    chunk = result((feat_in // 2, hidden), F32)
    by_block = (block_local, BLOCK, feat_in)

    own_arguments = (
        degree.reshape(block_local, BLOCK), train_mask.reshape(block_local, BLOCK),
        w_self, w_neigh, features, cotangent,
    )
    if small:
        own_arguments = [pltpu.with_memory_space_constraint(x, pltpu.HBM) for x in own_arguments]
    tiles_near, ws, wn, degree_wide, upstream, pre_self, feat_t, own, index = pl.pallas_call(
        stage_kernel,
        out_shape=(
            result(tiles.shape, BF16),
            result(w_self.shape, BF16),
            result(w_neigh.shape, BF16),
            result(by_block, F32),
            result((nodes, hidden), F32),
            result((nodes, hidden), F32),
            result(by_block, BF16),
            piece,
            pltpu.SMEM((2 * tile_count + 1,), jnp.int32),
        ),
        in_specs=[SMEM] * 3 + [VMEM] * 6 + [ANY],
        out_specs=(VMEM,) * 8 + (SMEM,),
        scratch_shapes=[pltpu.SemaphoreType.DMA],
        compiler_params=pltpu.CompilerParams(vmem_limit_bytes=limit),
        cost_estimate=pl.CostEstimate(flops=int(3 * 1.1e9), bytes_accessed=int(3 * 3.6e6), transcendentals=0),
        name="stage_arguments",
    )(me, tile_row, tile_col, *own_arguments, placed(tiles, ANY))

    same, other = gather_by_xor(features, own, n, call, result((4, nodes, feat_in), BF16))
    operands = (index, tiles_near, ws, wn, degree_wide, upstream, pre_self, feat_t, *same, *other)
    embedded, base, wkeep, wsend, gt = call(
        functools.partial(forward_kernel, n, group),
        "forward_layer",
        (
            result((nodes, hidden), BF16, False), wide, weight, weight,
            result((block_local, 2 * feat_in, BLOCK), BF16),
        ),
        operands,
        [SMEM] + [VMEM] * (len(operands) - 1),
        cost_us=5,
        scratch_shapes=[
            pltpu.VMEM((n * block_local, BLOCK, feat_in), BF16),
            pltpu.VMEM((block_local + 1, BLOCK, feat_in), F32),
            pltpu.VMEM((2, feat_in, hidden), F32),
        ],
    )

    acc_shape = result((n * block_local + 1, feat_in, BLOCK), F32)
    acc = call(
        functools.partial(backward_kernel, group), "backward_tiles", acc_shape,
        (index, tiles_near, gt), [SMEM, VMEM, VMEM], cost_us=3.5,
    )
    send_shape = result((4, nodes, feat_in), F32)
    send = [None] * squares
    for s in range(squares - 1, -1, -1):
        if s == squares - 1:
            send[s], wsum, wsend = call(
                functools.partial(send_weights_kernel, s, block_local), "send_weights",
                (send_shape, chunk, chunk), (index, acc, wkeep, swap(wsend, n, 1)),
                [SMEM] + [VMEM] * 3)
        else:
            send[s] = call(
                functools.partial(send_kernel, s, block_local), "send", send_shape, (acc,))

    terms = [None] * squares
    for s in range(squares - 1, 0, -1):
        own, *pieces = call(
            functools.partial(pair_kernel, s), "pair_sum", (wide, piece, piece, piece),
            (acc, swap(send[s], n, 1)))
        terms[s] = [own, *[swap(x, n, 2 * q + 2) for q, x in enumerate(pieces)]]
    wsum = call(add_two_kernel, "weight_sum", chunk, (wsum, swap(wsend, n, 8)), cost_us=WEIGHT_COST)
    bit = 16
    while bit < n:
        wsum = call(add_two_kernel, "weight_sum", chunk, (wsum, swap(wsum, n, bit)))
        bit *= 2
    rows = chunk.shape[0]
    extra = result((nodes + 2 * rows * (hidden // feat_in), feat_in), BF16)
    own, *pieces = call(
        functools.partial(pair_weights_kernel, 0), "pair_sum_weights", (wide, extra, extra, extra),
        (acc, swap(send[0], n, 1), wsum))
    near_total, wsum = call(
        near_kernel, "near_sum", (wide, chunk),
        (base, own, wsum, *[swap(x, n, 2 * q + 2) for q, x in enumerate(pieces)]),
        cost_us=NEAR_COST)
    terms[0] = [near_total]
    distance = 1
    while distance < squares:
        for s in range(squares - distance, 0, -2 * distance):
            total = call(add_kernel, "square_sum", piece, terms[s], cost_us=SQUARE_COST)
            if s == distance:
                total = swap(total, n, 8 * distance)
                terms[0].append(call(add_kernel, "far_sum", wide, (total,), cost_us=FAR_COST))
            else:
                terms[s - distance].append(swap(total, n, 8 * distance))
        distance *= 2
    mine = call(
        functools.partial(pack_kernel, (0, 1)), "pack_weights", result((2, rows, hidden), F32),
        (wsum, swap(wsum, n, 8)))
    main = call(main_kernel, "main_sum", piece, terms[0], cost_us=MAIN_COST)
    grad_input, grad_self, grad_neigh = call(
        last_kernel, "write_gradients",
        (
            result((nodes, feat_in), BF16, False), result((feat_in, hidden), F32, False),
            result((feat_in, hidden), F32, False),
        ),
        (index, mine, swap(mine, n, 1), main), [SMEM] + [VMEM] * 3,
    )
    return (embedded, grad_input, grad_self, grad_neigh)


def solution(mesh):
    placed = (
        P(("parts", "row"), None),
        P(("parts", "row"), None, None),
        P(("parts", "row")),
        P(("parts", "row")),
        P(("parts", "row")),
        P(("parts", "row")),
        P(),
        P(),
        P(("parts", "row"), None),
    )
    return jax.shard_map(
        body,
        mesh=mesh,
        in_specs=placed,
        out_specs=(
            P(("parts", "row"), None),
            P(("parts", "row"), None),
            P("parts", None),
            P("parts", None),
        ),
        check_vma=False,
    )
```

```python
import functools

import jax
import jax.numpy as jnp
from jax import lax
from jax.experimental import pallas as pl
from jax.experimental.pallas import tpu as pltpu
from jax.sharding import PartitionSpec as P

BLOCK = 128
F32, BF16 = jnp.float32, jnp.bfloat16
VMEM = pl.BlockSpec(memory_space=pltpu.VMEM)
SMEM = pl.BlockSpec(memory_space=pltpu.SMEM)
ANY = pl.BlockSpec(memory_space=pl.ANY)
MIB = 1024 * 1024
LAST = ((1,), (1,))
NEAR_COST, SQUARE_COST, MAIN_COST, FAR_COST = 4, 0.2, 0.2, 10


def swap(x, n, offset):
    return lax.ppermute(x, "row", [(i, i ^ offset) for i in range(n)])


def gather_by_xor(x, own, n, call, pack):
    blocks = [x]
    bit = n // 2
    while bit >= 8:
        blocks = blocks + [swap(v, n, bit) for v in blocks]
        bit //= 2
    offsets = [0]
    bit = n // 2
    while bit >= 8:
        offsets = offsets + [o ^ bit for o in offsets]
        bit //= 2
    blocks = [v for _, v in sorted(zip(offsets, blocks), key=lambda pair: pair[0])]
    same = []
    for v in blocks:
        order = (2, 6, 4) if v is x else (6, 2, 4)
        square = (own if v is x else v, *[swap(v, n, offset) for offset in order])
        slots = (0, *[offset // 2 for offset in order])
        same.append(call(functools.partial(pack_kernel, slots), "pack_square", pack, square))
    return same, [swap(v, n, 1) for v in same]


def split_bf16(x):
    high = x.astype(BF16)
    return high, (x - high.astype(F32)).astype(BF16)


def dot(a, b, dims=((1,), (0,))):
    return lax.dot_general(a, b, (dims, ((), ())), preferred_element_type=F32)


def dot_wide(a, b, dims=((1,), (0,))):
    high, low = split_bf16(a)
    return dot(high, b, dims) + dot(low, b, dims)


def rows_to_lanes(row):
    return jnp.transpose(jnp.broadcast_to(row, (BLOCK, BLOCK)))


def rows_of(b):
    return pl.ds(b * BLOCK, BLOCK)


def pack_kernel(slots, *refs):
    for slot, ref in zip(slots, refs[:-1]):
        refs[-1][slot] = ref[...]


def stage_kernel(me_ref, trow_ref, tcol_ref, deg_ref, mask_ref, ws_ref, wn_ref, feat_ref, cot_ref,
                 tiles_ref, tiles_out, ws_out, wn_out, inverse_out, up_out, pre_out, featt_out,
                 own_out, index_out, sem):
    copy = pltpu.make_async_copy(tiles_ref, tiles_out, sem)
    copy.start()
    block_local = feat_ref.shape[0] // BLOCK
    tile_count = trow_ref.shape[0]
    me = me_ref[0]
    index_out[2 * tile_count] = me

    def place(t, carry):
        col = tcol_ref[t]
        live = col >= 0
        col = jnp.maximum(col, 0)
        position = ((col // block_local) ^ me) * block_local + col % block_local
        row = jnp.clip(trow_ref[t] - me * block_local, 0, block_local - 1)
        index_out[t] = jnp.where(live, row, block_local)
        index_out[tile_count + t] = position
        return carry

    lax.fori_loop(0, tile_count, place, 0)
    own_out[...] = feat_ref[...]
    ws_out[...] = ws_ref[...]
    wn_out[...] = wn_ref[...]
    ws = ws_ref[...]
    for b in range(block_local):
        degree = rows_to_lanes(deg_ref[pl.ds(b, 1), :].astype(F32))
        mask = rows_to_lanes(mask_ref[pl.ds(b, 1), :].astype(F32))
        inverse_out[b] = 1.0 / degree
        feat = feat_ref[rows_of(b), :]
        featt_out[b] = jnp.transpose(feat.astype(F32)).astype(BF16)
        pre_out[rows_of(b), :] = dot(feat, ws)
        up_out[rows_of(b), :] = cot_ref[rows_of(b), :].astype(F32) * jnp.concatenate(
            [mask, mask], axis=1)
    copy.wait()


def forward_kernel(n, group, index_ref, tiles_ref, ws_ref, wn_ref, inverse_ref, up_ref, pre_ref,
                   featt_ref, *refs):
    squares = n // 8
    feat_refs, refs = refs[:2 * squares], refs[2 * squares:]
    emb_ref, base_ref, wkeep_ref, wsend_ref, gt_ref, feats, raw, wsum = refs
    block_local = inverse_ref.shape[0]
    tile_count = tiles_ref.shape[0]

    raw[...] = jnp.zeros_like(raw)
    for s in range(squares):
        for q in range(4):
            for core in range(2):
                for b in range(block_local):
                    spot = (8 * s + 2 * q + core) * block_local + b
                    feats[spot] = feat_refs[core * squares + s][q, rows_of(b), :]

    def forward(step, carry):
        rows, products = [], []
        for u in range(group):
            t = step * group + u
            rows.append(index_ref[t])
            products.append(dot(tiles_ref[t], feats[index_ref[tile_count + t]]))
        for row, product in zip(rows, products):
            raw[row] += product
        return carry

    lax.fori_loop(0, tile_count // group, forward, 0)

    wn = wn_ref[...]
    ws = ws_ref[...]
    for b in range(block_local):
        inverse = inverse_ref[b]
        raw_b = raw[b]
        pre = pre_ref[rows_of(b), :] + dot_wide(raw_b * inverse, wn)
        sig = jax.nn.sigmoid(pre)
        emb_ref[rows_of(b), :] = (pre * sig).astype(BF16)
        grad_pre = up_ref[rows_of(b), :] * sig * (1.0 + pre * (1.0 - sig))
        scaled = (grad_pre * jnp.concatenate([inverse, inverse], axis=1)).astype(BF16)
        gp_high, gp_low = split_bf16(grad_pre)
        feat_t = featt_ref[b]
        grad_self = dot(feat_t, gp_high) + dot(feat_t, gp_low)
        grad_neigh = dot_wide(jnp.transpose(raw_b), scaled)
        if b == 0:
            wsum[0], wsum[1] = grad_self, grad_neigh
        else:
            wsum[0] += grad_self
            wsum[1] += grad_neigh
        base_ref[rows_of(b), :] = dot(gp_high, ws, LAST) + dot(gp_low, ws, LAST)
        high, low = split_bf16(dot(wn, scaled, LAST))
        gt_ref[b, :BLOCK, :] = high
        gt_ref[b, BLOCK:, :] = low

    core = index_ref[2 * tile_count] % 2
    wkeep_ref[...] = wsum[core]
    wsend_ref[...] = wsum[1 - core]


def backward_kernel(group, index_ref, tiles_ref, gt_ref, acc_ref):
    block_local = gt_ref.shape[0]
    tile_count = tiles_ref.shape[0]
    dump = acc_ref.shape[0] - 1
    acc_ref[...] = jnp.zeros_like(acc_ref)

    def backward(step, carry):
        places, products = [], []
        for u in range(group):
            t = step * group + u
            row = index_ref[t]
            places.append(jnp.where(row < block_local, index_ref[tile_count + t], dump))
            both = dot(gt_ref[jnp.minimum(row, block_local - 1)], tiles_ref[t])
            products.append(both[:BLOCK] + both[BLOCK:])
        for position, product in zip(places, products):
            acc_ref[position] += product
        return carry

    lax.fori_loop(0, tile_count // group, backward, 0)


def send_kernel(square, block_local, acc_ref, send_ref):
    for q in range(4):
        for b in range(block_local):
            send_ref[q, rows_of(b), :] = acc_ref[(8 * square + 2 * q + 1) * block_local + b]


def send_weights_kernel(square, block_local, index_ref, acc_ref, wkeep_ref, wgot_ref, send_ref,
                        *parts):
    send_kernel(square, block_local, acc_ref, send_ref)
    rows = parts[0].shape[0]
    chip = index_ref[index_ref.shape[0] - 1] // 2 % 4
    for p, ref in enumerate(parts):
        span = pl.ds(pl.multiple_of((chip ^ p) * rows, rows), rows)
        ref[...] = wkeep_ref[span, :] + wgot_ref[span, :]


def pair_kernel(square, acc_ref, got_ref, own_ref, *pieces):
    block_local = own_ref.shape[0] // BLOCK
    for q, ref in enumerate((own_ref, *pieces)):
        for b in range(block_local):
            kept = acc_ref[(8 * square + 2 * q) * block_local + b]
            ref[rows_of(b), :] = (kept + got_ref[q, rows_of(b), :]).astype(ref.dtype)


def pair_weights_kernel(square, acc_ref, got_ref, w1, w2, w3, own_ref, *pieces):
    pair_kernel(square, acc_ref, got_ref, own_ref, *pieces)
    nodes, lanes = own_ref.shape
    for weight_ref, ref in zip((w1, w2, w3), pieces):
        rows, columns = weight_ref.shape
        start = nodes
        for part in split_bf16(weight_ref[...]):
            for column in range(0, columns, lanes):
                ref[pl.ds(start, rows), :] = part[:, column:column + lanes]
                start += rows


def add_two_kernel(own_ref, got_ref, out_ref):
    out_ref[...] = own_ref[...] + got_ref[...]


def add_kernel(own_ref, *refs):
    total = own_ref[...].astype(F32)
    for got_ref in refs[:-1]:
        total = total + got_ref[...].astype(F32)
    refs[-1][...] = total.astype(refs[-1].dtype)


def add_weights_kernel(weight_ref, own_ref, *refs):
    got_refs, (out_ref, weight_out) = refs[:-2], refs[-2:]
    nodes, lanes = own_ref.shape
    add_kernel(own_ref, *[ref.at[pl.ds(0, nodes), :] for ref in got_refs], out_ref)
    rows, columns = weight_ref.shape
    cuts = columns // lanes
    for cut in range(cuts):
        span = pl.ds(cut * lanes, lanes)
        total = weight_ref[:, span]
        for ref in got_refs[:3]:
            high = ref[pl.ds(nodes + cut * rows, rows), :]
            low = ref[pl.ds(nodes + (cuts + cut) * rows, rows), :]
            total = total + (high.astype(F32) + low.astype(F32))
        weight_out[:, span] = total


def near_kernel(base_ref, own_ref, *refs):
    for b in range(own_ref.shape[0] // BLOCK):
        total = own_ref[rows_of(b), :]
        for got_ref in refs[:-1]:
            total = total + got_ref[rows_of(b), :].astype(F32)
        refs[-1][rows_of(b), :] = base_ref[rows_of(b), :] + jnp.transpose(total)


def main_kernel(near_ref, *refs):
    for b in range(near_ref.shape[0] // BLOCK):
        total = refs[0][rows_of(b), :].astype(F32)
        for got_ref in refs[1:-1]:
            total = total + got_ref[rows_of(b), :].astype(F32)
        refs[-1][rows_of(b), :] = (near_ref[rows_of(b), :] + jnp.transpose(total)).astype(BF16)


def last_kernel(index_ref, weight_ref, other_ref, self_ref, neigh_ref):
    me = index_ref[index_ref.shape[0] - 1]
    first = me % 2 == 0
    chip = me // 2 % 4
    rows = weight_ref.shape[1]
    for p in range(4):
        span = pl.ds(pl.multiple_of((chip ^ p) * rows, rows), rows)
        mine, other = weight_ref[p], other_ref[p]
        self_ref[span, :] = jnp.where(first, mine, other)
        neigh_ref[span, :] = jnp.where(first, other, mine)


def body(features, tiles, tile_row, tile_col, degree, train_mask, w_self, w_neigh, cotangent):
    n = lax.axis_size("row")
    me = lax.axis_index("row").astype(jnp.int32).reshape(1)
    squares = n // 8
    nodes, feat_in = features.shape
    hidden = w_self.shape[1]
    block_local = nodes // BLOCK
    tile_count = tiles.shape[0]
    group = max(g for g in range(1, 7) if tile_count % g == 0)
    small = n * nodes * feat_in * 4 <= 4 * MIB
    limit = (24 if small else 56) * MIB

    def result(shape, dtype, stays=True):
        kind = pltpu.VMEM if small and stays else jax.ShapeDtypeStruct
        return kind(shape, dtype)

    def placed(x, spec):
        if spec is SMEM or not small:
            return x
        return pltpu.with_memory_space_constraint(x, pltpu.HBM if spec is ANY else pltpu.VMEM)

    def call(kernel, name, out_shape, operands, in_specs=None, out_specs=None, cost_us=0.2, **more):
        specs = in_specs or [VMEM] * len(operands)
        return pl.pallas_call(
            kernel,
            out_shape=out_shape,
            in_specs=specs,
            out_specs=out_specs or jax.tree.map(lambda _: VMEM, out_shape),
            compiler_params=pltpu.CompilerParams(vmem_limit_bytes=limit),
            cost_estimate=pl.CostEstimate(
                flops=int(cost_us * 1.1e9), bytes_accessed=int(cost_us * 3.6e6), transcendentals=0),
            name=name,
            **more,
        )(*[placed(x, spec) for x, spec in zip(operands, specs)])

    wide, piece = result((nodes, feat_in), F32), result((nodes, feat_in), BF16)
    weight = result((feat_in, hidden), F32)
    chunk = result((feat_in // 4, hidden), F32)
    by_block = (block_local, BLOCK, feat_in)

    own_arguments = (
        degree.reshape(block_local, BLOCK), train_mask.reshape(block_local, BLOCK),
        w_self, w_neigh, features, cotangent,
    )
    if small:
        own_arguments = [pltpu.with_memory_space_constraint(x, pltpu.HBM) for x in own_arguments]
    tiles_near, ws, wn, inverse, upstream, pre_self, feat_t, own, index = pl.pallas_call(
        stage_kernel,
        out_shape=(
            result(tiles.shape, BF16),
            result(w_self.shape, BF16),
            result(w_neigh.shape, BF16),
            result(by_block, F32),
            result((nodes, hidden), F32),
            result((nodes, hidden), F32),
            result(by_block, BF16),
            piece,
            pltpu.SMEM((2 * tile_count + 1,), jnp.int32),
        ),
        in_specs=[SMEM] * 3 + [VMEM] * 6 + [ANY],
        out_specs=(VMEM,) * 8 + (SMEM,),
        scratch_shapes=[pltpu.SemaphoreType.DMA],
        compiler_params=pltpu.CompilerParams(vmem_limit_bytes=limit),
        cost_estimate=pl.CostEstimate(flops=int(3 * 1.1e9), bytes_accessed=int(3 * 3.6e6), transcendentals=0),
        name="stage_arguments",
    )(me, tile_row, tile_col, *own_arguments, placed(tiles, ANY))

    same, other = gather_by_xor(features, own, n, call, result((4, nodes, feat_in), BF16))
    operands = (index, tiles_near, ws, wn, inverse, upstream, pre_self, feat_t, *same, *other)
    embedded, base, wkeep, wsend, gt = call(
        functools.partial(forward_kernel, n, group),
        "forward_layer",
        (
            result((nodes, hidden), BF16, False), wide, weight, weight,
            result((block_local, 2 * feat_in, BLOCK), BF16),
        ),
        operands,
        [SMEM] + [VMEM] * (len(operands) - 1),
        cost_us=5,
        scratch_shapes=[
            pltpu.VMEM((n * block_local, BLOCK, feat_in), BF16),
            pltpu.VMEM((block_local + 1, BLOCK, feat_in), F32),
            pltpu.VMEM((2, feat_in, hidden), F32),
        ],
    )

    acc_shape = result((n * block_local + 1, feat_in, BLOCK), F32)
    acc = call(
        functools.partial(backward_kernel, group), "backward_tiles", acc_shape,
        (index, tiles_near, gt), [SMEM, VMEM, VMEM], cost_us=3.5,
    )
    send_shape = result((4, nodes, feat_in), F32)
    send = [None] * squares
    for s in range(squares - 1, -1, -1):
        if s == squares - 1:
            send[s], w0, w1, w2, w3 = call(
                functools.partial(send_weights_kernel, s, block_local), "send_weights",
                (send_shape,) + (chunk,) * 4, (index, acc, wkeep, swap(wsend, n, 1)),
                [SMEM] + [VMEM] * 3)
        else:
            send[s] = call(
                functools.partial(send_kernel, s, block_local), "send", send_shape, (acc,))

    extra = result((nodes + 2 * chunk.shape[0] * (hidden // feat_in), feat_in), BF16)
    terms = [None] * squares
    for s in range(squares - 1, -1, -1):
        operands = (acc, swap(send[s], n, 1))
        if s == squares - 1:
            own, *pieces = call(
                functools.partial(pair_weights_kernel, s), "pair_sum_weights", (wide, extra, extra, extra),
                operands + (w1, w2, w3))
        else:
            own, *pieces = call(
                functools.partial(pair_kernel, s), "pair_sum", (wide, piece, piece, piece), operands)
        terms[s] = [own, *[swap(x, n, 2 * q + 2) for q, x in enumerate(pieces)]]
    near_total = call(near_kernel, "near_sum", wide, (base, *terms[0]), cost_us=NEAR_COST)
    terms[0] = [near_total]
    distance = 1
    while distance < squares:
        for s in range(squares - distance, 0, -2 * distance):
            if s == squares - 1:
                total, wsum = call(
                    add_weights_kernel, "square_sum_weights", (piece, chunk), (w0, *terms[s]),
                    cost_us=SQUARE_COST)
            else:
                total = call(add_kernel, "square_sum", piece, terms[s], cost_us=SQUARE_COST)
            if s == distance:
                total = swap(total, n, 8 * distance)
                terms[0].append(call(add_kernel, "far_sum", wide, (total,), cost_us=FAR_COST))
            else:
                terms[s - distance].append(swap(total, n, 8 * distance))
        distance *= 2
    bit = 8
    while bit < n:
        wsum = call(add_two_kernel, "weight_sum", chunk, (wsum, swap(wsum, n, bit)))
        bit *= 2
    rows = chunk.shape[0]
    mine = call(
        functools.partial(pack_kernel, (0, 1, 2, 3)), "pack_weights",
        result((4, rows, hidden), F32),
        (wsum, *[swap(wsum, n, offset) for offset in (2, 4, 6)], near_total))
    grad_input = call(
        main_kernel, "grad_input_sum", result((nodes, feat_in), BF16, False), terms[0],
        cost_us=MAIN_COST)
    full = result((feat_in, hidden), F32, False)
    grad_self, grad_neigh = call(
        last_kernel, "write_weights", (full, full), (index, mine, swap(mine, n, 1)),
        [SMEM] + [VMEM] * 2)
    return (embedded, grad_input, grad_self, grad_neigh)


def solution(mesh):
    placed = (
        P(("parts", "row"), None),
        P(("parts", "row"), None, None),
        P(("parts", "row")),
        P(("parts", "row")),
        P(("parts", "row")),
        P(("parts", "row")),
        P(),
        P(),
        P(("parts", "row"), None),
    )
    return jax.shard_map(
        body,
        mesh=mesh,
        in_specs=placed,
        out_specs=(
            P(("parts", "row"), None),
            P(("parts", "row"), None),
            P("parts", None),
            P("parts", None),
        ),
        check_vma=False,
    )
```

```python
import functools

import jax
import jax.numpy as jnp
from jax import lax
from jax.experimental import pallas as pl
from jax.experimental.pallas import tpu as pltpu
from jax.sharding import PartitionSpec as P

BLOCK = 128
F32, BF16 = jnp.float32, jnp.bfloat16
VMEM = pl.BlockSpec(memory_space=pltpu.VMEM)
SMEM = pl.BlockSpec(memory_space=pltpu.SMEM)
ANY = pl.BlockSpec(memory_space=pl.ANY)
MIB = 1024 * 1024
LAST = ((1,), (1,))
NEAR_COST, SQUARE_COST, MAIN_COST = 8, 4, 10


def swap(x, n, offset):
    return lax.ppermute(x, "row", [(i, i ^ offset) for i in range(n)])


def gather_by_xor(x, own, n, call, pack):
    blocks = [x]
    bit = n // 2
    while bit >= 8:
        blocks = blocks + [swap(v, n, bit) for v in blocks]
        bit //= 2
    offsets = [0]
    bit = n // 2
    while bit >= 8:
        offsets = offsets + [o ^ bit for o in offsets]
        bit //= 2
    blocks = [v for _, v in sorted(zip(offsets, blocks), key=lambda pair: pair[0])]
    same = []
    for v in blocks:
        order = (2, 6, 4) if v is x else (6, 2, 4)
        square = (own if v is x else v, *[swap(v, n, offset) for offset in order])
        slots = (0, *[offset // 2 for offset in order])
        same.append(call(functools.partial(pack_kernel, slots), "pack_square", pack, square))
    return same, [swap(v, n, 1) for v in same]


def split_bf16(x):
    high = x.astype(BF16)
    return high, (x - high.astype(F32)).astype(BF16)


def dot(a, b, dims=((1,), (0,))):
    return lax.dot_general(a, b, (dims, ((), ())), preferred_element_type=F32)


def dot_wide(a, b, dims=((1,), (0,))):
    high, low = split_bf16(a)
    return dot(high, b, dims) + dot(low, b, dims)


def rows_to_lanes(row):
    return jnp.transpose(jnp.broadcast_to(row, (BLOCK, BLOCK)))


def rows_of(b):
    return pl.ds(b * BLOCK, BLOCK)


def pack_kernel(slots, *refs):
    for slot, ref in zip(slots, refs[:-1]):
        refs[-1][slot] = ref[...]


def stage_kernel(dumps, me_ref, trow_ref, tcol_ref, deg_ref, mask_ref, ws_ref, wn_ref, feat_ref, cot_ref,
                 tiles_ref, tiles_out, ws_out, wn_out, inverse_out, up_out, pre_out, featt_out,
                 own_out, index_out, sem):
    copy = pltpu.make_async_copy(tiles_ref, tiles_out, sem)
    copy.start()
    block_local = feat_ref.shape[0] // BLOCK
    tile_count = trow_ref.shape[0]
    me = me_ref[0]
    index_out[index_out.shape[0] - 1] = me

    def clear(i, carry):
        for section in range(2):
            index_out[3 * section * tile_count + i] = 0
            index_out[(3 * section + 1) * tile_count + i] = block_local
            index_out[(3 * section + 2) * tile_count + i] = dumps[section]
        return carry

    def place(t, counts):
        col = tcol_ref[t]
        live = col >= 0
        col = jnp.maximum(col, 0)
        chip_core = (col // block_local) ^ me
        far = chip_core >= 8
        position = jnp.where(far, chip_core - 8, chip_core) * block_local + col % block_local
        row = jnp.clip(trow_ref[t] - me * block_local, 0, block_local - 1)
        near_count, far_count = counts
        spot = jnp.where(far, 3 * tile_count + far_count, near_count)

        @pl.when(live)
        def _():
            index_out[spot] = t
            index_out[spot + tile_count] = row
            index_out[spot + 2 * tile_count] = position

        add = live.astype(jnp.int32)
        add_far = far.astype(jnp.int32) * add
        return near_count + add - add_far, far_count + add_far

    lax.fori_loop(0, tile_count, clear, 0)
    near_count, far_count = lax.fori_loop(0, tile_count, place, (jnp.int32(0), jnp.int32(0)))
    index_out[6 * tile_count] = near_count
    index_out[6 * tile_count + 1] = far_count
    own_out[...] = feat_ref[...]
    ws_out[...] = ws_ref[...]
    wn_out[...] = wn_ref[...]
    ws = ws_ref[...]
    for b in range(block_local):
        degree = rows_to_lanes(deg_ref[pl.ds(b, 1), :].astype(F32))
        mask = rows_to_lanes(mask_ref[pl.ds(b, 1), :].astype(F32))
        inverse_out[b] = 1.0 / degree
        feat = feat_ref[rows_of(b), :]
        featt_out[b] = jnp.transpose(feat.astype(F32)).astype(BF16)
        pre_out[rows_of(b), :] = dot(feat, ws)
        up_out[rows_of(b), :] = cot_ref[rows_of(b), :].astype(F32) * jnp.concatenate(
            [mask, mask], axis=1)
    copy.wait()


def over_tiles(section, group, index_ref, product, add):
    tile_count = (index_ref.shape[0] - 3) // 6
    start = 3 * section * tile_count

    def step(i, carry):
        spots = [start + i * group + u for u in range(group)]
        entries = [
            (index_ref[spot], index_ref[spot + tile_count], index_ref[spot + 2 * tile_count])
            for spot in spots
        ]
        products = [product(*entry) for entry in entries]
        for entry, value in zip(entries, products):
            add(*entry, value)
        return carry

    count = index_ref[6 * tile_count + section]
    lax.fori_loop(0, (count + group - 1) // group, step, 0)


def gathered_products(section, group, index_ref, tiles_ref, feat_refs, feats, raw):
    squares = len(feat_refs) // 2
    block_local = raw.shape[0] - 1
    for s in range(squares):
        for q in range(4):
            for core in range(2):
                for b in range(block_local):
                    spot = (8 * s + 2 * q + core) * block_local + b
                    feats[spot] = feat_refs[core * squares + s][q, rows_of(b), :]

    def add(t, row, position, value):
        raw[row] += value

    over_tiles(
        section, group, index_ref,
        lambda t, row, position: dot(tiles_ref[t], feats[jnp.minimum(position, feats.shape[0] - 1)]),
        add)


def forward_near_kernel(group, index_ref, tiles_ref, same_ref, other_ref, raw, feats):
    raw[...] = jnp.zeros_like(raw)
    gathered_products(0, group, index_ref, tiles_ref, (same_ref, other_ref), feats, raw)


def forward_kernel(group, far, index_ref, tiles_ref, ws_ref, wn_ref, inverse_ref, up_ref, pre_ref,
                   featt_ref, near_ref, *refs):
    feat_refs, refs = refs[:2 * far], refs[2 * far:]
    emb_ref, base_ref, wkeep_ref, wsend_ref, gt_ref, feats, raw, wsum = refs
    block_local = inverse_ref.shape[0]
    raw[...] = near_ref[...]
    gathered_products(1, group, index_ref, tiles_ref, feat_refs, feats, raw)

    wn = wn_ref[...]
    ws = ws_ref[...]
    for b in range(block_local):
        inverse = inverse_ref[b]
        raw_b = raw[b]
        pre = pre_ref[rows_of(b), :] + dot_wide(raw_b * inverse, wn)
        sig = jax.nn.sigmoid(pre)
        emb_ref[rows_of(b), :] = (pre * sig).astype(BF16)
        grad_pre = up_ref[rows_of(b), :] * sig * (1.0 + pre * (1.0 - sig))
        scaled = (grad_pre * jnp.concatenate([inverse, inverse], axis=1)).astype(BF16)
        gp_high, gp_low = split_bf16(grad_pre)
        feat_t = featt_ref[b]
        grad_self = dot(feat_t, gp_high) + dot(feat_t, gp_low)
        grad_neigh = dot_wide(jnp.transpose(raw_b), scaled)
        if b == 0:
            wsum[0], wsum[1] = grad_self, grad_neigh
        else:
            wsum[0] += grad_self
            wsum[1] += grad_neigh
        base_ref[rows_of(b), :] = dot(gp_high, ws, LAST) + dot(gp_low, ws, LAST)
        high, low = split_bf16(dot(wn, scaled, LAST))
        gt_ref[b, :BLOCK, :] = high
        gt_ref[b, BLOCK:, :] = low

    core = index_ref[index_ref.shape[0] - 1] % 2
    wkeep_ref[...] = wsum[core]
    wsend_ref[...] = wsum[1 - core]


def backward_kernel(section, group, index_ref, tiles_ref, gt_ref, acc_ref):
    block_local = gt_ref.shape[0]
    acc_ref[...] = jnp.zeros_like(acc_ref)

    def product(t, row, position):
        both = dot(gt_ref[jnp.minimum(row, block_local - 1)], tiles_ref[t])
        return both[:BLOCK] + both[BLOCK:]

    def add(t, row, position, value):
        acc_ref[position] += value

    over_tiles(section, group, index_ref, product, add)


def send_kernel(square, acc_ref, *refs):
    send_ref = refs[-1]
    block_local = send_ref.shape[1] // BLOCK
    for q in range(4):
        for b in range(block_local):
            send_ref[q, rows_of(b), :] = acc_ref[(8 * square + 2 * q + 1) * block_local + b]


def cut_kernel(index_ref, wkeep_ref, wgot_ref, *parts):
    rows = parts[0].shape[0]
    chip = index_ref[index_ref.shape[0] - 1] // 2 % 4
    for p, ref in enumerate(parts):
        span = pl.ds(pl.multiple_of((chip ^ p) * rows, rows), rows)
        ref[...] = wkeep_ref[span, :] + wgot_ref[span, :]


def pair_kernel(square, acc_ref, got_ref, own_ref, *pieces):
    block_local = own_ref.shape[0] // BLOCK
    for q, ref in enumerate((own_ref, *pieces)):
        for b in range(block_local):
            kept = acc_ref[(8 * square + 2 * q) * block_local + b]
            ref[rows_of(b), :] = (kept + got_ref[q, rows_of(b), :]).astype(ref.dtype)


def pair_weights_kernel(square, acc_ref, got_ref, w1, w2, w3, own_ref, *pieces):
    pair_kernel(square, acc_ref, got_ref, own_ref, *pieces)
    nodes, lanes = own_ref.shape
    for weight_ref, ref in zip((w1, w2, w3), pieces):
        rows, columns = weight_ref.shape
        start = nodes
        for part in split_bf16(weight_ref[...]):
            for column in range(0, columns, lanes):
                ref[pl.ds(start, rows), :] = part[:, column:column + lanes]
                start += rows


def add_two_kernel(own_ref, got_ref, out_ref):
    out_ref[...] = own_ref[...] + got_ref[...]


def add_kernel(own_ref, *refs):
    total = own_ref[...]
    for got_ref in refs[:-1]:
        total = total + got_ref[...].astype(F32)
    refs[-1][...] = total.astype(BF16)


def add_weights_kernel(weight_ref, own_ref, *refs):
    got_refs, (out_ref, weight_out) = refs[:-2], refs[-2:]
    nodes, lanes = own_ref.shape
    add_kernel(own_ref, *[ref.at[pl.ds(0, nodes), :] for ref in got_refs], out_ref)
    rows, columns = weight_ref.shape
    cuts = columns // lanes
    for cut in range(cuts):
        span = pl.ds(cut * lanes, lanes)
        total = weight_ref[:, span]
        for ref in got_refs[:3]:
            high = ref[pl.ds(nodes + cut * rows, rows), :]
            low = ref[pl.ds(nodes + (cuts + cut) * rows, rows), :]
            total = total + (high.astype(F32) + low.astype(F32))
        weight_out[:, span] = total


def near_kernel(base_ref, own_ref, *refs):
    for b in range(own_ref.shape[0] // BLOCK):
        total = own_ref[rows_of(b), :]
        for got_ref in refs[:-1]:
            total = total + got_ref[rows_of(b), :].astype(F32)
        refs[-1][rows_of(b), :] = base_ref[rows_of(b), :] + jnp.transpose(total)


def main_kernel(near_ref, *refs):
    for b in range(near_ref.shape[0] // BLOCK):
        total = refs[0][rows_of(b), :].astype(F32)
        for got_ref in refs[1:-1]:
            total = total + got_ref[rows_of(b), :].astype(F32)
        refs[-1][rows_of(b), :] = (near_ref[rows_of(b), :] + jnp.transpose(total)).astype(BF16)


def last_kernel(index_ref, weight_ref, other_ref, self_ref, neigh_ref):
    me = index_ref[index_ref.shape[0] - 1]
    first = me % 2 == 0
    chip = me // 2 % 4
    rows = weight_ref.shape[2]
    for p in range(4):
        span = pl.ds(pl.multiple_of((chip ^ p) * rows, rows), rows)
        mine, other = weight_ref[p // 2, p % 2], other_ref[p // 2, p % 2]
        self_ref[span, :] = jnp.where(first, mine, other)
        neigh_ref[span, :] = jnp.where(first, other, mine)


def body(features, tiles, tile_row, tile_col, degree, train_mask, w_self, w_neigh, cotangent):
    n = lax.axis_size("row")
    me = lax.axis_index("row").astype(jnp.int32).reshape(1)
    squares = n // 8
    nodes, feat_in = features.shape
    hidden = w_self.shape[1]
    block_local = nodes // BLOCK
    tile_count = tiles.shape[0]
    group = max(g for g in range(1, 7) if tile_count % g == 0)
    small = n * nodes * feat_in * 4 <= 4 * MIB
    limit = (24 if small else 56) * MIB

    def result(shape, dtype, stays=True):
        kind = pltpu.VMEM if small and stays else jax.ShapeDtypeStruct
        return kind(shape, dtype)

    def placed(x, spec):
        if spec is SMEM or not small:
            return x
        return pltpu.with_memory_space_constraint(x, pltpu.HBM if spec is ANY else pltpu.VMEM)

    def call(kernel, name, out_shape, operands, in_specs=None, out_specs=None, cost_us=0.2, **more):
        specs = in_specs or [VMEM] * len(operands)
        return pl.pallas_call(
            kernel,
            out_shape=out_shape,
            in_specs=specs,
            out_specs=out_specs or jax.tree.map(lambda _: VMEM, out_shape),
            compiler_params=pltpu.CompilerParams(vmem_limit_bytes=limit),
            cost_estimate=pl.CostEstimate(
                flops=int(cost_us * 1.1e9), bytes_accessed=int(cost_us * 3.6e6), transcendentals=0),
            name=name,
            **more,
        )(*[placed(x, spec) for x, spec in zip(operands, specs)])

    wide, piece = result((nodes, feat_in), F32), result((nodes, feat_in), BF16)
    weight = result((feat_in, hidden), F32)
    chunk = result((feat_in // 4, hidden), F32)
    by_block = (block_local, BLOCK, feat_in)

    own_arguments = (
        degree.reshape(block_local, BLOCK), train_mask.reshape(block_local, BLOCK),
        w_self, w_neigh, features, cotangent,
    )
    if small:
        own_arguments = [pltpu.with_memory_space_constraint(x, pltpu.HBM) for x in own_arguments]
    tiles_near, ws, wn, inverse, upstream, pre_self, feat_t, own, index = pl.pallas_call(
        functools.partial(stage_kernel, (8 * block_local, (n - 8) * block_local)),
        out_shape=(
            result(tiles.shape, BF16),
            result(w_self.shape, BF16),
            result(w_neigh.shape, BF16),
            result(by_block, F32),
            result((nodes, hidden), F32),
            result((nodes, hidden), F32),
            result(by_block, BF16),
            piece,
            pltpu.SMEM((6 * tile_count + 3,), jnp.int32),
        ),
        in_specs=[SMEM] * 3 + [VMEM] * 6 + [ANY],
        out_specs=(VMEM,) * 8 + (SMEM,),
        scratch_shapes=[pltpu.SemaphoreType.DMA],
        compiler_params=pltpu.CompilerParams(vmem_limit_bytes=limit),
        cost_estimate=pl.CostEstimate(flops=int(3 * 1.1e9), bytes_accessed=int(3 * 3.6e6), transcendentals=0),
        name="stage_arguments",
    )(me, tile_row, tile_col, *own_arguments, placed(tiles, ANY))

    same, other = gather_by_xor(features, own, n, call, result((4, nodes, feat_in), BF16))
    near_square = (8 * block_local, BLOCK, feat_in)
    far_squares = ((n - 8) * block_local, BLOCK, feat_in)
    raw_shape = (block_local + 1, BLOCK, feat_in)
    raw = call(
        functools.partial(forward_near_kernel, group), "forward_near", result(raw_shape, F32),
        (index, tiles_near, same[0], other[0]), [SMEM] + [VMEM] * 3, cost_us=0.1,
        scratch_shapes=[pltpu.VMEM(near_square, BF16)],
    )
    operands = (
        index, tiles_near, ws, wn, inverse, upstream, pre_self, feat_t, raw, *same[1:], *other[1:])
    embedded, base, wkeep, wsend, gt = call(
        functools.partial(forward_kernel, group, squares - 1),
        "forward_layer",
        (
            result((nodes, hidden), BF16, False), wide, weight, weight,
            result((block_local, 2 * feat_in, BLOCK), BF16),
        ),
        operands,
        [SMEM] + [VMEM] * (len(operands) - 1),
        cost_us=4,
        scratch_shapes=[
            pltpu.VMEM(far_squares, BF16),
            pltpu.VMEM(raw_shape, F32),
            pltpu.VMEM((2, feat_in, hidden), F32),
        ],
    )

    w0, w1, w2, w3 = call(
        cut_kernel, "cut_weights", (chunk,) * 4, (index, wkeep, swap(wsend, n, 1)),
        [SMEM, VMEM, VMEM])

    send_shape = result((4, nodes, feat_in), F32)
    sums, got = [], [None] * squares
    for section, shape in ((1, far_squares), (0, near_square)):
        acc = call(
            functools.partial(backward_kernel, section, group), "backward_tiles",
            result((shape[0] + 1,) + shape[1:], F32), (index, tiles_near, gt), [SMEM, VMEM, VMEM],
            cost_us=1.5)
        sums.insert(0, acc)
        for s in range(squares - 1, 0, -1) if section else (0,):
            operands = (acc,) if section else (acc, w0)
            got[s] = swap(
                call(functools.partial(send_kernel, s - section), "send", send_shape, operands), n, 1)
    extra = result((nodes + 2 * chunk.shape[0] * (hidden // feat_in), feat_in), BF16)
    terms = [None] * squares
    for s in range(squares - 1, -1, -1):
        operands = (sums[min(s, 1)], got[s])
        if s == squares - 1:
            own, *pieces = call(
                functools.partial(pair_weights_kernel, max(s - 1, 0)), "pair_sum_weights", (wide, extra, extra, extra),
                operands + (w1, w2, w3))
        else:
            own, *pieces = call(
                functools.partial(pair_kernel, max(s - 1, 0)), "pair_sum", (wide, piece, piece, piece), operands)
        terms[s] = [own, *[swap(x, n, 2 * q + 2) for q, x in enumerate(pieces)]]
    near_total = call(near_kernel, "near_sum", wide, (base, *terms[0]), cost_us=NEAR_COST)
    terms[0] = [near_total]
    distance = 1
    while distance < squares:
        for s in range(squares - distance, 0, -2 * distance):
            if s == squares - 1:
                total, wsum = call(
                    add_weights_kernel, "square_sum_weights", (piece, chunk), (w0, *terms[s]),
                    cost_us=SQUARE_COST)
            else:
                total = call(add_kernel, "square_sum", piece, terms[s], cost_us=SQUARE_COST)
            terms[s - distance].append(swap(total, n, 8 * distance))
        distance *= 2
    bit = 8
    while bit < n:
        wsum = call(add_two_kernel, "weight_sum", chunk, (wsum, swap(wsum, n, bit)))
        bit *= 2
    rows = chunk.shape[0]
    two = call(functools.partial(pack_kernel, (0, 1)), "pack_weights", result((2, rows, hidden), F32), (wsum, swap(wsum, n, 2)))
    mine = call(
        functools.partial(pack_kernel, (0, 1)), "pack_weights", result((2, 2, rows, hidden), F32), (two, swap(two, n, 4), near_total))
    grad_input = call(
        main_kernel, "grad_input_sum", result((nodes, feat_in), BF16, False), terms[0],
        cost_us=MAIN_COST)
    full = result((feat_in, hidden), F32, False)
    grad_self, grad_neigh = call(
        last_kernel, "write_weights", (full, full), (index, mine, swap(mine, n, 1)),
        [SMEM] + [VMEM] * 2)
    return (embedded, grad_input, grad_self, grad_neigh)


def solution(mesh):
    placed = (
        P(("parts", "row"), None),
        P(("parts", "row"), None, None),
        P(("parts", "row")),
        P(("parts", "row")),
        P(("parts", "row")),
        P(("parts", "row")),
        P(),
        P(),
        P(("parts", "row"), None),
    )
    return jax.shard_map(
        body,
        mesh=mesh,
        in_specs=placed,
        out_specs=(
            P(("parts", "row"), None),
            P(("parts", "row"), None),
            P("parts", None),
            P("parts", None),
        ),
        check_vma=False,
    )
```

```python
import functools

import jax
import jax.numpy as jnp
from jax import lax
from jax.experimental import pallas as pl
from jax.experimental.pallas import tpu as pltpu
from jax.sharding import PartitionSpec as P

BLOCK = 128
F32, BF16 = jnp.float32, jnp.bfloat16
VMEM = pl.BlockSpec(memory_space=pltpu.VMEM)
SMEM = pl.BlockSpec(memory_space=pltpu.SMEM)
ANY = pl.BlockSpec(memory_space=pl.ANY)
MIB = 1024 * 1024
LAST = ((1,), (1,))
NEAR_COST, SQUARE_COST, MAIN_COST = 8, 4, 10


def swap(x, n, offset):
    return lax.ppermute(x, "row", [(i, i ^ offset) for i in range(n)])


def gather_by_xor(x, own, n, call, pack):
    blocks = [x]
    bit = n // 2
    while bit >= 8:
        blocks = blocks + [swap(v, n, bit) for v in blocks]
        bit //= 2
    offsets = [0]
    bit = n // 2
    while bit >= 8:
        offsets = offsets + [o ^ bit for o in offsets]
        bit //= 2
    blocks = [v for _, v in sorted(zip(offsets, blocks), key=lambda pair: pair[0])]
    same = []
    for v in blocks:
        order = (2, 6, 4) if v is x else (6, 2, 4)
        square = (own if v is x else v, *[swap(v, n, offset) for offset in order])
        slots = (0, *[offset // 2 for offset in order])
        same.append(call(functools.partial(pack_kernel, slots), "pack_square", pack, square))
    return same, [swap(v, n, 1) for v in same]


def split_bf16(x):
    high = x.astype(BF16)
    return high, (x - high.astype(F32)).astype(BF16)


def dot(a, b, dims=((1,), (0,))):
    return lax.dot_general(a, b, (dims, ((), ())), preferred_element_type=F32)


def dot_wide(a, b, dims=((1,), (0,))):
    high, low = split_bf16(a)
    return dot(high, b, dims) + dot(low, b, dims)


def rows_to_lanes(row):
    return jnp.transpose(jnp.broadcast_to(row, (BLOCK, BLOCK)))


def rows_of(b):
    return pl.ds(b * BLOCK, BLOCK)


def pack_kernel(slots, *refs):
    for slot, ref in zip(slots, refs[:-1]):
        refs[-1][slot] = ref[...]


def stage_kernel(dumps, me_ref, trow_ref, tcol_ref, deg_ref, mask_ref, ws_ref, wn_ref, feat_ref, cot_ref,
                 tiles_ref, tiles_out, ws_out, wn_out, inverse_out, up_out, pre_out, featt_out,
                 own_out, index_out, sem):
    copy = pltpu.make_async_copy(tiles_ref, tiles_out, sem)
    copy.start()
    block_local = feat_ref.shape[0] // BLOCK
    tile_count = trow_ref.shape[0]
    me = me_ref[0]
    index_out[index_out.shape[0] - 1] = me

    def clear(i, carry):
        for section in range(2):
            index_out[3 * section * tile_count + i] = 0
            index_out[(3 * section + 1) * tile_count + i] = block_local
            index_out[(3 * section + 2) * tile_count + i] = dumps[section]
        return carry

    def place(t, counts):
        col = tcol_ref[t]
        live = col >= 0
        col = jnp.maximum(col, 0)
        chip_core = (col // block_local) ^ me
        far = chip_core >= 8
        position = jnp.where(far, chip_core - 8, chip_core) * block_local + col % block_local
        row = jnp.clip(trow_ref[t] - me * block_local, 0, block_local - 1)
        near_count, far_count = counts
        spot = jnp.where(far, 3 * tile_count + far_count, near_count)

        @pl.when(live)
        def _():
            index_out[spot] = t
            index_out[spot + tile_count] = row
            index_out[spot + 2 * tile_count] = position

        add = live.astype(jnp.int32)
        add_far = far.astype(jnp.int32) * add
        return near_count + add - add_far, far_count + add_far

    lax.fori_loop(0, tile_count, clear, 0)
    near_count, far_count = lax.fori_loop(0, tile_count, place, (jnp.int32(0), jnp.int32(0)))
    index_out[6 * tile_count] = near_count
    index_out[6 * tile_count + 1] = far_count
    own_out[...] = feat_ref[...]
    ws_out[...] = ws_ref[...]
    wn_out[...] = wn_ref[...]
    ws = ws_ref[...]
    for b in range(block_local):
        degree = rows_to_lanes(deg_ref[pl.ds(b, 1), :].astype(F32))
        mask = rows_to_lanes(mask_ref[pl.ds(b, 1), :].astype(F32))
        inverse_out[b] = 1.0 / degree
        feat = feat_ref[rows_of(b), :]
        featt_out[b] = jnp.transpose(feat.astype(F32)).astype(BF16)
        pre_out[rows_of(b), :] = dot(feat, ws)
        up_out[rows_of(b), :] = cot_ref[rows_of(b), :].astype(F32) * jnp.concatenate(
            [mask, mask], axis=1)
    copy.wait()


def over_tiles(section, group, index_ref, product, add):
    tile_count = (index_ref.shape[0] - 3) // 6
    start = 3 * section * tile_count

    def step(i, carry):
        spots = [start + i * group + u for u in range(group)]
        entries = [
            (index_ref[spot], index_ref[spot + tile_count], index_ref[spot + 2 * tile_count])
            for spot in spots
        ]
        products = [product(*entry) for entry in entries]
        for entry, value in zip(entries, products):
            add(*entry, value)
        return carry

    count = index_ref[6 * tile_count + section]
    lax.fori_loop(0, (count + group - 1) // group, step, 0)


def gathered_products(section, group, index_ref, tiles_ref, feat_refs, feats, raw):
    squares = len(feat_refs) // 2
    block_local = raw.shape[0] - 1
    for s in range(squares):
        for q in range(4):
            for core in range(2):
                for b in range(block_local):
                    spot = (8 * s + 2 * q + core) * block_local + b
                    feats[spot] = feat_refs[core * squares + s][q, rows_of(b), :]

    def add(t, row, position, value):
        raw[row] += value

    over_tiles(
        section, group, index_ref,
        lambda t, row, position: dot(tiles_ref[t], feats[jnp.minimum(position, feats.shape[0] - 1)]),
        add)


def forward_near_kernel(group, index_ref, tiles_ref, same_ref, other_ref, raw, feats):
    raw[...] = jnp.zeros_like(raw)
    gathered_products(0, group, index_ref, tiles_ref, (same_ref, other_ref), feats, raw)


def forward_kernel(group, far, index_ref, tiles_ref, ws_ref, wn_ref, inverse_ref, up_ref, pre_ref,
                   featt_ref, near_ref, *refs):
    feat_refs, refs = refs[:2 * far], refs[2 * far:]
    emb_ref, base_ref, wkeep_ref, wsend_ref, gt_ref, feats, raw, wsum = refs
    block_local = inverse_ref.shape[0]
    raw[...] = near_ref[...]
    gathered_products(1, group, index_ref, tiles_ref, feat_refs, feats, raw)

    wn = wn_ref[...]
    ws = ws_ref[...]
    for b in range(block_local):
        inverse = inverse_ref[b]
        raw_b = raw[b]
        pre = pre_ref[rows_of(b), :] + dot_wide(raw_b * inverse, wn)
        sig = jax.nn.sigmoid(pre)
        emb_ref[rows_of(b), :] = (pre * sig).astype(BF16)
        grad_pre = up_ref[rows_of(b), :] * sig * (1.0 + pre * (1.0 - sig))
        scaled = (grad_pre * jnp.concatenate([inverse, inverse], axis=1)).astype(BF16)
        gp_high, gp_low = split_bf16(grad_pre)
        feat_t = featt_ref[b]
        grad_self = dot(feat_t, gp_high) + dot(feat_t, gp_low)
        grad_neigh = dot_wide(jnp.transpose(raw_b), scaled)
        if b == 0:
            wsum[0], wsum[1] = grad_self, grad_neigh
        else:
            wsum[0] += grad_self
            wsum[1] += grad_neigh
        base_ref[rows_of(b), :] = dot(gp_high, ws, LAST) + dot(gp_low, ws, LAST)
        high, low = split_bf16(dot(wn, scaled, LAST))
        gt_ref[b, :BLOCK, :] = high
        gt_ref[b, BLOCK:, :] = low

    core = index_ref[index_ref.shape[0] - 1] % 2
    wkeep_ref[...] = wsum[core]
    wsend_ref[...] = wsum[1 - core]


def backward_kernel(section, group, index_ref, tiles_ref, gt_ref, acc_ref):
    block_local = gt_ref.shape[0]
    acc_ref[...] = jnp.zeros_like(acc_ref)

    def product(t, row, position):
        both = dot(gt_ref[jnp.minimum(row, block_local - 1)], tiles_ref[t])
        return both[:BLOCK] + both[BLOCK:]

    def add(t, row, position, value):
        acc_ref[position] += value

    over_tiles(section, group, index_ref, product, add)


def send_kernel(square, acc_ref, *refs):
    send_ref = refs[-1]
    block_local = send_ref.shape[1] // BLOCK
    for q in range(4):
        for b in range(block_local):
            send_ref[q, rows_of(b), :] = acc_ref[(8 * square + 2 * q + 1) * block_local + b]


def cut_kernel(index_ref, wkeep_ref, wgot_ref, *parts):
    rows = parts[0].shape[0]
    chip = index_ref[index_ref.shape[0] - 1] // 2 % 4
    for p, ref in enumerate(parts):
        span = pl.ds(pl.multiple_of((chip ^ p) * rows, rows), rows)
        ref[...] = wkeep_ref[span, :] + wgot_ref[span, :]


def pair_kernel(square, acc_ref, got_ref, own_ref, *pieces):
    block_local = own_ref.shape[0] // BLOCK
    for q, ref in enumerate((own_ref, *pieces)):
        for b in range(block_local):
            kept = acc_ref[(8 * square + 2 * q) * block_local + b]
            ref[rows_of(b), :] = (kept + got_ref[q, rows_of(b), :]).astype(ref.dtype)


def pair_weights_kernel(square, acc_ref, got_ref, w1, w2, w3, own_ref, *pieces):
    pair_kernel(square, acc_ref, got_ref, own_ref, *pieces)
    nodes, lanes = own_ref.shape
    for weight_ref, ref in zip((w1, w2, w3), pieces):
        rows, columns = weight_ref.shape
        start = nodes
        for part in split_bf16(weight_ref[...]):
            for column in range(0, columns, lanes):
                ref[pl.ds(start, rows), :] = part[:, column:column + lanes]
                start += rows


def add_two_kernel(own_ref, got_ref, out_ref):
    out_ref[...] = own_ref[...] + got_ref[...]


def add_kernel(own_ref, *refs):
    total = own_ref[...]
    for got_ref in refs[:-1]:
        total = total + got_ref[...].astype(F32)
    refs[-1][...] = total.astype(BF16)


def add_weights_kernel(weight_ref, own_ref, *refs):
    got_refs, (out_ref, weight_out) = refs[:-2], refs[-2:]
    nodes, lanes = own_ref.shape
    add_kernel(own_ref, *[ref.at[pl.ds(0, nodes), :] for ref in got_refs], out_ref)
    rows, columns = weight_ref.shape
    cuts = columns // lanes
    for cut in range(cuts):
        span = pl.ds(cut * lanes, lanes)
        total = weight_ref[:, span]
        for ref in got_refs[:3]:
            high = ref[pl.ds(nodes + cut * rows, rows), :]
            low = ref[pl.ds(nodes + (cuts + cut) * rows, rows), :]
            total = total + (high.astype(F32) + low.astype(F32))
        weight_out[:, span] = total


def near_kernel(base_ref, own_ref, *refs):
    for b in range(own_ref.shape[0] // BLOCK):
        total = own_ref[rows_of(b), :]
        for got_ref in refs[:-1]:
            total = total + got_ref[rows_of(b), :].astype(F32)
        refs[-1][rows_of(b), :] = base_ref[rows_of(b), :] + jnp.transpose(total)


def main_kernel(near_ref, *refs):
    for b in range(near_ref.shape[0] // BLOCK):
        total = refs[0][rows_of(b), :].astype(F32)
        for got_ref in refs[1:-1]:
            total = total + got_ref[rows_of(b), :].astype(F32)
        refs[-1][rows_of(b), :] = (near_ref[rows_of(b), :] + jnp.transpose(total)).astype(BF16)


def last_kernel(index_ref, weight_ref, other_ref, self_ref, neigh_ref):
    me = index_ref[index_ref.shape[0] - 1]
    first = me % 2 == 0
    chip = me // 2 % 4
    rows = weight_ref.shape[2]
    for p in range(4):
        span = pl.ds(pl.multiple_of((chip ^ p) * rows, rows), rows)
        mine, other = weight_ref[p // 2, p % 2], other_ref[p // 2, p % 2]
        self_ref[span, :] = jnp.where(first, mine, other)
        neigh_ref[span, :] = jnp.where(first, other, mine)


def body(features, tiles, tile_row, tile_col, degree, train_mask, w_self, w_neigh, cotangent):
    n = lax.axis_size("row")
    me = lax.axis_index("row").astype(jnp.int32).reshape(1)
    squares = n // 8
    nodes, feat_in = features.shape
    hidden = w_self.shape[1]
    block_local = nodes // BLOCK
    tile_count = tiles.shape[0]
    group = max(g for g in range(1, 7) if tile_count % g == 0)
    small = n * nodes * feat_in * 4 <= 4 * MIB
    limit = (24 if small else 56) * MIB

    def result(shape, dtype, stays=True):
        kind = pltpu.VMEM if small and stays else jax.ShapeDtypeStruct
        return kind(shape, dtype)

    def placed(x, spec):
        if spec is SMEM or not small:
            return x
        return pltpu.with_memory_space_constraint(x, pltpu.HBM if spec is ANY else pltpu.VMEM)

    def call(kernel, name, out_shape, operands, in_specs=None, out_specs=None, cost_us=0.2, **more):
        specs = in_specs or [VMEM] * len(operands)
        return pl.pallas_call(
            kernel,
            out_shape=out_shape,
            in_specs=specs,
            out_specs=out_specs or jax.tree.map(lambda _: VMEM, out_shape),
            compiler_params=pltpu.CompilerParams(vmem_limit_bytes=limit),
            cost_estimate=pl.CostEstimate(
                flops=int(cost_us * 1.1e9), bytes_accessed=int(cost_us * 3.6e6), transcendentals=0),
            name=name,
            **more,
        )(*[placed(x, spec) for x, spec in zip(operands, specs)])

    wide, piece = result((nodes, feat_in), F32), result((nodes, feat_in), BF16)
    weight = result((feat_in, hidden), F32)
    chunk = result((feat_in // 4, hidden), F32)
    by_block = (block_local, BLOCK, feat_in)

    own_arguments = (
        degree.reshape(block_local, BLOCK), train_mask.reshape(block_local, BLOCK),
        w_self, w_neigh, features, cotangent,
    )
    if small:
        own_arguments = [pltpu.with_memory_space_constraint(x, pltpu.HBM) for x in own_arguments]
    tiles_near, ws, wn, inverse, upstream, pre_self, feat_t, own, index = pl.pallas_call(
        functools.partial(stage_kernel, (8 * block_local, (n - 8) * block_local)),
        out_shape=(
            result(tiles.shape, BF16),
            result(w_self.shape, BF16),
            result(w_neigh.shape, BF16),
            result(by_block, F32),
            result((nodes, hidden), F32),
            result((nodes, hidden), F32),
            result(by_block, BF16),
            piece,
            pltpu.SMEM((6 * tile_count + 3,), jnp.int32),
        ),
        in_specs=[SMEM] * 3 + [VMEM] * 6 + [ANY],
        out_specs=(VMEM,) * 8 + (SMEM,),
        scratch_shapes=[pltpu.SemaphoreType.DMA],
        compiler_params=pltpu.CompilerParams(vmem_limit_bytes=limit),
        cost_estimate=pl.CostEstimate(flops=int(3 * 1.1e9), bytes_accessed=int(3 * 3.6e6), transcendentals=0),
        name="stage_arguments",
    )(me, tile_row, tile_col, *own_arguments, placed(tiles, ANY))

    same, other = gather_by_xor(features, own, n, call, result((4, nodes, feat_in), BF16))
    near_square = (8 * block_local, BLOCK, feat_in)
    far_squares = ((n - 8) * block_local, BLOCK, feat_in)
    raw_shape = (block_local + 1, BLOCK, feat_in)
    raw = call(
        functools.partial(forward_near_kernel, group), "forward_near", result(raw_shape, F32),
        (index, tiles_near, same[0], other[0]), [SMEM] + [VMEM] * 3, cost_us=0.1,
        scratch_shapes=[pltpu.VMEM(near_square, BF16)],
    )
    operands = (
        index, tiles_near, ws, wn, inverse, upstream, pre_self, feat_t, raw, *same[1:], *other[1:])
    embedded, base, wkeep, wsend, gt = call(
        functools.partial(forward_kernel, group, squares - 1),
        "forward_layer",
        (
            result((nodes, hidden), BF16, False), wide, weight, weight,
            result((block_local, 2 * feat_in, BLOCK), BF16),
        ),
        operands,
        [SMEM] + [VMEM] * (len(operands) - 1),
        cost_us=4,
        scratch_shapes=[
            pltpu.VMEM(far_squares, BF16),
            pltpu.VMEM(raw_shape, F32),
            pltpu.VMEM((2, feat_in, hidden), F32),
        ],
    )

    w0, w1, w2, w3 = call(
        cut_kernel, "cut_weights", (chunk,) * 4, (index, wkeep, swap(wsend, n, 1)),
        [SMEM, VMEM, VMEM])

    send_shape = result((4, nodes, feat_in), F32)
    sums, got = [], [None] * squares
    for section, shape in ((1, far_squares), (0, near_square)):
        acc = call(
            functools.partial(backward_kernel, section, group), "backward_tiles",
            result((shape[0] + 1,) + shape[1:], F32), (index, tiles_near, gt), [SMEM, VMEM, VMEM],
            cost_us=1.5)
        sums.insert(0, acc)
        for s in range(squares - 1, 0, -1) if section else (0,):
            operands = (acc,) if section else (acc, w0)
            got[s] = swap(
                call(functools.partial(send_kernel, s - section), "send", send_shape, operands), n, 1)
    extra = result((nodes + 2 * chunk.shape[0] * (hidden // feat_in), feat_in), BF16)
    terms = [None] * squares
    for s in range(squares - 1, -1, -1):
        operands = (sums[min(s, 1)], got[s])
        if s == squares - 1:
            own, *pieces = call(
                functools.partial(pair_weights_kernel, max(s - 1, 0)), "pair_sum_weights", (wide, extra, extra, extra),
                operands + (w1, w2, w3))
        else:
            own, *pieces = call(
                functools.partial(pair_kernel, max(s - 1, 0)), "pair_sum", (wide, piece, piece, piece), operands)
        terms[s] = [own, *[swap(pieces[q - 1], n, 2 * q) for q in (3, 1, 2)]]
    near_total = call(near_kernel, "near_sum", wide, (base, *terms[0]), cost_us=NEAR_COST)
    terms[0] = [near_total]
    distance = 1
    while distance < squares:
        for s in range(squares - distance, 0, -2 * distance):
            if s == squares - 1:
                total, wsum = call(
                    add_weights_kernel, "square_sum_weights", (piece, chunk), (w0, *terms[s]),
                    cost_us=SQUARE_COST)
            else:
                total = call(add_kernel, "square_sum", piece, terms[s], cost_us=SQUARE_COST)
            terms[s - distance].append(swap(total, n, 8 * distance))
        distance *= 2
    bit = 8
    while bit < n:
        wsum = call(add_two_kernel, "weight_sum", chunk, (wsum, swap(wsum, n, bit)))
        bit *= 2
    rows = chunk.shape[0]
    two = call(functools.partial(pack_kernel, (0, 1)), "pack_weights", result((2, rows, hidden), F32), (wsum, swap(wsum, n, 2)))
    mine = call(
        functools.partial(pack_kernel, (0, 1)), "pack_weights", result((2, 2, rows, hidden), F32), (two, swap(two, n, 4), near_total))
    grad_input = call(
        main_kernel, "grad_input_sum", result((nodes, feat_in), BF16, False), terms[0],
        cost_us=MAIN_COST)
    full = result((feat_in, hidden), F32, False)
    grad_self, grad_neigh = call(
        last_kernel, "write_weights", (full, full), (index, mine, swap(mine, n, 1)),
        [SMEM] + [VMEM] * 2)
    return (embedded, grad_input, grad_self, grad_neigh)


def solution(mesh):
    placed = (
        P(("parts", "row"), None),
        P(("parts", "row"), None, None),
        P(("parts", "row")),
        P(("parts", "row")),
        P(("parts", "row")),
        P(("parts", "row")),
        P(),
        P(),
        P(("parts", "row"), None),
    )
    return jax.shard_map(
        body,
        mesh=mesh,
        in_specs=placed,
        out_specs=(
            P(("parts", "row"), None),
            P(("parts", "row"), None),
            P("parts", None),
            P("parts", None),
        ),
        check_vma=False,
    )
```

```python
import functools

import jax
import jax.numpy as jnp
from jax import lax
from jax.experimental import pallas as pl
from jax.experimental.pallas import tpu as pltpu
from jax.sharding import PartitionSpec as P

BLOCK = 128
F32, BF16 = jnp.float32, jnp.bfloat16
VMEM = pl.BlockSpec(memory_space=pltpu.VMEM)
SMEM = pl.BlockSpec(memory_space=pltpu.SMEM)
ANY = pl.BlockSpec(memory_space=pl.ANY)
MIB = 1024 * 1024
LAST = ((1,), (1,))
NEAR_COST, SQUARE_COST, MAIN_COST = 8, 4, 10


def swap(x, n, offset):
    return lax.ppermute(x, "row", [(i, i ^ offset) for i in range(n)])


def gather_by_xor(x, own, n, call, pack):
    blocks = [x]
    bit = n // 2
    while bit >= 8:
        blocks = blocks + [swap(v, n, bit) for v in blocks]
        bit //= 2
    offsets = [0]
    bit = n // 2
    while bit >= 8:
        offsets = offsets + [o ^ bit for o in offsets]
        bit //= 2
    blocks = [v for _, v in sorted(zip(offsets, blocks), key=lambda pair: pair[0])]
    same = []
    for v in blocks:
        order = (2, 6, 4) if v is x else (6, 2, 4)
        square = (own if v is x else v, *[swap(v, n, offset) for offset in order])
        slots = (0, *[offset // 2 for offset in order])
        same.append(call(functools.partial(pack_kernel, slots), "pack_square", pack, square))
    return same, [swap(v, n, 1) for v in same]


def split_bf16(x):
    high = x.astype(BF16)
    return high, (x - high.astype(F32)).astype(BF16)


def dot(a, b, dims=((1,), (0,))):
    return lax.dot_general(a, b, (dims, ((), ())), preferred_element_type=F32)


def dot_wide(a, b, dims=((1,), (0,))):
    high, low = split_bf16(a)
    return dot(high, b, dims) + dot(low, b, dims)


def rows_to_lanes(row):
    return jnp.transpose(jnp.broadcast_to(row, (BLOCK, BLOCK)))


def rows_of(b):
    return pl.ds(b * BLOCK, BLOCK)


def pack_kernel(slots, *refs):
    for slot, ref in zip(slots, refs[:-1]):
        refs[-1][slot] = ref[...]


def stage_kernel(dumps, me_ref, trow_ref, tcol_ref, deg_ref, mask_ref, ws_ref, wn_ref, feat_ref, cot_ref,
                 tiles_ref, tiles_out, ws_out, wn_out, inverse_out, up_out, pre_out, featt_out,
                 own_out, index_out, sem):
    copy = pltpu.make_async_copy(tiles_ref, tiles_out, sem)
    copy.start()
    block_local = feat_ref.shape[0] // BLOCK
    tile_count = trow_ref.shape[0]
    me = me_ref[0]
    index_out[index_out.shape[0] - 1] = me

    def clear(i, carry):
        for section in range(2):
            index_out[3 * section * tile_count + i] = 0
            index_out[(3 * section + 1) * tile_count + i] = block_local
            index_out[(3 * section + 2) * tile_count + i] = dumps[section]
        return carry

    def place(t, counts):
        col = tcol_ref[t]
        live = col >= 0
        col = jnp.maximum(col, 0)
        chip_core = (col // block_local) ^ me
        far = chip_core >= 8
        position = jnp.where(far, chip_core - 8, chip_core) * block_local + col % block_local
        row = jnp.clip(trow_ref[t] - me * block_local, 0, block_local - 1)
        near_count, far_count = counts
        spot = jnp.where(far, 3 * tile_count + far_count, near_count)

        @pl.when(live)
        def _():
            index_out[spot] = t
            index_out[spot + tile_count] = row
            index_out[spot + 2 * tile_count] = position

        add = live.astype(jnp.int32)
        add_far = far.astype(jnp.int32) * add
        return near_count + add - add_far, far_count + add_far

    lax.fori_loop(0, tile_count, clear, 0)
    near_count, far_count = lax.fori_loop(0, tile_count, place, (jnp.int32(0), jnp.int32(0)))
    index_out[6 * tile_count] = near_count
    index_out[6 * tile_count + 1] = far_count
    own_out[...] = feat_ref[...]
    ws_out[...] = ws_ref[...]
    wn_out[...] = wn_ref[...]
    ws = ws_ref[...]
    for b in range(block_local):
        degree = rows_to_lanes(deg_ref[pl.ds(b, 1), :].astype(F32))
        mask = rows_to_lanes(mask_ref[pl.ds(b, 1), :].astype(F32))
        inverse_out[b] = 1.0 / degree
        feat = feat_ref[rows_of(b), :]
        featt_out[b] = jnp.transpose(feat.astype(F32)).astype(BF16)
        pre_out[rows_of(b), :] = dot(feat, ws)
        up_out[rows_of(b), :] = cot_ref[rows_of(b), :].astype(F32) * jnp.concatenate(
            [mask, mask], axis=1)
    copy.wait()


def over_tiles(section, group, index_ref, product, add):
    tile_count = (index_ref.shape[0] - 3) // 6
    start = 3 * section * tile_count

    def step(i, carry):
        spots = [start + i * group + u for u in range(group)]
        entries = [
            (index_ref[spot], index_ref[spot + tile_count], index_ref[spot + 2 * tile_count])
            for spot in spots
        ]
        products = [product(*entry) for entry in entries]
        for entry, value in zip(entries, products):
            add(*entry, value)
        return carry

    count = index_ref[6 * tile_count + section]
    lax.fori_loop(0, (count + group - 1) // group, step, 0)


def gathered_products(section, group, index_ref, tiles_ref, feat_refs, feats, raw):
    squares = len(feat_refs) // 2
    block_local = raw.shape[0] - 1
    for s in range(squares):
        for q in range(4):
            for core in range(2):
                for b in range(block_local):
                    spot = (8 * s + 2 * q + core) * block_local + b
                    feats[spot] = feat_refs[core * squares + s][q, rows_of(b), :]

    def add(t, row, position, value):
        raw[row] += value

    over_tiles(
        section, group, index_ref,
        lambda t, row, position: dot(tiles_ref[t], feats[jnp.minimum(position, feats.shape[0] - 1)]),
        add)


def forward_near_kernel(group, index_ref, tiles_ref, same_ref, other_ref, raw, feats):
    raw[...] = jnp.zeros_like(raw)
    gathered_products(0, group, index_ref, tiles_ref, (same_ref, other_ref), feats, raw)


def forward_kernel(group, far, index_ref, tiles_ref, wn_ref, inverse_ref, up_ref, pre_ref,
                   near_ref, *refs):
    feat_refs, refs = refs[:2 * far], refs[2 * far:]
    emb_ref, high_ref, low_ref, scaled_ref, gt_ref, raw, feats = refs
    block_local = inverse_ref.shape[0]
    raw[...] = near_ref[...]
    gathered_products(1, group, index_ref, tiles_ref, feat_refs, feats, raw)
    wn = wn_ref[...]
    for b in range(block_local):
        inverse = inverse_ref[b]
        pre = pre_ref[rows_of(b), :] + dot_wide(raw[b] * inverse, wn)
        sig = jax.nn.sigmoid(pre)
        emb_ref[rows_of(b), :] = (pre * sig).astype(BF16)
        grad_pre = up_ref[rows_of(b), :] * sig * (1.0 + pre * (1.0 - sig))
        scaled = (grad_pre * jnp.concatenate([inverse, inverse], axis=1)).astype(BF16)
        scaled_ref[rows_of(b), :] = scaled
        high_ref[rows_of(b), :], low_ref[rows_of(b), :] = split_bf16(grad_pre)
        high, low = split_bf16(dot(wn, scaled, LAST))
        gt_ref[b, :BLOCK, :] = high
        gt_ref[b, BLOCK:, :] = low


def weights_kernel(index_ref, high_ref, low_ref, scaled_ref, raw_ref, featt_ref, *refs):
    wkeep_ref, wsend_ref, wsum = refs[-3:]
    for b in range(featt_ref.shape[0]):
        feat_t = featt_ref[b]
        grad_self = dot(feat_t, high_ref[rows_of(b), :]) + dot(feat_t, low_ref[rows_of(b), :])
        grad_neigh = dot_wide(jnp.transpose(raw_ref[b]), scaled_ref[rows_of(b), :])
        if b == 0:
            wsum[0], wsum[1] = grad_self, grad_neigh
        else:
            wsum[0] += grad_self
            wsum[1] += grad_neigh
    core = index_ref[index_ref.shape[0] - 1] % 2
    wkeep_ref[...] = wsum[core]
    wsend_ref[...] = wsum[1 - core]


def backward_kernel(section, group, index_ref, tiles_ref, gt_ref, acc_ref):
    block_local = gt_ref.shape[0]
    acc_ref[...] = jnp.zeros_like(acc_ref)

    def product(t, row, position):
        both = dot(gt_ref[jnp.minimum(row, block_local - 1)], tiles_ref[t])
        return both[:BLOCK] + both[BLOCK:]

    def add(t, row, position, value):
        acc_ref[position] += value

    over_tiles(section, group, index_ref, product, add)


def send_kernel(square, acc_ref, *refs):
    send_ref = refs[-1]
    block_local = send_ref.shape[1] // BLOCK
    for q in range(4):
        for b in range(block_local):
            send_ref[q, rows_of(b), :] = acc_ref[(8 * square + 2 * q + 1) * block_local + b]


def cut_kernel(index_ref, wkeep_ref, wgot_ref, *parts):
    rows = parts[0].shape[0]
    chip = index_ref[index_ref.shape[0] - 1] // 2 % 4
    for p, ref in enumerate(parts):
        span = pl.ds(pl.multiple_of((chip ^ p) * rows, rows), rows)
        ref[...] = wkeep_ref[span, :] + wgot_ref[span, :]


def pair_kernel(square, acc_ref, got_ref, own_ref, *pieces):
    block_local = own_ref.shape[0] // BLOCK
    for q, ref in enumerate((own_ref, *pieces)):
        for b in range(block_local):
            kept = acc_ref[(8 * square + 2 * q) * block_local + b]
            ref[rows_of(b), :] = (kept + got_ref[q, rows_of(b), :]).astype(ref.dtype)


def pair_weights_kernel(square, acc_ref, got_ref, w1, w2, w3, own_ref, *pieces):
    pair_kernel(square, acc_ref, got_ref, own_ref, *pieces)
    nodes, lanes = own_ref.shape
    for weight_ref, ref in zip((w1, w2, w3), pieces):
        rows, columns = weight_ref.shape
        start = nodes
        for part in split_bf16(weight_ref[...]):
            for column in range(0, columns, lanes):
                ref[pl.ds(start, rows), :] = part[:, column:column + lanes]
                start += rows


def add_two_kernel(own_ref, got_ref, out_ref):
    out_ref[...] = own_ref[...] + got_ref[...]


def add_kernel(own_ref, *refs):
    total = own_ref[...]
    for got_ref in refs[:-1]:
        total = total + got_ref[...].astype(F32)
    refs[-1][...] = total.astype(BF16)


def add_weights_kernel(weight_ref, own_ref, *refs):
    got_refs, (out_ref, weight_out) = refs[:-2], refs[-2:]
    nodes, lanes = own_ref.shape
    add_kernel(own_ref, *[ref.at[pl.ds(0, nodes), :] for ref in got_refs], out_ref)
    rows, columns = weight_ref.shape
    cuts = columns // lanes
    for cut in range(cuts):
        span = pl.ds(cut * lanes, lanes)
        total = weight_ref[:, span]
        for ref in got_refs[:3]:
            high = ref[pl.ds(nodes + cut * rows, rows), :]
            low = ref[pl.ds(nodes + (cuts + cut) * rows, rows), :]
            total = total + (high.astype(F32) + low.astype(F32))
        weight_out[:, span] = total


def near_kernel(high_ref, low_ref, ws_ref, own_ref, *refs):
    ws = ws_ref[...]
    for b in range(own_ref.shape[0] // BLOCK):
        total = own_ref[rows_of(b), :]
        for got_ref in refs[:-1]:
            total = total + got_ref[rows_of(b), :].astype(F32)
        base = dot(high_ref[rows_of(b), :], ws, LAST) + dot(low_ref[rows_of(b), :], ws, LAST)
        refs[-1][rows_of(b), :] = base + jnp.transpose(total)


def main_kernel(near_ref, *refs):
    for b in range(near_ref.shape[0] // BLOCK):
        total = refs[0][rows_of(b), :].astype(F32)
        for got_ref in refs[1:-1]:
            total = total + got_ref[rows_of(b), :].astype(F32)
        refs[-1][rows_of(b), :] = (near_ref[rows_of(b), :] + jnp.transpose(total)).astype(BF16)


def last_kernel(index_ref, weight_ref, other_ref, self_ref, neigh_ref):
    me = index_ref[index_ref.shape[0] - 1]
    first = me % 2 == 0
    chip = me // 2 % 4
    rows = weight_ref.shape[2]
    for p in range(4):
        span = pl.ds(pl.multiple_of((chip ^ p) * rows, rows), rows)
        mine, other = weight_ref[p % 2, p // 2], other_ref[p % 2, p // 2]
        self_ref[span, :] = jnp.where(first, mine, other)
        neigh_ref[span, :] = jnp.where(first, other, mine)


def body(features, tiles, tile_row, tile_col, degree, train_mask, w_self, w_neigh, cotangent):
    n = lax.axis_size("row")
    me = lax.axis_index("row").astype(jnp.int32).reshape(1)
    squares = n // 8
    nodes, feat_in = features.shape
    hidden = w_self.shape[1]
    block_local = nodes // BLOCK
    tile_count = tiles.shape[0]
    group = max(g for g in range(1, 11) if tile_count % g == 0)
    small = n * nodes * feat_in * 4 <= 4 * MIB
    limit = (24 if small else 56) * MIB

    def result(shape, dtype, stays=True):
        kind = pltpu.VMEM if small and stays else jax.ShapeDtypeStruct
        return kind(shape, dtype)

    def placed(x, spec):
        if spec is SMEM or not small:
            return x
        return pltpu.with_memory_space_constraint(x, pltpu.HBM if spec is ANY else pltpu.VMEM)

    def call(kernel, name, out_shape, operands, in_specs=None, out_specs=None, cost_us=0.2, **more):
        specs = in_specs or [VMEM] * len(operands)
        return pl.pallas_call(
            kernel,
            out_shape=out_shape,
            in_specs=specs,
            out_specs=out_specs or jax.tree.map(lambda _: VMEM, out_shape),
            compiler_params=pltpu.CompilerParams(vmem_limit_bytes=limit),
            cost_estimate=pl.CostEstimate(
                flops=int(cost_us * 1.1e9), bytes_accessed=int(cost_us * 3.6e6), transcendentals=0),
            name=name,
            **more,
        )(*[placed(x, spec) for x, spec in zip(operands, specs)])

    wide, piece = result((nodes, feat_in), F32), result((nodes, feat_in), BF16)
    weight = result((feat_in, hidden), F32)
    chunk = result((feat_in // 4, hidden), F32)
    by_block = (block_local, BLOCK, feat_in)

    own_arguments = (
        degree.reshape(block_local, BLOCK), train_mask.reshape(block_local, BLOCK),
        w_self, w_neigh, features, cotangent,
    )
    if small:
        own_arguments = [pltpu.with_memory_space_constraint(x, pltpu.HBM) for x in own_arguments]
    tiles_near, ws, wn, inverse, upstream, pre_self, feat_t, own, index = pl.pallas_call(
        functools.partial(stage_kernel, (8 * block_local, (n - 8) * block_local)),
        out_shape=(
            result(tiles.shape, BF16),
            result(w_self.shape, BF16),
            result(w_neigh.shape, BF16),
            result(by_block, F32),
            result((nodes, hidden), F32),
            result((nodes, hidden), F32),
            result(by_block, BF16),
            piece,
            pltpu.SMEM((6 * tile_count + 3,), jnp.int32),
        ),
        in_specs=[SMEM] * 3 + [VMEM] * 6 + [ANY],
        out_specs=(VMEM,) * 8 + (SMEM,),
        scratch_shapes=[pltpu.SemaphoreType.DMA],
        compiler_params=pltpu.CompilerParams(vmem_limit_bytes=limit),
        cost_estimate=pl.CostEstimate(flops=int(3 * 1.1e9), bytes_accessed=int(3 * 3.6e6), transcendentals=0),
        name="stage_arguments",
    )(me, tile_row, tile_col, *own_arguments, placed(tiles, ANY))

    same, other = gather_by_xor(features, own, n, call, result((4, nodes, feat_in), BF16))
    near_square = (8 * block_local, BLOCK, feat_in)
    far_squares = ((n - 8) * block_local, BLOCK, feat_in)
    raw_shape = (block_local + 1, BLOCK, feat_in)
    raw = call(
        functools.partial(forward_near_kernel, group), "forward_near", result(raw_shape, F32),
        (index, tiles_near, same[0], other[0]), [SMEM] + [VMEM] * 3, cost_us=0.1,
        scratch_shapes=[pltpu.VMEM(near_square, BF16)],
    )
    operands = (index, tiles_near, wn, inverse, upstream, pre_self, raw, *same[1:], *other[1:])
    wide_out = result((nodes, hidden), BF16)
    embedded, high, low, scaled, gt, raw = call(
        functools.partial(forward_kernel, group, squares - 1),
        "forward_layer",
        (
            result((nodes, hidden), BF16, False), wide_out, wide_out, wide_out,
            result((block_local, 2 * feat_in, BLOCK), BF16), result(raw_shape, F32),
        ),
        operands,
        [SMEM] + [VMEM] * (len(operands) - 1),
        cost_us=3,
        scratch_shapes=[pltpu.VMEM(far_squares, BF16)],
    )

    send_shape = result((4, nodes, feat_in), F32)
    sums, got = [], [None] * squares
    after = None
    for section, shape in ((1, far_squares), (0, near_square)):
        acc = call(
            functools.partial(backward_kernel, section, group), "backward_tiles",
            result((shape[0] + 1,) + shape[1:], F32), (index, tiles_near, gt), [SMEM, VMEM, VMEM],
            cost_us=1.5)
        sums.insert(0, acc)
        for s in range(squares - 1, 0, -1) if section else (0,):
            operands = (acc,) if section else (acc, w0)
            send = call(functools.partial(send_kernel, s - section), "send", send_shape, operands)
            got[s] = swap(send, n, 1)
            after = send if after is None else after
        if section:
            wkeep, wsend = call(
                weights_kernel, "weights", (weight, weight),
                (index, high, low, scaled, raw, feat_t, after), [SMEM] + [VMEM] * 6, cost_us=1,
                scratch_shapes=[pltpu.VMEM((2, feat_in, hidden), F32)])
            w0, w1, w2, w3 = call(
                cut_kernel, "cut_weights", (chunk,) * 4, (index, wkeep, swap(wsend, n, 1)),
                [SMEM, VMEM, VMEM])

    extra = result((nodes + 2 * chunk.shape[0] * (hidden // feat_in), feat_in), BF16)
    terms = [None] * squares
    for s in range(squares - 1, -1, -1):
        operands = (sums[min(s, 1)], got[s])
        if s == squares - 1:
            own, *pieces = call(
                functools.partial(pair_weights_kernel, max(s - 1, 0)), "pair_sum_weights", (wide, extra, extra, extra),
                operands + (w1, w2, w3))
        else:
            own, *pieces = call(
                functools.partial(pair_kernel, max(s - 1, 0)), "pair_sum", (wide, piece, piece, piece), operands)
        terms[s] = [own, *[swap(pieces[q - 1], n, 2 * q) for q in (3, 1, 2)]]
    near_total = call(near_kernel, "near_sum", wide, (high, low, ws, *terms[0]), cost_us=NEAR_COST)
    terms[0] = [near_total]
    distance = 1
    while distance < squares:
        for s in range(squares - distance, 0, -2 * distance):
            if s == squares - 1:
                total, wsum = call(
                    add_weights_kernel, "square_sum_weights", (piece, chunk), (w0, *terms[s]),
                    cost_us=SQUARE_COST)
            else:
                total = call(add_kernel, "square_sum", piece, terms[s], cost_us=SQUARE_COST)
            terms[s - distance].append(swap(total, n, 8 * distance))
        distance *= 2
    bit = 8
    while bit < n:
        wsum = call(add_two_kernel, "weight_sum", chunk, (wsum, swap(wsum, n, bit)))
        bit *= 2
    rows = chunk.shape[0]
    two = call(functools.partial(pack_kernel, (0, 1)), "pack_weights", result((2, rows, hidden), F32), (wsum, swap(wsum, n, 4)))
    mine = call(
        functools.partial(pack_kernel, (0, 1)), "pack_weights", result((2, 2, rows, hidden), F32), (two, swap(two, n, 2), near_total))
    grad_input = call(
        main_kernel, "grad_input_sum", result((nodes, feat_in), BF16, False), terms[0],
        cost_us=MAIN_COST)
    full = result((feat_in, hidden), F32, False)
    grad_self, grad_neigh = call(
        last_kernel, "write_weights", (full, full), (index, mine, swap(mine, n, 1)),
        [SMEM] + [VMEM] * 2)
    return (embedded, grad_input, grad_self, grad_neigh)


def solution(mesh):
    placed = (
        P(("parts", "row"), None),
        P(("parts", "row"), None, None),
        P(("parts", "row")),
        P(("parts", "row")),
        P(("parts", "row")),
        P(("parts", "row")),
        P(),
        P(),
        P(("parts", "row"), None),
    )
    return jax.shard_map(
        body,
        mesh=mesh,
        in_specs=placed,
        out_specs=(
            P(("parts", "row"), None),
            P(("parts", "row"), None),
            P("parts", None),
            P("parts", None),
        ),
        check_vma=False,
    )
```

```python
import functools

import jax
import jax.numpy as jnp
from jax import lax
from jax.experimental import pallas as pl
from jax.experimental.pallas import tpu as pltpu
from jax.sharding import PartitionSpec as P

BLOCK = 128
F32, BF16 = jnp.float32, jnp.bfloat16
VMEM = pl.BlockSpec(memory_space=pltpu.VMEM)
SMEM = pl.BlockSpec(memory_space=pltpu.SMEM)
ANY = pl.BlockSpec(memory_space=pl.ANY)
MIB = 1024 * 1024
LAST = ((1,), (1,))
NEAR_COST, SQUARE_COST, MAIN_COST = 0.2, 4, 10


def swap(x, n, offset):
    return lax.ppermute(x, "row", [(i, i ^ offset) for i in range(n)])


def gather_by_xor(x, own, n, call, pack):
    blocks = [x]
    bit = n // 2
    while bit >= 8:
        blocks = blocks + [swap(v, n, bit) for v in blocks]
        bit //= 2
    offsets = [0]
    bit = n // 2
    while bit >= 8:
        offsets = offsets + [o ^ bit for o in offsets]
        bit //= 2
    blocks = [v for _, v in sorted(zip(offsets, blocks), key=lambda pair: pair[0])]
    same = []
    for v in blocks:
        order = (2, 6, 4) if v is x else (6, 2, 4)
        square = (own if v is x else v, *[swap(v, n, offset) for offset in order])
        slots = (0, *[offset // 2 for offset in order])
        same.append(call(functools.partial(pack_kernel, slots), "pack_square", pack, square))
    return same, [swap(v, n, 1) for v in same]


def split_bf16(x):
    high = x.astype(BF16)
    return high, (x - high.astype(F32)).astype(BF16)


def dot(a, b, dims=((1,), (0,))):
    return lax.dot_general(a, b, (dims, ((), ())), preferred_element_type=F32)


def dot_wide(a, b, dims=((1,), (0,))):
    high, low = split_bf16(a)
    return dot(high, b, dims) + dot(low, b, dims)


def rows_to_lanes(row):
    return jnp.transpose(jnp.broadcast_to(row, (BLOCK, BLOCK)))


def rows_of(b):
    return pl.ds(b * BLOCK, BLOCK)


def pack_kernel(slots, *refs):
    for slot, ref in zip(slots, refs[:-1]):
        refs[-1][slot] = ref[...]


def stage_kernel(dumps, me_ref, trow_ref, tcol_ref, deg_ref, mask_ref, ws_ref, wn_ref, feat_ref, cot_ref,
                 tiles_ref, tiles_out, ws_out, wn_out, inverse_out, up_out, pre_out, featt_out,
                 own_out, index_out, sem):
    copy = pltpu.make_async_copy(tiles_ref, tiles_out, sem)
    copy.start()
    block_local = feat_ref.shape[0] // BLOCK
    tile_count = trow_ref.shape[0]
    me = me_ref[0]
    index_out[index_out.shape[0] - 1] = me

    def clear(i, carry):
        for section in range(2):
            index_out[3 * section * tile_count + i] = 0
            index_out[(3 * section + 1) * tile_count + i] = block_local
            index_out[(3 * section + 2) * tile_count + i] = dumps[section]
        return carry

    def place(t, counts):
        col = tcol_ref[t]
        live = col >= 0
        col = jnp.maximum(col, 0)
        chip_core = (col // block_local) ^ me
        far = chip_core >= 8
        position = jnp.where(far, chip_core - 8, chip_core) * block_local + col % block_local
        row = jnp.clip(trow_ref[t] - me * block_local, 0, block_local - 1)
        near_count, far_count = counts
        spot = jnp.where(far, 3 * tile_count + far_count, near_count)

        @pl.when(live)
        def _():
            index_out[spot] = t
            index_out[spot + tile_count] = row
            index_out[spot + 2 * tile_count] = position

        add = live.astype(jnp.int32)
        add_far = far.astype(jnp.int32) * add
        return near_count + add - add_far, far_count + add_far

    lax.fori_loop(0, tile_count, clear, 0)
    near_count, far_count = lax.fori_loop(0, tile_count, place, (jnp.int32(0), jnp.int32(0)))
    index_out[6 * tile_count] = near_count
    index_out[6 * tile_count + 1] = far_count
    own_out[...] = feat_ref[...]
    ws_out[...] = ws_ref[...]
    wn_out[...] = wn_ref[...]
    ws = ws_ref[...]
    for b in range(block_local):
        degree = rows_to_lanes(deg_ref[pl.ds(b, 1), :].astype(F32))
        mask = rows_to_lanes(mask_ref[pl.ds(b, 1), :].astype(F32))
        inverse_out[b] = 1.0 / degree
        feat = feat_ref[rows_of(b), :]
        featt_out[b] = jnp.transpose(feat.astype(F32)).astype(BF16)
        pre_out[rows_of(b), :] = dot(feat, ws)
        up_out[rows_of(b), :] = cot_ref[rows_of(b), :].astype(F32) * jnp.concatenate(
            [mask, mask], axis=1)
    copy.wait()


def over_tiles(section, group, index_ref, product, add):
    tile_count = (index_ref.shape[0] - 3) // 6
    start = 3 * section * tile_count

    def step(i, carry):
        spots = [start + i * group + u for u in range(group)]
        entries = [
            (index_ref[spot], index_ref[spot + tile_count], index_ref[spot + 2 * tile_count])
            for spot in spots
        ]
        products = [product(*entry) for entry in entries]
        for entry, value in zip(entries, products):
            add(*entry, value)
        return carry

    count = index_ref[6 * tile_count + section]
    lax.fori_loop(0, (count + group - 1) // group, step, 0)


def gathered_products(section, group, index_ref, tiles_ref, feat_refs, feats, raw):
    squares = len(feat_refs) // 2
    block_local = raw.shape[0] - 1
    for s in range(squares):
        for q in range(4):
            for core in range(2):
                for b in range(block_local):
                    spot = (8 * s + 2 * q + core) * block_local + b
                    feats[spot] = feat_refs[core * squares + s][q, rows_of(b), :]

    def add(t, row, position, value):
        raw[row] += value

    over_tiles(
        section, group, index_ref,
        lambda t, row, position: dot(tiles_ref[t], feats[jnp.minimum(position, feats.shape[0] - 1)]),
        add)


def forward_near_kernel(group, index_ref, tiles_ref, same_ref, other_ref, raw, feats):
    raw[...] = jnp.zeros_like(raw)
    gathered_products(0, group, index_ref, tiles_ref, (same_ref, other_ref), feats, raw)


def forward_kernel(group, far, index_ref, tiles_ref, wn_ref, inverse_ref, up_ref, pre_ref,
                   near_ref, *refs):
    feat_refs, refs = refs[:2 * far], refs[2 * far:]
    emb_ref, high_ref, low_ref, scaled_ref, gt_ref, raw, feats = refs
    block_local = inverse_ref.shape[0]
    raw[...] = near_ref[...]
    gathered_products(1, group, index_ref, tiles_ref, feat_refs, feats, raw)
    wn = wn_ref[...]
    for b in range(block_local):
        inverse = inverse_ref[b]
        pre = pre_ref[rows_of(b), :] + dot_wide(raw[b] * inverse, wn)
        sig = jax.nn.sigmoid(pre)
        emb_ref[rows_of(b), :] = (pre * sig).astype(BF16)
        grad_pre = up_ref[rows_of(b), :] * sig * (1.0 + pre * (1.0 - sig))
        scaled = (grad_pre * jnp.concatenate([inverse, inverse], axis=1)).astype(BF16)
        scaled_ref[rows_of(b), :] = scaled
        high_ref[rows_of(b), :], low_ref[rows_of(b), :] = split_bf16(grad_pre)
        high, low = split_bf16(dot(wn, scaled, LAST))
        gt_ref[b, :BLOCK, :] = high
        gt_ref[b, BLOCK:, :] = low


def weights_kernel(index_ref, high_ref, low_ref, scaled_ref, raw_ref, featt_ref, *refs):
    wkeep_ref, wsend_ref, wsum = refs[-3:]
    for b in range(featt_ref.shape[0]):
        feat_t = featt_ref[b]
        grad_self = dot(feat_t, high_ref[rows_of(b), :]) + dot(feat_t, low_ref[rows_of(b), :])
        grad_neigh = dot_wide(jnp.transpose(raw_ref[b]), scaled_ref[rows_of(b), :])
        if b == 0:
            wsum[0], wsum[1] = grad_self, grad_neigh
        else:
            wsum[0] += grad_self
            wsum[1] += grad_neigh
    core = index_ref[index_ref.shape[0] - 1] % 2
    wkeep_ref[...] = wsum[core]
    wsend_ref[...] = wsum[1 - core]


def backward_kernel(section, group, index_ref, tiles_ref, gt_ref, *refs):
    acc_ref = refs[-1]
    block_local = gt_ref.shape[0]
    acc_ref[...] = jnp.zeros_like(acc_ref)

    def product(t, row, position):
        both = dot(gt_ref[jnp.minimum(row, block_local - 1)], tiles_ref[t])
        return both[:BLOCK] + both[BLOCK:]

    def add(t, row, position, value):
        acc_ref[position] += value

    over_tiles(section, group, index_ref, product, add)


def send_kernel(square, acc_ref, *refs):
    send_ref = refs[-1]
    block_local = send_ref.shape[1] // BLOCK
    for q in range(4):
        for b in range(block_local):
            send_ref[q, rows_of(b), :] = acc_ref[(8 * square + 2 * q + 1) * block_local + b]


def cut_kernel(index_ref, wkeep_ref, wgot_ref, *parts):
    rows = parts[0].shape[0]
    chip = index_ref[index_ref.shape[0] - 1] // 2 % 4
    for p, ref in enumerate(parts):
        span = pl.ds(pl.multiple_of((chip ^ p) * rows, rows), rows)
        ref[...] = wkeep_ref[span, :] + wgot_ref[span, :]


def pair_kernel(square, chips, acc_ref, got_ref, *refs):
    refs = refs[-len(chips):]
    block_local = got_ref.shape[1] // BLOCK
    for q, ref in zip(chips, refs):
        for b in range(block_local):
            kept = acc_ref[(8 * square + 2 * q) * block_local + b]
            ref[rows_of(b), :] = (kept + got_ref[q, rows_of(b), :]).astype(ref.dtype)


def pair_weights_kernel(square, acc_ref, got_ref, w1, w2, w3, own_ref, *pieces):
    pair_kernel(square, range(4), acc_ref, got_ref, own_ref, *pieces)
    nodes, lanes = own_ref.shape
    for weight_ref, ref in zip((w1, w2, w3), pieces):
        rows, columns = weight_ref.shape
        start = nodes
        for part in split_bf16(weight_ref[...]):
            for column in range(0, columns, lanes):
                ref[pl.ds(start, rows), :] = part[:, column:column + lanes]
                start += rows


def add_two_kernel(own_ref, got_ref, out_ref):
    out_ref[...] = own_ref[...] + got_ref[...]


def add_kernel(own_ref, *refs):
    total = own_ref[...]
    for got_ref in refs[:-1]:
        total = total + got_ref[...].astype(F32)
    refs[-1][...] = total.astype(BF16)


def add_weights_kernel(weight_ref, own_ref, *refs):
    got_refs, (out_ref, weight_out) = refs[:-2], refs[-2:]
    nodes, lanes = own_ref.shape
    add_kernel(own_ref, *[ref.at[pl.ds(0, nodes), :] for ref in got_refs], out_ref)
    rows, columns = weight_ref.shape
    cuts = columns // lanes
    for cut in range(cuts):
        span = pl.ds(cut * lanes, lanes)
        total = weight_ref[:, span]
        for ref in got_refs[:3]:
            high = ref[pl.ds(nodes + cut * rows, rows), :]
            low = ref[pl.ds(nodes + (cuts + cut) * rows, rows), :]
            total = total + (high.astype(F32) + low.astype(F32))
        weight_out[:, span] = total


def near_kernel(high_ref, low_ref, ws_ref, own_ref, *refs):
    ws = ws_ref[...]
    for b in range(own_ref.shape[0] // BLOCK):
        total = own_ref[rows_of(b), :]
        for got_ref in refs[:-1]:
            total = total + got_ref[rows_of(b), :].astype(F32)
        base = dot(high_ref[rows_of(b), :], ws, LAST) + dot(low_ref[rows_of(b), :], ws, LAST)
        refs[-1][rows_of(b), :] = base + jnp.transpose(total)


def main_kernel(near_ref, *refs):
    for b in range(near_ref.shape[0] // BLOCK):
        total = refs[0][rows_of(b), :].astype(F32)
        for got_ref in refs[1:-1]:
            total = total + got_ref[rows_of(b), :].astype(F32)
        refs[-1][rows_of(b), :] = (near_ref[rows_of(b), :] + jnp.transpose(total)).astype(BF16)


def last_kernel(index_ref, weight_ref, other_ref, self_ref, neigh_ref):
    me = index_ref[index_ref.shape[0] - 1]
    first = me % 2 == 0
    chip = me // 2 % 4
    rows = weight_ref.shape[2]
    for p in range(4):
        span = pl.ds(pl.multiple_of((chip ^ p) * rows, rows), rows)
        mine, other = weight_ref[p % 2, p // 2], other_ref[p % 2, p // 2]
        self_ref[span, :] = jnp.where(first, mine, other)
        neigh_ref[span, :] = jnp.where(first, other, mine)


def body(features, tiles, tile_row, tile_col, degree, train_mask, w_self, w_neigh, cotangent):
    n = lax.axis_size("row")
    me = lax.axis_index("row").astype(jnp.int32).reshape(1)
    squares = n // 8
    nodes, feat_in = features.shape
    hidden = w_self.shape[1]
    block_local = nodes // BLOCK
    tile_count = tiles.shape[0]
    group = max(g for g in range(1, 11) if tile_count % g == 0)
    small = n * nodes * feat_in * 4 <= 4 * MIB
    limit = (24 if small else 56) * MIB

    def result(shape, dtype, stays=True):
        kind = pltpu.VMEM if small and stays else jax.ShapeDtypeStruct
        return kind(shape, dtype)

    def placed(x, spec):
        if spec is SMEM or not small:
            return x
        return pltpu.with_memory_space_constraint(x, pltpu.HBM if spec is ANY else pltpu.VMEM)

    def call(kernel, name, out_shape, operands, in_specs=None, out_specs=None, cost_us=0.2, **more):
        specs = in_specs or [VMEM] * len(operands)
        return pl.pallas_call(
            kernel,
            out_shape=out_shape,
            in_specs=specs,
            out_specs=out_specs or jax.tree.map(lambda _: VMEM, out_shape),
            compiler_params=pltpu.CompilerParams(vmem_limit_bytes=limit),
            cost_estimate=pl.CostEstimate(
                flops=int(cost_us * 1.1e9), bytes_accessed=int(cost_us * 3.6e6), transcendentals=0),
            name=name,
            **more,
        )(*[placed(x, spec) for x, spec in zip(operands, specs)])

    wide, piece = result((nodes, feat_in), F32), result((nodes, feat_in), BF16)
    weight = result((feat_in, hidden), F32)
    chunk = result((feat_in // 4, hidden), F32)
    by_block = (block_local, BLOCK, feat_in)

    own_arguments = (
        degree.reshape(block_local, BLOCK), train_mask.reshape(block_local, BLOCK),
        w_self, w_neigh, features, cotangent,
    )
    if small:
        own_arguments = [pltpu.with_memory_space_constraint(x, pltpu.HBM) for x in own_arguments]
    tiles_near, ws, wn, inverse, upstream, pre_self, feat_t, own, index = pl.pallas_call(
        functools.partial(stage_kernel, (8 * block_local, (n - 8) * block_local)),
        out_shape=(
            result(tiles.shape, BF16),
            result(w_self.shape, BF16),
            result(w_neigh.shape, BF16),
            result(by_block, F32),
            result((nodes, hidden), F32),
            result((nodes, hidden), F32),
            result(by_block, BF16),
            piece,
            pltpu.SMEM((6 * tile_count + 3,), jnp.int32),
        ),
        in_specs=[SMEM] * 3 + [VMEM] * 6 + [ANY],
        out_specs=(VMEM,) * 8 + (SMEM,),
        scratch_shapes=[pltpu.SemaphoreType.DMA],
        compiler_params=pltpu.CompilerParams(vmem_limit_bytes=limit),
        cost_estimate=pl.CostEstimate(flops=int(3 * 1.1e9), bytes_accessed=int(3 * 3.6e6), transcendentals=0),
        name="stage_arguments",
    )(me, tile_row, tile_col, *own_arguments, placed(tiles, ANY))

    same, other = gather_by_xor(features, own, n, call, result((4, nodes, feat_in), BF16))
    near_square = (8 * block_local, BLOCK, feat_in)
    far_squares = ((n - 8) * block_local, BLOCK, feat_in)
    raw_shape = (block_local + 1, BLOCK, feat_in)
    raw = call(
        functools.partial(forward_near_kernel, group), "forward_near", result(raw_shape, F32),
        (index, tiles_near, same[0], other[0]), [SMEM] + [VMEM] * 3, cost_us=0.1,
        scratch_shapes=[pltpu.VMEM(near_square, BF16)],
    )
    operands = (index, tiles_near, wn, inverse, upstream, pre_self, raw, *same[1:], *other[1:])
    wide_out = result((nodes, hidden), BF16)
    embedded, high, low, scaled, gt, raw = call(
        functools.partial(forward_kernel, group, squares - 1),
        "forward_layer",
        (
            result((nodes, hidden), BF16, False), wide_out, wide_out, wide_out,
            result((block_local, 2 * feat_in, BLOCK), BF16), result(raw_shape, F32),
        ),
        operands,
        [SMEM] + [VMEM] * (len(operands) - 1),
        cost_us=3,
        scratch_shapes=[pltpu.VMEM(far_squares, BF16)],
    )

    wkeep, wsend = call(
        weights_kernel, "weights", (weight, weight),
        (index, high, low, scaled, raw, feat_t), [SMEM] + [VMEM] * 5, cost_us=1,
        scratch_shapes=[pltpu.VMEM((2, feat_in, hidden), F32)])
    w0, w1, w2, w3 = call(
        cut_kernel, "cut_weights", (chunk,) * 4, (index, wkeep, swap(wsend, n, 1)),
        [SMEM, VMEM, VMEM])

    send_shape = result((4, nodes, feat_in), F32)
    sums, got = [], [None] * squares
    for section, shape in ((1, far_squares), (0, near_square)):
        acc = call(
            functools.partial(backward_kernel, section, group), "backward_tiles",
            result((shape[0] + 1,) + shape[1:], F32), (index, tiles_near, gt, wkeep),
            [SMEM] + [VMEM] * 3, cost_us=1.5 if section else 0.3)
        sums.insert(0, acc)
        for s in range(squares - 1, 0, -1) if section else (0,):
            operands = (acc, wkeep if section else w0)
            send = call(functools.partial(send_kernel, s - section), "send", send_shape, operands)
            got[s] = swap(send, n, 1)

    extra = result((nodes + 2 * chunk.shape[0] * (hidden // feat_in), feat_in), BF16)
    terms = [[]]
    for s in range(1, squares):
        operands = (sums[1], got[s])
        if s == squares - 1:
            own, *pieces = call(
                functools.partial(pair_weights_kernel, s - 1), "pair_sum_weights",
                (wide, extra, extra, extra), operands + (w1, w2, w3))
        else:
            own, *pieces = call(
                functools.partial(pair_kernel, s - 1, range(4)), "pair_sum",
                (wide, piece, piece, piece), operands)
        terms.append([own, *[swap(pieces[q - 1], n, 2 * q) for q in (3, 1, 2)]])
    near_operands = (sums[0], got[0])
    own, *pieces = call(
        functools.partial(pair_kernel, 0, (0, 3, 1)), "pair_sum", (wide, piece, piece),
        near_operands)
    near = [own, swap(pieces[0], n, 6), swap(pieces[1], n, 2)]
    distance = 1
    while distance < squares:
        for s in range(squares - distance, 0, -2 * distance):
            if s == squares - 1:
                total, wsum = call(
                    add_weights_kernel, "square_sum_weights", (piece, chunk), (w0, *terms[s]),
                    cost_us=SQUARE_COST)
            else:
                total = call(add_kernel, "square_sum", piece, terms[s], cost_us=SQUARE_COST)
            terms[s - distance].append(swap(total, n, 8 * distance))
        distance *= 2
    later = call(
        functools.partial(pair_kernel, 0, (2,)), "pair_sum_later", piece, near_operands + (total,))
    near.append(swap(later, n, 4))
    near_total = call(near_kernel, "near_sum", wide, (high, low, ws, *near), cost_us=NEAR_COST)
    terms[0].insert(0, near_total)
    bit = 8
    while bit < n:
        wsum = call(add_two_kernel, "weight_sum", chunk, (wsum, swap(wsum, n, bit)))
        bit *= 2
    rows = chunk.shape[0]
    two = call(functools.partial(pack_kernel, (0, 1)), "pack_weights", result((2, rows, hidden), F32), (wsum, swap(wsum, n, 4)))
    mine = call(
        functools.partial(pack_kernel, (0, 1)), "pack_weights", result((2, 2, rows, hidden), F32), (two, swap(two, n, 2), near_total))
    grad_input = call(
        main_kernel, "grad_input_sum", result((nodes, feat_in), BF16, False), terms[0],
        cost_us=MAIN_COST)
    full = result((feat_in, hidden), F32, False)
    grad_self, grad_neigh = call(
        last_kernel, "write_weights", (full, full), (index, mine, swap(mine, n, 1)),
        [SMEM] + [VMEM] * 2)
    return (embedded, grad_input, grad_self, grad_neigh)


def solution(mesh):
    placed = (
        P(("parts", "row"), None),
        P(("parts", "row"), None, None),
        P(("parts", "row")),
        P(("parts", "row")),
        P(("parts", "row")),
        P(("parts", "row")),
        P(),
        P(),
        P(("parts", "row"), None),
    )
    return jax.shard_map(
        body,
        mesh=mesh,
        in_specs=placed,
        out_specs=(
            P(("parts", "row"), None),
            P(("parts", "row"), None),
            P("parts", None),
            P("parts", None),
        ),
        check_vma=False,
    )
```

```python
import functools

import jax
import jax.numpy as jnp
from jax import lax
from jax.experimental import pallas as pl
from jax.experimental.pallas import tpu as pltpu
from jax.sharding import PartitionSpec as P

BLOCK = 128
F32, BF16 = jnp.float32, jnp.bfloat16
VMEM = pl.BlockSpec(memory_space=pltpu.VMEM)
SMEM = pl.BlockSpec(memory_space=pltpu.SMEM)
ANY = pl.BlockSpec(memory_space=pl.ANY)
MIB = 1024 * 1024
LAST = ((1,), (1,))
NEAR_COST, SQUARE_COST, MAIN_COST = 0.2, 4, 10


def swap(x, n, offset):
    return lax.ppermute(x, "row", [(i, i ^ offset) for i in range(n)])


def gather_by_xor(x, own, n, call, pack):
    blocks = [x]
    bit = n // 2
    while bit >= 8:
        blocks = blocks + [swap(v, n, bit) for v in blocks]
        bit //= 2
    offsets = [0]
    bit = n // 2
    while bit >= 8:
        offsets = offsets + [o ^ bit for o in offsets]
        bit //= 2
    blocks = [v for _, v in sorted(zip(offsets, blocks), key=lambda pair: pair[0])]
    same = []
    for v in blocks:
        order = (2, 6, 4) if v is x else (6, 2, 4)
        square = (own if v is x else v, *[swap(v, n, offset) for offset in order])
        slots = (0, *[offset // 2 for offset in order])
        same.append(call(functools.partial(pack_kernel, slots), "pack_square", pack, square))
    return same, [swap(v, n, 1) for v in same]


def split_bf16(x):
    high = x.astype(BF16)
    return high, (x - high.astype(F32)).astype(BF16)


def dot(a, b, dims=((1,), (0,))):
    return lax.dot_general(a, b, (dims, ((), ())), preferred_element_type=F32)


def dot_wide(a, b, dims=((1,), (0,))):
    high, low = split_bf16(a)
    return dot(high, b, dims) + dot(low, b, dims)


def rows_to_lanes(row):
    return jnp.transpose(jnp.broadcast_to(row, (BLOCK, BLOCK)))


def rows_of(b):
    return pl.ds(b * BLOCK, BLOCK)


def pack_kernel(slots, *refs):
    for slot, ref in zip(slots, refs[:-1]):
        refs[-1][slot] = ref[...]


def stage_kernel(dumps, me_ref, trow_ref, tcol_ref, deg_ref, mask_ref, ws_ref, wn_ref, feat_ref, cot_ref,
                 tiles_ref, tiles_out, ws_out, wn_out, inverse_out, up_out, pre_out, featt_out,
                 own_out, index_out, sem):
    copy = pltpu.make_async_copy(tiles_ref, tiles_out, sem)
    copy.start()
    block_local = feat_ref.shape[0] // BLOCK
    tile_count = trow_ref.shape[0]
    me = me_ref[0]
    index_out[index_out.shape[0] - 1] = me

    def clear(i, carry):
        for section in range(2):
            index_out[3 * section * tile_count + i] = 0
            index_out[(3 * section + 1) * tile_count + i] = block_local
            index_out[(3 * section + 2) * tile_count + i] = dumps[section]
        return carry

    def place(t, counts):
        col = tcol_ref[t]
        live = col >= 0
        col = jnp.maximum(col, 0)
        chip_core = (col // block_local) ^ me
        far = chip_core >= 8
        position = jnp.where(far, chip_core - 8, chip_core) * block_local + col % block_local
        row = jnp.clip(trow_ref[t] - me * block_local, 0, block_local - 1)
        near_count, far_count = counts
        spot = jnp.where(far, 3 * tile_count + far_count, near_count)

        @pl.when(live)
        def _():
            index_out[spot] = t
            index_out[spot + tile_count] = row
            index_out[spot + 2 * tile_count] = position

        add = live.astype(jnp.int32)
        add_far = far.astype(jnp.int32) * add
        return near_count + add - add_far, far_count + add_far

    lax.fori_loop(0, tile_count, clear, 0)
    near_count, far_count = lax.fori_loop(0, tile_count, place, (jnp.int32(0), jnp.int32(0)))
    index_out[6 * tile_count] = near_count
    index_out[6 * tile_count + 1] = far_count
    own_out[...] = feat_ref[...]
    ws_out[...] = ws_ref[...]
    wn_out[...] = wn_ref[...]
    ws = ws_ref[...]
    for b in range(block_local):
        degree = rows_to_lanes(deg_ref[pl.ds(b, 1), :].astype(F32))
        mask = rows_to_lanes(mask_ref[pl.ds(b, 1), :].astype(F32))
        inverse_out[b] = 1.0 / degree
        feat = feat_ref[rows_of(b), :]
        featt_out[b] = jnp.transpose(feat.astype(F32)).astype(BF16)
        pre_out[rows_of(b), :] = dot(feat, ws)
        up_out[rows_of(b), :] = cot_ref[rows_of(b), :].astype(F32) * jnp.concatenate(
            [mask, mask], axis=1)
    copy.wait()


def over_tiles(section, group, index_ref, product, add):
    tile_count = (index_ref.shape[0] - 3) // 6
    start = 3 * section * tile_count

    def step(i, carry):
        spots = [start + i * group + u for u in range(group)]
        entries = [
            (index_ref[spot], index_ref[spot + tile_count], index_ref[spot + 2 * tile_count])
            for spot in spots
        ]
        products = [product(*entry) for entry in entries]
        for entry, value in zip(entries, products):
            add(*entry, value)
        return carry

    count = index_ref[6 * tile_count + section]
    lax.fori_loop(0, (count + group - 1) // group, step, 0)


def gathered_products(section, group, index_ref, tiles_ref, feat_refs, feats, raw):
    squares = len(feat_refs) // 2
    block_local = raw.shape[0] - 1
    for s in range(squares):
        for q in range(4):
            for core in range(2):
                for b in range(block_local):
                    spot = (8 * s + 2 * q + core) * block_local + b
                    feats[spot] = feat_refs[core * squares + s][q, rows_of(b), :]

    def add(t, row, position, value):
        raw[row] += value

    over_tiles(
        section, group, index_ref,
        lambda t, row, position: dot(tiles_ref[t], feats[jnp.minimum(position, feats.shape[0] - 1)]),
        add)


def forward_near_kernel(group, index_ref, tiles_ref, same_ref, other_ref, raw, feats):
    raw[...] = jnp.zeros_like(raw)
    gathered_products(0, group, index_ref, tiles_ref, (same_ref, other_ref), feats, raw)


def forward_kernel(group, far, index_ref, tiles_ref, wn_ref, inverse_ref, up_ref, pre_ref,
                   near_ref, *refs):
    feat_refs, refs = refs[:2 * far], refs[2 * far:]
    emb_ref, high_ref, low_ref, scaled_ref, gt_ref, raw, feats = refs
    block_local = inverse_ref.shape[0]
    raw[...] = near_ref[...]
    gathered_products(1, group, index_ref, tiles_ref, feat_refs, feats, raw)
    wn = wn_ref[...]
    for b in range(block_local):
        inverse = inverse_ref[b]
        pre = pre_ref[rows_of(b), :] + dot_wide(raw[b] * inverse, wn)
        sig = jax.nn.sigmoid(pre)
        emb_ref[rows_of(b), :] = (pre * sig).astype(BF16)
        grad_pre = up_ref[rows_of(b), :] * sig * (1.0 + pre * (1.0 - sig))
        scaled = (grad_pre * jnp.concatenate([inverse, inverse], axis=1)).astype(BF16)
        scaled_ref[rows_of(b), :] = scaled
        high_ref[rows_of(b), :], low_ref[rows_of(b), :] = split_bf16(grad_pre)
        high, low = split_bf16(dot(wn, scaled, LAST))
        gt_ref[b, :BLOCK, :] = high
        gt_ref[b, BLOCK:, :] = low


def weights_kernel(index_ref, high_ref, low_ref, scaled_ref, raw_ref, featt_ref, *refs):
    wkeep_ref, wsend_ref, wsum = refs[-3:]
    for b in range(featt_ref.shape[0]):
        feat_t = featt_ref[b]
        grad_self = dot(feat_t, high_ref[rows_of(b), :]) + dot(feat_t, low_ref[rows_of(b), :])
        grad_neigh = dot_wide(jnp.transpose(raw_ref[b]), scaled_ref[rows_of(b), :])
        if b == 0:
            wsum[0], wsum[1] = grad_self, grad_neigh
        else:
            wsum[0] += grad_self
            wsum[1] += grad_neigh
    core = index_ref[index_ref.shape[0] - 1] % 2
    wkeep_ref[...] = wsum[core]
    wsend_ref[...] = wsum[1 - core]


def backward_kernel(section, group, index_ref, tiles_ref, gt_ref, *refs):
    acc_ref = refs[-1]
    block_local = gt_ref.shape[0]
    acc_ref[...] = jnp.zeros_like(acc_ref)

    def product(t, row, position):
        both = dot(gt_ref[jnp.minimum(row, block_local - 1)], tiles_ref[t])
        return both[:BLOCK] + both[BLOCK:]

    def add(t, row, position, value):
        acc_ref[position] += value

    over_tiles(section, group, index_ref, product, add)


def send_kernel(square, acc_ref, *refs):
    send_ref = refs[-1]
    block_local = send_ref.shape[1] // BLOCK
    for q in range(4):
        for b in range(block_local):
            send_ref[q, rows_of(b), :] = acc_ref[(8 * square + 2 * q + 1) * block_local + b]


def cut_kernel(index_ref, wkeep_ref, wgot_ref, *parts):
    rows = parts[0].shape[0]
    chip = index_ref[index_ref.shape[0] - 1] // 2 % 4
    for p, ref in enumerate(parts):
        span = pl.ds(pl.multiple_of((chip ^ p) * rows, rows), rows)
        ref[...] = wkeep_ref[span, :] + wgot_ref[span, :]


def pair_kernel(square, chips, acc_ref, got_ref, *refs):
    refs = refs[-len(chips):]
    block_local = got_ref.shape[1] // BLOCK
    for q, ref in zip(chips, refs):
        for b in range(block_local):
            kept = acc_ref[(8 * square + 2 * q) * block_local + b]
            ref[rows_of(b), :] = (kept + got_ref[q, rows_of(b), :]).astype(ref.dtype)


def pair_weights_kernel(square, acc_ref, got_ref, w1, w2, w3, own_ref, *pieces):
    pair_kernel(square, range(4), acc_ref, got_ref, own_ref, *pieces)
    nodes, lanes = own_ref.shape
    for weight_ref, ref in zip((w1, w2, w3), pieces):
        rows, columns = weight_ref.shape
        start = nodes
        for part in split_bf16(weight_ref[...]):
            for column in range(0, columns, lanes):
                ref[pl.ds(start, rows), :] = part[:, column:column + lanes]
                start += rows


def add_two_kernel(own_ref, got_ref, out_ref):
    out_ref[...] = own_ref[...] + got_ref[...]


def add_kernel(own_ref, *refs):
    total = own_ref[...]
    for got_ref in refs[:-1]:
        total = total + got_ref[...].astype(F32)
    refs[-1][...] = total.astype(BF16)


def add_weights_kernel(weight_ref, own_ref, *refs):
    got_refs, (out_ref, weight_out) = refs[:-2], refs[-2:]
    nodes, lanes = own_ref.shape
    add_kernel(own_ref, *[ref.at[pl.ds(0, nodes), :] for ref in got_refs], out_ref)
    rows, columns = weight_ref.shape
    cuts = columns // lanes
    for cut in range(cuts):
        span = pl.ds(cut * lanes, lanes)
        total = weight_ref[:, span]
        for ref in got_refs[:3]:
            high = ref[pl.ds(nodes + cut * rows, rows), :]
            low = ref[pl.ds(nodes + (cuts + cut) * rows, rows), :]
            total = total + (high.astype(F32) + low.astype(F32))
        weight_out[:, span] = total


def near_kernel(high_ref, low_ref, ws_ref, own_ref, *refs):
    ws = ws_ref[...]
    for b in range(own_ref.shape[0] // BLOCK):
        total = own_ref[rows_of(b), :]
        for got_ref in refs[:-1]:
            total = total + got_ref[rows_of(b), :].astype(F32)
        base = dot(high_ref[rows_of(b), :], ws, LAST) + dot(low_ref[rows_of(b), :], ws, LAST)
        refs[-1][rows_of(b), :] = base + jnp.transpose(total)


def main_kernel(near_ref, *refs):
    for b in range(near_ref.shape[0] // BLOCK):
        total = refs[0][rows_of(b), :].astype(F32)
        for got_ref in refs[1:-1]:
            total = total + got_ref[rows_of(b), :].astype(F32)
        refs[-1][rows_of(b), :] = (near_ref[rows_of(b), :] + jnp.transpose(total)).astype(BF16)


def last_kernel(index_ref, weight_ref, other_ref, self_ref, neigh_ref):
    me = index_ref[index_ref.shape[0] - 1]
    first = me % 2 == 0
    chip = me // 2 % 4
    rows = weight_ref.shape[2]
    for p in range(4):
        span = pl.ds(pl.multiple_of((chip ^ p) * rows, rows), rows)
        mine, other = weight_ref[p % 2, p // 2], other_ref[p % 2, p // 2]
        self_ref[span, :] = jnp.where(first, mine, other)
        neigh_ref[span, :] = jnp.where(first, other, mine)


def body(features, tiles, tile_row, tile_col, degree, train_mask, w_self, w_neigh, cotangent):
    n = lax.axis_size("row")
    me = lax.axis_index("row").astype(jnp.int32).reshape(1)
    squares = n // 8
    nodes, feat_in = features.shape
    hidden = w_self.shape[1]
    block_local = nodes // BLOCK
    tile_count = tiles.shape[0]
    group = max(g for g in range(1, 11) if tile_count % g == 0)
    small = n * nodes * feat_in * 4 <= 4 * MIB
    limit = (24 if small else 56) * MIB

    def result(shape, dtype, stays=True):
        kind = pltpu.VMEM if small and stays else jax.ShapeDtypeStruct
        return kind(shape, dtype)

    def placed(x, spec):
        if spec is SMEM or not small:
            return x
        return pltpu.with_memory_space_constraint(x, pltpu.HBM if spec is ANY else pltpu.VMEM)

    def call(kernel, name, out_shape, operands, in_specs=None, out_specs=None, cost_us=0.2, **more):
        specs = in_specs or [VMEM] * len(operands)
        return pl.pallas_call(
            kernel,
            out_shape=out_shape,
            in_specs=specs,
            out_specs=out_specs or jax.tree.map(lambda _: VMEM, out_shape),
            compiler_params=pltpu.CompilerParams(vmem_limit_bytes=limit),
            cost_estimate=pl.CostEstimate(
                flops=int(cost_us * 1.1e9), bytes_accessed=int(cost_us * 3.6e6), transcendentals=0),
            name=name,
            **more,
        )(*[placed(x, spec) for x, spec in zip(operands, specs)])

    wide, piece = result((nodes, feat_in), F32), result((nodes, feat_in), BF16)
    weight = result((feat_in, hidden), F32)
    chunk = result((feat_in // 4, hidden), F32)
    by_block = (block_local, BLOCK, feat_in)

    own_arguments = (
        degree.reshape(block_local, BLOCK), train_mask.reshape(block_local, BLOCK),
        w_self, w_neigh, features, cotangent,
    )
    if small:
        own_arguments = [pltpu.with_memory_space_constraint(x, pltpu.HBM) for x in own_arguments]
    tiles_near, ws, wn, inverse, upstream, pre_self, feat_t, own, index = pl.pallas_call(
        functools.partial(stage_kernel, (8 * block_local, (n - 8) * block_local)),
        out_shape=(
            result(tiles.shape, BF16),
            result(w_self.shape, BF16),
            result(w_neigh.shape, BF16),
            result(by_block, F32),
            result((nodes, hidden), F32),
            result((nodes, hidden), F32),
            result(by_block, BF16),
            piece,
            pltpu.SMEM((6 * tile_count + 3,), jnp.int32),
        ),
        in_specs=[SMEM] * 3 + [VMEM] * 6 + [ANY],
        out_specs=(VMEM,) * 8 + (SMEM,),
        scratch_shapes=[pltpu.SemaphoreType.DMA],
        compiler_params=pltpu.CompilerParams(vmem_limit_bytes=limit),
        cost_estimate=pl.CostEstimate(flops=int(3 * 1.1e9), bytes_accessed=int(3 * 3.6e6), transcendentals=0),
        name="stage_arguments",
    )(me, tile_row, tile_col, *own_arguments, placed(tiles, ANY))

    same, other = gather_by_xor(features, own, n, call, result((4, nodes, feat_in), BF16))
    near_square = (8 * block_local, BLOCK, feat_in)
    far_squares = ((n - 8) * block_local, BLOCK, feat_in)
    raw_shape = (block_local + 1, BLOCK, feat_in)
    raw = call(
        functools.partial(forward_near_kernel, group), "forward_near", result(raw_shape, F32),
        (index, tiles_near, same[0], other[0]), [SMEM] + [VMEM] * 3, cost_us=0.1,
        scratch_shapes=[pltpu.VMEM(near_square, BF16)],
    )
    operands = (index, tiles_near, wn, inverse, upstream, pre_self, raw, *same[1:], *other[1:])
    wide_out = result((nodes, hidden), BF16)
    embedded, high, low, scaled, gt, raw = call(
        functools.partial(forward_kernel, group, squares - 1),
        "forward_layer",
        (
            result((nodes, hidden), BF16, False), wide_out, wide_out, wide_out,
            result((block_local, 2 * feat_in, BLOCK), BF16), result(raw_shape, F32),
        ),
        operands,
        [SMEM] + [VMEM] * (len(operands) - 1),
        cost_us=3,
        scratch_shapes=[pltpu.VMEM(far_squares, BF16)],
    )

    wkeep, wsend = call(
        weights_kernel, "weights", (weight, weight),
        (index, high, low, scaled, raw, feat_t), [SMEM] + [VMEM] * 5, cost_us=1,
        scratch_shapes=[pltpu.VMEM((2, feat_in, hidden), F32)])
    w0, w1, w2, w3 = call(
        cut_kernel, "cut_weights", (chunk,) * 4, (index, wkeep, swap(wsend, n, 1)),
        [SMEM, VMEM, VMEM])

    send_shape = result((4, nodes, feat_in), F32)
    sums, got = [], [None] * squares
    for section, shape in ((1, far_squares), (0, near_square)):
        acc = call(
            functools.partial(backward_kernel, section, group), "backward_tiles",
            result((shape[0] + 1,) + shape[1:], F32), (index, tiles_near, gt, wkeep),
            [SMEM] + [VMEM] * 3, cost_us=1.5 if section else 0.3)
        sums.insert(0, acc)
        for s in range(squares - 1, 0, -1) if section else (0,):
            operands = (acc, wkeep if section else w0)
            send = call(functools.partial(send_kernel, s - section), "send", send_shape, operands)
            got[s] = swap(send, n, 1)

    extra = result((nodes + 2 * chunk.shape[0] * (hidden // feat_in), feat_in), BF16)
    terms = [[]]
    for s in range(1, squares):
        operands = (sums[1], got[s])
        if s == squares - 1:
            own, *pieces = call(
                functools.partial(pair_weights_kernel, s - 1), "pair_sum_weights",
                (wide, extra, extra, extra), operands + (w1, w2, w3))
        else:
            own, *pieces = call(
                functools.partial(pair_kernel, s - 1, range(4)), "pair_sum",
                (wide, piece, piece, piece), operands)
        terms.append([own, *[swap(pieces[q - 1], n, 2 * q) for q in (3, 1, 2)]])
    near_operands = (sums[0], got[0])
    own, *pieces = call(
        functools.partial(pair_kernel, 0, (0, 3)), "pair_sum", (wide, piece), near_operands)
    near = [own, swap(pieces[0], n, 6)]
    distance = 1
    while distance < squares:
        for s in range(squares - distance, 0, -2 * distance):
            if s == squares - 1:
                total, wsum = call(
                    add_weights_kernel, "square_sum_weights", (piece, chunk), (w0, *terms[s]),
                    cost_us=SQUARE_COST)
            else:
                total = call(add_kernel, "square_sum", piece, terms[s], cost_us=SQUARE_COST)
            terms[s - distance].append(swap(total, n, 8 * distance))
        distance *= 2
    along_z, along_y = call(
        functools.partial(pair_kernel, 0, (2, 1)), "pair_sum_later", (piece, piece),
        near_operands + (total,))
    near += [swap(along_z, n, 4), swap(along_y, n, 2)]
    near_total = call(near_kernel, "near_sum", wide, (high, low, ws, *near), cost_us=NEAR_COST)
    terms[0].insert(0, near_total)
    bit = 8
    while bit < n:
        wsum = call(add_two_kernel, "weight_sum", chunk, (wsum, swap(wsum, n, bit)))
        bit *= 2
    rows = chunk.shape[0]
    two = call(functools.partial(pack_kernel, (0, 1)), "pack_weights", result((2, rows, hidden), F32), (wsum, swap(wsum, n, 4)))
    mine = call(
        functools.partial(pack_kernel, (0, 1)), "pack_weights", result((2, 2, rows, hidden), F32), (two, swap(two, n, 2), near_total))
    grad_input = call(
        main_kernel, "grad_input_sum", result((nodes, feat_in), BF16, False), terms[0],
        cost_us=MAIN_COST)
    full = result((feat_in, hidden), F32, False)
    grad_self, grad_neigh = call(
        last_kernel, "write_weights", (full, full), (index, mine, swap(mine, n, 1)),
        [SMEM] + [VMEM] * 2)
    return (embedded, grad_input, grad_self, grad_neigh)


def solution(mesh):
    placed = (
        P(("parts", "row"), None),
        P(("parts", "row"), None, None),
        P(("parts", "row")),
        P(("parts", "row")),
        P(("parts", "row")),
        P(("parts", "row")),
        P(),
        P(),
        P(("parts", "row"), None),
    )
    return jax.shard_map(
        body,
        mesh=mesh,
        in_specs=placed,
        out_specs=(
            P(("parts", "row"), None),
            P(("parts", "row"), None),
            P("parts", None),
            P("parts", None),
        ),
        check_vma=False,
    )
```

```python
import functools

import jax
import jax.numpy as jnp
from jax import lax
from jax.experimental import pallas as pl
from jax.experimental.pallas import tpu as pltpu
from jax.sharding import PartitionSpec as P

BLOCK = 128
F32, BF16 = jnp.float32, jnp.bfloat16
VMEM = pl.BlockSpec(memory_space=pltpu.VMEM)
SMEM = pl.BlockSpec(memory_space=pltpu.SMEM)
ANY = pl.BlockSpec(memory_space=pl.ANY)
MIB = 1024 * 1024
LAST = ((1,), (1,))
NEAR_COST, SQUARE_COST, MAIN_COST, FAR_COST = 0.2, 4, 0.2, 10


def swap(x, n, offset):
    return lax.ppermute(x, "row", [(i, i ^ offset) for i in range(n)])


def gather_by_xor(x, own, n, call, pack):
    blocks = [x]
    bit = n // 2
    while bit >= 8:
        blocks = blocks + [swap(v, n, bit) for v in blocks]
        bit //= 2
    offsets = [0]
    bit = n // 2
    while bit >= 8:
        offsets = offsets + [o ^ bit for o in offsets]
        bit //= 2
    blocks = [v for _, v in sorted(zip(offsets, blocks), key=lambda pair: pair[0])]
    same = []
    for v in blocks:
        order = (2, 6, 4) if v is x else (6, 2, 4)
        square = (own if v is x else v, *[swap(v, n, offset) for offset in order])
        slots = (0, *[offset // 2 for offset in order])
        same.append(call(functools.partial(pack_kernel, slots), "pack_square", pack, square))
    return same, [swap(v, n, 1) for v in same]


def split_bf16(x):
    high = x.astype(BF16)
    return high, (x - high.astype(F32)).astype(BF16)


def dot(a, b, dims=((1,), (0,))):
    return lax.dot_general(a, b, (dims, ((), ())), preferred_element_type=F32)


def dot_wide(a, b, dims=((1,), (0,))):
    high, low = split_bf16(a)
    return dot(high, b, dims) + dot(low, b, dims)


def rows_to_lanes(row):
    return jnp.transpose(jnp.broadcast_to(row, (BLOCK, BLOCK)))


def rows_of(b):
    return pl.ds(b * BLOCK, BLOCK)


def pack_kernel(slots, *refs):
    for slot, ref in zip(slots, refs[:-1]):
        refs[-1][slot] = ref[...]


def stage_kernel(dumps, me_ref, trow_ref, tcol_ref, deg_ref, mask_ref, ws_ref, wn_ref, feat_ref, cot_ref,
                 tiles_ref, tiles_out, ws_out, wn_out, inverse_out, up_out, pre_out, featt_out,
                 own_out, index_out, sem):
    copy = pltpu.make_async_copy(tiles_ref, tiles_out, sem)
    copy.start()
    block_local = feat_ref.shape[0] // BLOCK
    tile_count = trow_ref.shape[0]
    me = me_ref[0]
    index_out[index_out.shape[0] - 1] = me

    def clear(i, carry):
        for section in range(2):
            index_out[3 * section * tile_count + i] = 0
            index_out[(3 * section + 1) * tile_count + i] = block_local
            index_out[(3 * section + 2) * tile_count + i] = dumps[section]
        return carry

    def place(t, counts):
        col = tcol_ref[t]
        live = col >= 0
        col = jnp.maximum(col, 0)
        chip_core = (col // block_local) ^ me
        far = chip_core >= 8
        position = jnp.where(far, chip_core - 8, chip_core) * block_local + col % block_local
        row = jnp.clip(trow_ref[t] - me * block_local, 0, block_local - 1)
        near_count, far_count = counts
        spot = jnp.where(far, 3 * tile_count + far_count, near_count)

        @pl.when(live)
        def _():
            index_out[spot] = t
            index_out[spot + tile_count] = row
            index_out[spot + 2 * tile_count] = position

        add = live.astype(jnp.int32)
        add_far = far.astype(jnp.int32) * add
        return near_count + add - add_far, far_count + add_far

    lax.fori_loop(0, tile_count, clear, 0)
    near_count, far_count = lax.fori_loop(0, tile_count, place, (jnp.int32(0), jnp.int32(0)))
    index_out[6 * tile_count] = near_count
    index_out[6 * tile_count + 1] = far_count
    own_out[...] = feat_ref[...]
    ws_out[...] = ws_ref[...]
    wn_out[...] = wn_ref[...]
    ws = ws_ref[...]
    for b in range(block_local):
        degree = rows_to_lanes(deg_ref[pl.ds(b, 1), :].astype(F32))
        mask = rows_to_lanes(mask_ref[pl.ds(b, 1), :].astype(F32))
        inverse_out[b] = 1.0 / degree
        feat = feat_ref[rows_of(b), :]
        featt_out[b] = jnp.transpose(feat.astype(F32)).astype(BF16)
        pre_out[rows_of(b), :] = dot(feat, ws)
        up_out[rows_of(b), :] = cot_ref[rows_of(b), :].astype(F32) * jnp.concatenate(
            [mask, mask], axis=1)
    copy.wait()


def over_tiles(section, group, index_ref, product, add):
    tile_count = (index_ref.shape[0] - 3) // 6
    start = 3 * section * tile_count

    def step(i, carry):
        spots = [start + i * group + u for u in range(group)]
        entries = [
            (index_ref[spot], index_ref[spot + tile_count], index_ref[spot + 2 * tile_count])
            for spot in spots
        ]
        products = [product(*entry) for entry in entries]
        for entry, value in zip(entries, products):
            add(*entry, value)
        return carry

    count = index_ref[6 * tile_count + section]
    lax.fori_loop(0, (count + group - 1) // group, step, 0)


def gathered_products(section, group, index_ref, tiles_ref, feat_refs, feats, raw):
    squares = len(feat_refs) // 2
    block_local = raw.shape[0] - 1
    for s in range(squares):
        for q in range(4):
            for core in range(2):
                for b in range(block_local):
                    spot = (8 * s + 2 * q + core) * block_local + b
                    feats[spot] = feat_refs[core * squares + s][q, rows_of(b), :]

    def add(t, row, position, value):
        raw[row] += value

    over_tiles(
        section, group, index_ref,
        lambda t, row, position: dot(tiles_ref[t], feats[jnp.minimum(position, feats.shape[0] - 1)]),
        add)


def forward_near_kernel(group, index_ref, tiles_ref, same_ref, other_ref, raw, feats):
    raw[...] = jnp.zeros_like(raw)
    gathered_products(0, group, index_ref, tiles_ref, (same_ref, other_ref), feats, raw)


def forward_kernel(group, far, index_ref, tiles_ref, wn_ref, inverse_ref, up_ref, pre_ref,
                   near_ref, *refs):
    feat_refs, refs = refs[:2 * far], refs[2 * far:]
    emb_ref, high_ref, low_ref, scaled_ref, gt_ref, raw, feats = refs
    block_local = inverse_ref.shape[0]
    raw[...] = near_ref[...]
    gathered_products(1, group, index_ref, tiles_ref, feat_refs, feats, raw)
    wn = wn_ref[...]
    for b in range(block_local):
        inverse = inverse_ref[b]
        pre = pre_ref[rows_of(b), :] + dot_wide(raw[b] * inverse, wn)
        sig = jax.nn.sigmoid(pre)
        emb_ref[rows_of(b), :] = (pre * sig).astype(BF16)
        grad_pre = up_ref[rows_of(b), :] * sig * (1.0 + pre * (1.0 - sig))
        scaled = (grad_pre * jnp.concatenate([inverse, inverse], axis=1)).astype(BF16)
        scaled_ref[rows_of(b), :] = scaled
        high_ref[rows_of(b), :], low_ref[rows_of(b), :] = split_bf16(grad_pre)
        high, low = split_bf16(dot(wn, scaled, LAST))
        gt_ref[b, :BLOCK, :] = high
        gt_ref[b, BLOCK:, :] = low


def weights_kernel(index_ref, high_ref, low_ref, scaled_ref, raw_ref, featt_ref, *refs):
    wkeep_ref, wsend_ref, wsum = refs[-3:]
    for b in range(featt_ref.shape[0]):
        feat_t = featt_ref[b]
        grad_self = dot(feat_t, high_ref[rows_of(b), :]) + dot(feat_t, low_ref[rows_of(b), :])
        grad_neigh = dot_wide(jnp.transpose(raw_ref[b]), scaled_ref[rows_of(b), :])
        if b == 0:
            wsum[0], wsum[1] = grad_self, grad_neigh
        else:
            wsum[0] += grad_self
            wsum[1] += grad_neigh
    core = index_ref[index_ref.shape[0] - 1] % 2
    wkeep_ref[...] = wsum[core]
    wsend_ref[...] = wsum[1 - core]


def backward_kernel(section, group, index_ref, tiles_ref, gt_ref, *refs):
    acc_ref = refs[-1]
    block_local = gt_ref.shape[0]
    acc_ref[...] = jnp.zeros_like(acc_ref)

    def product(t, row, position):
        both = dot(gt_ref[jnp.minimum(row, block_local - 1)], tiles_ref[t])
        return both[:BLOCK] + both[BLOCK:]

    def add(t, row, position, value):
        acc_ref[position] += value

    over_tiles(section, group, index_ref, product, add)


def send_kernel(square, acc_ref, *refs):
    send_ref = refs[-1]
    block_local = send_ref.shape[1] // BLOCK
    for q in range(4):
        for b in range(block_local):
            send_ref[q, rows_of(b), :] = acc_ref[(8 * square + 2 * q + 1) * block_local + b]


def cut_kernel(index_ref, wkeep_ref, wgot_ref, *parts):
    rows = parts[0].shape[0]
    chip = index_ref[index_ref.shape[0] - 1] // 2 % 4
    for p, ref in enumerate(parts):
        span = pl.ds(pl.multiple_of((chip ^ p) * rows, rows), rows)
        ref[...] = wkeep_ref[span, :] + wgot_ref[span, :]


def pair_kernel(square, chips, acc_ref, got_ref, *refs):
    refs = refs[-len(chips):]
    block_local = got_ref.shape[1] // BLOCK
    for q, ref in zip(chips, refs):
        for b in range(block_local):
            kept = acc_ref[(8 * square + 2 * q) * block_local + b]
            ref[rows_of(b), :] = (kept + got_ref[q, rows_of(b), :]).astype(ref.dtype)


def pair_weights_kernel(square, acc_ref, got_ref, w1, w2, w3, own_ref, *pieces):
    pair_kernel(square, range(4), acc_ref, got_ref, own_ref, *pieces)
    nodes, lanes = own_ref.shape
    for weight_ref, ref in zip((w1, w2, w3), pieces):
        rows, columns = weight_ref.shape
        start = nodes
        for part in split_bf16(weight_ref[...]):
            for column in range(0, columns, lanes):
                ref[pl.ds(start, rows), :] = part[:, column:column + lanes]
                start += rows


def add_two_kernel(own_ref, got_ref, *refs):
    refs[-1][...] = own_ref[...] + got_ref[...]


def add_kernel(own_ref, *refs):
    total = own_ref[...].astype(F32)
    for got_ref in refs[:-1]:
        total = total + got_ref[...].astype(F32)
    refs[-1][...] = total.astype(refs[-1].dtype)


def add_weights_kernel(weight_ref, own_ref, *refs):
    got_refs, (out_ref, weight_out) = refs[:-2], refs[-2:]
    nodes, lanes = own_ref.shape
    add_kernel(own_ref, *[ref.at[pl.ds(0, nodes), :] for ref in got_refs], out_ref)
    rows, columns = weight_ref.shape
    cuts = columns // lanes
    for cut in range(cuts):
        span = pl.ds(cut * lanes, lanes)
        total = weight_ref[:, span]
        for ref in got_refs[:3]:
            high = ref[pl.ds(nodes + cut * rows, rows), :]
            low = ref[pl.ds(nodes + (cuts + cut) * rows, rows), :]
            total = total + (high.astype(F32) + low.astype(F32))
        weight_out[:, span] = total


def near_kernel(high_ref, low_ref, ws_ref, own_ref, *refs):
    ws = ws_ref[...]
    for b in range(own_ref.shape[0] // BLOCK):
        total = own_ref[rows_of(b), :]
        for got_ref in refs[:-1]:
            total = total + got_ref[rows_of(b), :].astype(F32)
        base = dot(high_ref[rows_of(b), :], ws, LAST) + dot(low_ref[rows_of(b), :], ws, LAST)
        refs[-1][rows_of(b), :] = base + jnp.transpose(total)


def main_kernel(near_ref, *refs):
    for b in range(near_ref.shape[0] // BLOCK):
        total = refs[0][rows_of(b), :].astype(F32)
        for got_ref in refs[1:-1]:
            total = total + got_ref[rows_of(b), :].astype(F32)
        refs[-1][rows_of(b), :] = (near_ref[rows_of(b), :] + jnp.transpose(total)).astype(BF16)


def last_kernel(index_ref, weight_ref, other_ref, self_ref, neigh_ref):
    me = index_ref[index_ref.shape[0] - 1]
    first = me % 2 == 0
    chip = me // 2 % 4
    rows = weight_ref.shape[2]
    for p in range(4):
        span = pl.ds(pl.multiple_of((chip ^ p) * rows, rows), rows)
        mine, other = weight_ref[p % 2, p // 2], other_ref[p % 2, p // 2]
        self_ref[span, :] = jnp.where(first, mine, other)
        neigh_ref[span, :] = jnp.where(first, other, mine)


def body(features, tiles, tile_row, tile_col, degree, train_mask, w_self, w_neigh, cotangent):
    n = lax.axis_size("row")
    me = lax.axis_index("row").astype(jnp.int32).reshape(1)
    squares = n // 8
    nodes, feat_in = features.shape
    hidden = w_self.shape[1]
    block_local = nodes // BLOCK
    tile_count = tiles.shape[0]
    group = max(g for g in range(1, 11) if tile_count % g == 0)
    small = n * nodes * feat_in * 4 <= 4 * MIB
    limit = (24 if small else 56) * MIB

    def result(shape, dtype, stays=True):
        kind = pltpu.VMEM if small and stays else jax.ShapeDtypeStruct
        return kind(shape, dtype)

    def placed(x, spec):
        if spec is SMEM or not small:
            return x
        return pltpu.with_memory_space_constraint(x, pltpu.HBM if spec is ANY else pltpu.VMEM)

    def call(kernel, name, out_shape, operands, in_specs=None, out_specs=None, cost_us=0.2, **more):
        specs = in_specs or [VMEM] * len(operands)
        return pl.pallas_call(
            kernel,
            out_shape=out_shape,
            in_specs=specs,
            out_specs=out_specs or jax.tree.map(lambda _: VMEM, out_shape),
            compiler_params=pltpu.CompilerParams(vmem_limit_bytes=limit),
            cost_estimate=pl.CostEstimate(
                flops=int(cost_us * 1.1e9), bytes_accessed=int(cost_us * 3.6e6), transcendentals=0),
            name=name,
            **more,
        )(*[placed(x, spec) for x, spec in zip(operands, specs)])

    wide, piece = result((nodes, feat_in), F32), result((nodes, feat_in), BF16)
    weight = result((feat_in, hidden), F32)
    chunk = result((feat_in // 4, hidden), F32)
    by_block = (block_local, BLOCK, feat_in)

    own_arguments = (
        degree.reshape(block_local, BLOCK), train_mask.reshape(block_local, BLOCK),
        w_self, w_neigh, features, cotangent,
    )
    if small:
        own_arguments = [pltpu.with_memory_space_constraint(x, pltpu.HBM) for x in own_arguments]
    tiles_near, ws, wn, inverse, upstream, pre_self, feat_t, own, index = pl.pallas_call(
        functools.partial(stage_kernel, (8 * block_local, (n - 8) * block_local)),
        out_shape=(
            result(tiles.shape, BF16),
            result(w_self.shape, BF16),
            result(w_neigh.shape, BF16),
            result(by_block, F32),
            result((nodes, hidden), F32),
            result((nodes, hidden), F32),
            result(by_block, BF16),
            piece,
            pltpu.SMEM((6 * tile_count + 3,), jnp.int32),
        ),
        in_specs=[SMEM] * 3 + [VMEM] * 6 + [ANY],
        out_specs=(VMEM,) * 8 + (SMEM,),
        scratch_shapes=[pltpu.SemaphoreType.DMA],
        compiler_params=pltpu.CompilerParams(vmem_limit_bytes=limit),
        cost_estimate=pl.CostEstimate(flops=int(3 * 1.1e9), bytes_accessed=int(3 * 3.6e6), transcendentals=0),
        name="stage_arguments",
    )(me, tile_row, tile_col, *own_arguments, placed(tiles, ANY))

    same, other = gather_by_xor(features, own, n, call, result((4, nodes, feat_in), BF16))
    near_square = (8 * block_local, BLOCK, feat_in)
    far_squares = ((n - 8) * block_local, BLOCK, feat_in)
    raw_shape = (block_local + 1, BLOCK, feat_in)
    raw = call(
        functools.partial(forward_near_kernel, group), "forward_near", result(raw_shape, F32),
        (index, tiles_near, same[0], other[0]), [SMEM] + [VMEM] * 3, cost_us=0.1,
        scratch_shapes=[pltpu.VMEM(near_square, BF16)],
    )
    operands = (index, tiles_near, wn, inverse, upstream, pre_self, raw, *same[1:], *other[1:])
    wide_out = result((nodes, hidden), BF16)
    embedded, high, low, scaled, gt, raw = call(
        functools.partial(forward_kernel, group, squares - 1),
        "forward_layer",
        (
            result((nodes, hidden), BF16, False), wide_out, wide_out, wide_out,
            result((block_local, 2 * feat_in, BLOCK), BF16), result(raw_shape, F32),
        ),
        operands,
        [SMEM] + [VMEM] * (len(operands) - 1),
        cost_us=3,
        scratch_shapes=[pltpu.VMEM(far_squares, BF16)],
    )

    wkeep, wsend = call(
        weights_kernel, "weights", (weight, weight),
        (index, high, low, scaled, raw, feat_t), [SMEM] + [VMEM] * 5, cost_us=1,
        scratch_shapes=[pltpu.VMEM((2, feat_in, hidden), F32)])
    w0, w1, w2, w3 = call(
        cut_kernel, "cut_weights", (chunk,) * 4, (index, wkeep, swap(wsend, n, 1)),
        [SMEM, VMEM, VMEM])

    send_shape = result((4, nodes, feat_in), F32)
    sums, got = [], [None] * squares
    for section, shape in ((1, far_squares), (0, near_square)):
        acc = call(
            functools.partial(backward_kernel, section, group), "backward_tiles",
            result((shape[0] + 1,) + shape[1:], F32), (index, tiles_near, gt, wkeep),
            [SMEM] + [VMEM] * 3, cost_us=1.5 if section else 0.3)
        sums.insert(0, acc)
        for s in range(squares - 1, 0, -1) if section else (0,):
            operands = (acc, wkeep if section else w0)
            send = call(functools.partial(send_kernel, s - section), "send", send_shape, operands)
            got[s] = swap(send, n, 1)

    extra = result((nodes + 2 * chunk.shape[0] * (hidden // feat_in), feat_in), BF16)
    terms = [[]]
    for s in range(1, squares):
        operands = (sums[1], got[s])
        if s == squares - 1:
            own, *pieces = call(
                functools.partial(pair_weights_kernel, s - 1), "pair_sum_weights",
                (wide, extra, extra, extra), operands + (w1, w2, w3))
        else:
            own, *pieces = call(
                functools.partial(pair_kernel, s - 1, range(4)), "pair_sum",
                (wide, piece, piece, piece), operands)
        terms.append([own, *[swap(pieces[q - 1], n, 2 * q) for q in (3, 1, 2)]])
    near_operands = (sums[0], got[0])
    own, *pieces = call(
        functools.partial(pair_kernel, 0, (0, 3)), "pair_sum", (wide, piece), near_operands)
    near = [own, swap(pieces[0], n, 6)]
    distance = 1
    while distance < squares:
        for s in range(squares - distance, 0, -2 * distance):
            if s == squares - 1:
                total, wsum = call(
                    add_weights_kernel, "square_sum_weights", (piece, chunk), (w0, *terms[s]),
                    cost_us=SQUARE_COST)
            else:
                total = call(add_kernel, "square_sum", piece, terms[s], cost_us=SQUARE_COST)
            terms[s - distance].append(swap(total, n, 8 * distance))
        distance *= 2
    bit = 8
    while bit < n:
        wsum = call(add_two_kernel, "weight_sum", chunk, (wsum, swap(wsum, n, bit), near[1]))
        bit *= 2
    rows = chunk.shape[0]
    two = call(functools.partial(pack_kernel, (0, 1)), "pack_weights", result((2, rows, hidden), F32), (wsum, swap(wsum, n, 4)))
    along_z, along_y = call(
        functools.partial(pair_kernel, 0, (2, 1)), "pair_sum_later", (piece, piece),
        near_operands + (two,))
    near += [swap(along_z, n, 4), swap(along_y, n, 2)]
    near_total = call(near_kernel, "near_sum", wide, (high, low, ws, *near), cost_us=NEAR_COST)
    mine = call(
        functools.partial(pack_kernel, (0, 1)), "pack_weights", result((2, 2, rows, hidden), F32), (two, swap(two, n, 2)))
    from_far = [
        call(add_kernel, "far_sum", wide, (x,), cost_us=FAR_COST) for x in terms[0]]
    grad_input = call(
        main_kernel, "grad_input_sum", result((nodes, feat_in), BF16, False), (near_total, *from_far),
        cost_us=MAIN_COST)
    full = result((feat_in, hidden), F32, False)
    grad_self, grad_neigh = call(
        last_kernel, "write_weights", (full, full), (index, mine, swap(mine, n, 1)),
        [SMEM] + [VMEM] * 2)
    return (embedded, grad_input, grad_self, grad_neigh)


def solution(mesh):
    placed = (
        P(("parts", "row"), None),
        P(("parts", "row"), None, None),
        P(("parts", "row")),
        P(("parts", "row")),
        P(("parts", "row")),
        P(("parts", "row")),
        P(),
        P(),
        P(("parts", "row"), None),
    )
    return jax.shard_map(
        body,
        mesh=mesh,
        in_specs=placed,
        out_specs=(
            P(("parts", "row"), None),
            P(("parts", "row"), None),
            P("parts", None),
            P("parts", None),
        ),
        check_vma=False,
    )
```

```python
import functools

import jax
import jax.numpy as jnp
from jax import lax
from jax.experimental import pallas as pl
from jax.experimental.pallas import tpu as pltpu
from jax.sharding import PartitionSpec as P

BLOCK = 128
F32, BF16 = jnp.float32, jnp.bfloat16
VMEM = pl.BlockSpec(memory_space=pltpu.VMEM)
SMEM = pl.BlockSpec(memory_space=pltpu.SMEM)
ANY = pl.BlockSpec(memory_space=pl.ANY)
MIB = 1024 * 1024
LAST = ((1,), (1,))
NEAR_COST, SQUARE_COST, MAIN_COST = 0.2, 4, 10


def swap(x, n, offset):
    return lax.ppermute(x, "row", [(i, i ^ offset) for i in range(n)])


def gather_by_xor(x, own, n, call, pack):
    blocks = [x]
    bit = n // 2
    while bit >= 8:
        blocks = blocks + [swap(v, n, bit) for v in blocks]
        bit //= 2
    offsets = [0]
    bit = n // 2
    while bit >= 8:
        offsets = offsets + [o ^ bit for o in offsets]
        bit //= 2
    blocks = [v for _, v in sorted(zip(offsets, blocks), key=lambda pair: pair[0])]
    same = []
    for v in blocks:
        order = (2, 6, 4) if v is x else (6, 2, 4)
        square = (own if v is x else v, *[swap(v, n, offset) for offset in order])
        slots = (0, *[offset // 2 for offset in order])
        same.append(call(functools.partial(pack_kernel, slots), "pack_square", pack, square))
    return same, [swap(v, n, 1) for v in same]


def split_bf16(x):
    high = x.astype(BF16)
    return high, (x - high.astype(F32)).astype(BF16)


def dot(a, b, dims=((1,), (0,))):
    return lax.dot_general(a, b, (dims, ((), ())), preferred_element_type=F32)


def dot_wide(a, b, dims=((1,), (0,))):
    high, low = split_bf16(a)
    return dot(high, b, dims) + dot(low, b, dims)


def rows_to_lanes(row):
    return jnp.transpose(jnp.broadcast_to(row, (BLOCK, BLOCK)))


def rows_of(b):
    return pl.ds(b * BLOCK, BLOCK)


def pack_kernel(slots, *refs):
    for slot, ref in zip(slots, refs[:-1]):
        refs[-1][slot] = ref[...]


def stage_kernel(dumps, me_ref, trow_ref, tcol_ref, deg_ref, mask_ref, ws_ref, wn_ref, feat_ref, cot_ref,
                 tiles_ref, tiles_out, ws_out, wn_out, inverse_out, up_out, pre_out, featt_out,
                 own_out, index_out, sem):
    copy = pltpu.make_async_copy(tiles_ref, tiles_out, sem)
    copy.start()
    block_local = feat_ref.shape[0] // BLOCK
    tile_count = trow_ref.shape[0]
    me = me_ref[0]
    index_out[index_out.shape[0] - 1] = me

    def clear(i, carry):
        for section in range(2):
            index_out[3 * section * tile_count + i] = 0
            index_out[(3 * section + 1) * tile_count + i] = block_local
            index_out[(3 * section + 2) * tile_count + i] = dumps[section]
        return carry

    def place(t, counts):
        col = tcol_ref[t]
        live = col >= 0
        col = jnp.maximum(col, 0)
        chip_core = (col // block_local) ^ me
        far = chip_core >= 8
        position = jnp.where(far, chip_core - 8, chip_core) * block_local + col % block_local
        row = jnp.clip(trow_ref[t] - me * block_local, 0, block_local - 1)
        near_count, far_count = counts
        spot = jnp.where(far, 3 * tile_count + far_count, near_count)

        @pl.when(live)
        def _():
            index_out[spot] = t
            index_out[spot + tile_count] = row
            index_out[spot + 2 * tile_count] = position

        add = live.astype(jnp.int32)
        add_far = far.astype(jnp.int32) * add
        return near_count + add - add_far, far_count + add_far

    lax.fori_loop(0, tile_count, clear, 0)
    near_count, far_count = lax.fori_loop(0, tile_count, place, (jnp.int32(0), jnp.int32(0)))
    index_out[6 * tile_count] = near_count
    index_out[6 * tile_count + 1] = far_count
    own_out[...] = feat_ref[...]
    ws_out[...] = ws_ref[...]
    wn_out[...] = wn_ref[...]
    ws = ws_ref[...]
    for b in range(block_local):
        degree = rows_to_lanes(deg_ref[pl.ds(b, 1), :].astype(F32))
        mask = rows_to_lanes(mask_ref[pl.ds(b, 1), :].astype(F32))
        inverse_out[b] = 1.0 / degree
        feat = feat_ref[rows_of(b), :]
        featt_out[b] = jnp.transpose(feat.astype(F32)).astype(BF16)
        pre_out[rows_of(b), :] = dot(feat, ws)
        up_out[rows_of(b), :] = cot_ref[rows_of(b), :].astype(F32) * jnp.concatenate(
            [mask, mask], axis=1)
    copy.wait()


def over_tiles(section, group, index_ref, product, add):
    tile_count = (index_ref.shape[0] - 3) // 6
    start = 3 * section * tile_count

    def step(i, carry):
        spots = [start + i * group + u for u in range(group)]
        entries = [
            (index_ref[spot], index_ref[spot + tile_count], index_ref[spot + 2 * tile_count])
            for spot in spots
        ]
        products = [product(*entry) for entry in entries]
        for entry, value in zip(entries, products):
            add(*entry, value)
        return carry

    count = index_ref[6 * tile_count + section]
    lax.fori_loop(0, (count + group - 1) // group, step, 0)


def gathered_products(section, group, index_ref, tiles_ref, feat_refs, feats, raw):
    squares = len(feat_refs) // 2
    block_local = raw.shape[0] - 1
    for s in range(squares):
        for q in range(4):
            for core in range(2):
                for b in range(block_local):
                    spot = (8 * s + 2 * q + core) * block_local + b
                    feats[spot] = feat_refs[core * squares + s][q, rows_of(b), :]

    def add(t, row, position, value):
        raw[row] += value

    over_tiles(
        section, group, index_ref,
        lambda t, row, position: dot(tiles_ref[t], feats[jnp.minimum(position, feats.shape[0] - 1)]),
        add)


def forward_near_kernel(group, index_ref, tiles_ref, same_ref, other_ref, raw, feats):
    raw[...] = jnp.zeros_like(raw)
    gathered_products(0, group, index_ref, tiles_ref, (same_ref, other_ref), feats, raw)


def forward_kernel(group, far, index_ref, tiles_ref, wn_ref, inverse_ref, up_ref, pre_ref,
                   near_ref, *refs):
    feat_refs, refs = refs[:2 * far], refs[2 * far:]
    emb_ref, high_ref, low_ref, scaled_ref, gt_ref, raw, feats = refs
    block_local = inverse_ref.shape[0]
    raw[...] = near_ref[...]
    gathered_products(1, group, index_ref, tiles_ref, feat_refs, feats, raw)
    wn = wn_ref[...]
    for b in range(block_local):
        inverse = inverse_ref[b]
        pre = pre_ref[rows_of(b), :] + dot_wide(raw[b] * inverse, wn)
        sig = jax.nn.sigmoid(pre)
        emb_ref[rows_of(b), :] = (pre * sig).astype(BF16)
        grad_pre = up_ref[rows_of(b), :] * sig * (1.0 + pre * (1.0 - sig))
        scaled = (grad_pre * jnp.concatenate([inverse, inverse], axis=1)).astype(BF16)
        scaled_ref[rows_of(b), :] = scaled
        high_ref[rows_of(b), :], low_ref[rows_of(b), :] = split_bf16(grad_pre)
        high, low = split_bf16(dot(wn, scaled, LAST))
        gt_ref[b, :BLOCK, :] = high
        gt_ref[b, BLOCK:, :] = low


def weights_kernel(index_ref, high_ref, low_ref, scaled_ref, raw_ref, featt_ref, *refs):
    wkeep_ref, wsend_ref, wsum = refs[-3:]
    for b in range(featt_ref.shape[0]):
        feat_t = featt_ref[b]
        grad_self = dot(feat_t, high_ref[rows_of(b), :]) + dot(feat_t, low_ref[rows_of(b), :])
        grad_neigh = dot_wide(jnp.transpose(raw_ref[b]), scaled_ref[rows_of(b), :])
        if b == 0:
            wsum[0], wsum[1] = grad_self, grad_neigh
        else:
            wsum[0] += grad_self
            wsum[1] += grad_neigh
    core = index_ref[index_ref.shape[0] - 1] % 2
    wkeep_ref[...] = wsum[core]
    wsend_ref[...] = wsum[1 - core]


def backward_kernel(section, group, index_ref, tiles_ref, gt_ref, *refs):
    acc_ref = refs[-1]
    block_local = gt_ref.shape[0]
    acc_ref[...] = jnp.zeros_like(acc_ref)

    def product(t, row, position):
        both = dot(gt_ref[jnp.minimum(row, block_local - 1)], tiles_ref[t])
        return both[:BLOCK] + both[BLOCK:]

    def add(t, row, position, value):
        acc_ref[position] += value

    over_tiles(section, group, index_ref, product, add)


def send_kernel(square, acc_ref, *refs):
    send_ref = refs[-1]
    block_local = send_ref.shape[1] // BLOCK
    for q in range(4):
        for b in range(block_local):
            send_ref[q, rows_of(b), :] = acc_ref[(8 * square + 2 * q + 1) * block_local + b]


def cut_kernel(index_ref, wkeep_ref, wgot_ref, *parts):
    rows = parts[0].shape[0]
    chip = index_ref[index_ref.shape[0] - 1] // 2 % 4
    for p, ref in enumerate(parts):
        span = pl.ds(pl.multiple_of((chip ^ p) * rows, rows), rows)
        ref[...] = wkeep_ref[span, :] + wgot_ref[span, :]


def pair_kernel(square, chips, acc_ref, got_ref, *refs):
    refs = refs[-len(chips):]
    block_local = got_ref.shape[1] // BLOCK
    for q, ref in zip(chips, refs):
        for b in range(block_local):
            kept = acc_ref[(8 * square + 2 * q) * block_local + b]
            ref[rows_of(b), :] = (kept + got_ref[q, rows_of(b), :]).astype(ref.dtype)


def pair_weights_kernel(square, acc_ref, got_ref, w1, w2, w3, own_ref, *pieces):
    pair_kernel(square, range(4), acc_ref, got_ref, own_ref, *pieces)
    nodes, lanes = own_ref.shape
    for weight_ref, ref in zip((w1, w2, w3), pieces):
        rows, columns = weight_ref.shape
        start = nodes
        for column in range(0, columns, lanes):
            ref[pl.ds(start, rows), :] = weight_ref[:, column:column + lanes].astype(BF16)
            start += rows


def add_two_kernel(own_ref, got_ref, out_ref):
    out_ref[...] = own_ref[...] + got_ref[...]


def add_kernel(own_ref, *refs):
    total = own_ref[...]
    for got_ref in refs[:-1]:
        total = total + got_ref[...].astype(F32)
    refs[-1][...] = total.astype(BF16)


def add_weights_kernel(weight_ref, own_ref, *refs):
    got_refs, (out_ref, weight_out) = refs[:-2], refs[-2:]
    nodes, lanes = own_ref.shape
    add_kernel(own_ref, *[ref.at[pl.ds(0, nodes), :] for ref in got_refs], out_ref)
    rows, columns = weight_ref.shape
    for cut in range(columns // lanes):
        span = pl.ds(cut * lanes, lanes)
        total = weight_ref[:, span]
        for ref in got_refs[:3]:
            total = total + ref[pl.ds(nodes + cut * rows, rows), :].astype(F32)
        weight_out[:, span] = total


def near_kernel(high_ref, low_ref, ws_ref, own_ref, *refs):
    ws = ws_ref[...]
    for b in range(own_ref.shape[0] // BLOCK):
        total = own_ref[rows_of(b), :]
        for got_ref in refs[:-1]:
            total = total + got_ref[rows_of(b), :].astype(F32)
        base = dot(high_ref[rows_of(b), :], ws, LAST) + dot(low_ref[rows_of(b), :], ws, LAST)
        refs[-1][rows_of(b), :] = base + jnp.transpose(total)


def main_kernel(near_ref, *refs):
    for b in range(near_ref.shape[0] // BLOCK):
        total = refs[0][rows_of(b), :].astype(F32)
        for got_ref in refs[1:-1]:
            total = total + got_ref[rows_of(b), :].astype(F32)
        refs[-1][rows_of(b), :] = (near_ref[rows_of(b), :] + jnp.transpose(total)).astype(BF16)


def last_kernel(index_ref, weight_ref, other_ref, self_ref, neigh_ref):
    me = index_ref[index_ref.shape[0] - 1]
    first = me % 2 == 0
    chip = me // 2 % 4
    rows = weight_ref.shape[2]
    for p in range(4):
        span = pl.ds(pl.multiple_of((chip ^ p) * rows, rows), rows)
        mine, other = weight_ref[p % 2, p // 2], other_ref[p % 2, p // 2]
        self_ref[span, :] = jnp.where(first, mine, other)
        neigh_ref[span, :] = jnp.where(first, other, mine)


def body(features, tiles, tile_row, tile_col, degree, train_mask, w_self, w_neigh, cotangent):
    n = lax.axis_size("row")
    me = lax.axis_index("row").astype(jnp.int32).reshape(1)
    squares = n // 8
    nodes, feat_in = features.shape
    hidden = w_self.shape[1]
    block_local = nodes // BLOCK
    tile_count = tiles.shape[0]
    group = max(g for g in range(1, 11) if tile_count % g == 0)
    small = n * nodes * feat_in * 4 <= 4 * MIB
    limit = (24 if small else 56) * MIB

    def result(shape, dtype, stays=True):
        kind = pltpu.VMEM if small and stays else jax.ShapeDtypeStruct
        return kind(shape, dtype)

    def placed(x, spec):
        if spec is SMEM or not small:
            return x
        return pltpu.with_memory_space_constraint(x, pltpu.HBM if spec is ANY else pltpu.VMEM)

    def call(kernel, name, out_shape, operands, in_specs=None, out_specs=None, cost_us=0.2, **more):
        specs = in_specs or [VMEM] * len(operands)
        return pl.pallas_call(
            kernel,
            out_shape=out_shape,
            in_specs=specs,
            out_specs=out_specs or jax.tree.map(lambda _: VMEM, out_shape),
            compiler_params=pltpu.CompilerParams(vmem_limit_bytes=limit),
            cost_estimate=pl.CostEstimate(
                flops=int(cost_us * 1.1e9), bytes_accessed=int(cost_us * 3.6e6), transcendentals=0),
            name=name,
            **more,
        )(*[placed(x, spec) for x, spec in zip(operands, specs)])

    wide, piece = result((nodes, feat_in), F32), result((nodes, feat_in), BF16)
    weight = result((feat_in, hidden), F32)
    chunk = result((feat_in // 4, hidden), F32)
    by_block = (block_local, BLOCK, feat_in)

    own_arguments = (
        degree.reshape(block_local, BLOCK), train_mask.reshape(block_local, BLOCK),
        w_self, w_neigh, features, cotangent,
    )
    if small:
        own_arguments = [pltpu.with_memory_space_constraint(x, pltpu.HBM) for x in own_arguments]
    tiles_near, ws, wn, inverse, upstream, pre_self, feat_t, own, index = pl.pallas_call(
        functools.partial(stage_kernel, (8 * block_local, (n - 8) * block_local)),
        out_shape=(
            result(tiles.shape, BF16),
            result(w_self.shape, BF16),
            result(w_neigh.shape, BF16),
            result(by_block, F32),
            result((nodes, hidden), F32),
            result((nodes, hidden), F32),
            result(by_block, BF16),
            piece,
            pltpu.SMEM((6 * tile_count + 3,), jnp.int32),
        ),
        in_specs=[SMEM] * 3 + [VMEM] * 6 + [ANY],
        out_specs=(VMEM,) * 8 + (SMEM,),
        scratch_shapes=[pltpu.SemaphoreType.DMA],
        compiler_params=pltpu.CompilerParams(vmem_limit_bytes=limit),
        cost_estimate=pl.CostEstimate(flops=int(3 * 1.1e9), bytes_accessed=int(3 * 3.6e6), transcendentals=0),
        name="stage_arguments",
    )(me, tile_row, tile_col, *own_arguments, placed(tiles, ANY))

    same, other = gather_by_xor(features, own, n, call, result((4, nodes, feat_in), BF16))
    near_square = (8 * block_local, BLOCK, feat_in)
    far_squares = ((n - 8) * block_local, BLOCK, feat_in)
    raw_shape = (block_local + 1, BLOCK, feat_in)
    raw = call(
        functools.partial(forward_near_kernel, group), "forward_near", result(raw_shape, F32),
        (index, tiles_near, same[0], other[0]), [SMEM] + [VMEM] * 3, cost_us=0.1,
        scratch_shapes=[pltpu.VMEM(near_square, BF16)],
    )
    operands = (index, tiles_near, wn, inverse, upstream, pre_self, raw, *same[1:], *other[1:])
    wide_out = result((nodes, hidden), BF16)
    embedded, high, low, scaled, gt, raw = call(
        functools.partial(forward_kernel, group, squares - 1),
        "forward_layer",
        (
            result((nodes, hidden), BF16, False), wide_out, wide_out, wide_out,
            result((block_local, 2 * feat_in, BLOCK), BF16), result(raw_shape, F32),
        ),
        operands,
        [SMEM] + [VMEM] * (len(operands) - 1),
        cost_us=3,
        scratch_shapes=[pltpu.VMEM(far_squares, BF16)],
    )

    wkeep, wsend = call(
        weights_kernel, "weights", (weight, weight),
        (index, high, low, scaled, raw, feat_t), [SMEM] + [VMEM] * 5, cost_us=1,
        scratch_shapes=[pltpu.VMEM((2, feat_in, hidden), F32)])
    w0, w1, w2, w3 = call(
        cut_kernel, "cut_weights", (chunk,) * 4, (index, wkeep, swap(wsend, n, 1)),
        [SMEM, VMEM, VMEM])

    send_shape = result((4, nodes, feat_in), F32)
    sums, got = [], [None] * squares
    for section, shape in ((1, far_squares), (0, near_square)):
        acc = call(
            functools.partial(backward_kernel, section, group), "backward_tiles",
            result((shape[0] + 1,) + shape[1:], F32), (index, tiles_near, gt, wkeep),
            [SMEM] + [VMEM] * 3, cost_us=1.5 if section else 0.3)
        sums.insert(0, acc)
        for s in range(squares - 1, 0, -1) if section else (0,):
            operands = (acc, wkeep if section else w0)
            send = call(functools.partial(send_kernel, s - section), "send", send_shape, operands)
            got[s] = swap(send, n, 1)

    extra = result((nodes + chunk.shape[0] * (hidden // feat_in), feat_in), BF16)
    terms = [[]]
    for s in range(1, squares):
        operands = (sums[1], got[s])
        if s == squares - 1:
            own, *pieces = call(
                functools.partial(pair_weights_kernel, s - 1), "pair_sum_weights",
                (wide, extra, extra, extra), operands + (w1, w2, w3))
        else:
            own, *pieces = call(
                functools.partial(pair_kernel, s - 1, range(4)), "pair_sum",
                (wide, piece, piece, piece), operands)
        terms.append([own, *[swap(pieces[q - 1], n, 2 * q) for q in (3, 1, 2)]])
    near_operands = (sums[0], got[0])
    own, *pieces = call(
        functools.partial(pair_kernel, 0, (0, 3, 1)), "pair_sum", (wide, piece, piece),
        near_operands)
    near = [own, swap(pieces[0], n, 6), swap(pieces[1], n, 2)]
    distance = 1
    while distance < squares:
        for s in range(squares - distance, 0, -2 * distance):
            if s == squares - 1:
                total, wsum = call(
                    add_weights_kernel, "square_sum_weights", (piece, chunk), (w0, *terms[s]),
                    cost_us=SQUARE_COST)
            else:
                total = call(add_kernel, "square_sum", piece, terms[s], cost_us=SQUARE_COST)
            terms[s - distance].append(swap(total, n, 8 * distance))
        distance *= 2
    later = call(
        functools.partial(pair_kernel, 0, (2,)), "pair_sum_later", piece, near_operands + (total,))
    near.append(swap(later, n, 4))
    near_total = call(near_kernel, "near_sum", wide, (high, low, ws, *near), cost_us=NEAR_COST)
    terms[0].insert(0, near_total)
    bit = 8
    while bit < n:
        wsum = call(add_two_kernel, "weight_sum", chunk, (wsum, swap(wsum, n, bit)))
        bit *= 2
    rows = chunk.shape[0]
    two = call(functools.partial(pack_kernel, (0, 1)), "pack_weights", result((2, rows, hidden), F32), (wsum, swap(wsum, n, 4)))
    mine = call(
        functools.partial(pack_kernel, (0, 1)), "pack_weights", result((2, 2, rows, hidden), F32), (two, swap(two, n, 2), near_total))
    grad_input = call(
        main_kernel, "grad_input_sum", result((nodes, feat_in), BF16, False), terms[0],
        cost_us=MAIN_COST)
    full = result((feat_in, hidden), F32, False)
    grad_self, grad_neigh = call(
        last_kernel, "write_weights", (full, full), (index, mine, swap(mine, n, 1)),
        [SMEM] + [VMEM] * 2)
    return (embedded, grad_input, grad_self, grad_neigh)


def solution(mesh):
    placed = (
        P(("parts", "row"), None),
        P(("parts", "row"), None, None),
        P(("parts", "row")),
        P(("parts", "row")),
        P(("parts", "row")),
        P(("parts", "row")),
        P(),
        P(),
        P(("parts", "row"), None),
    )
    return jax.shard_map(
        body,
        mesh=mesh,
        in_specs=placed,
        out_specs=(
            P(("parts", "row"), None),
            P(("parts", "row"), None),
            P("parts", None),
            P("parts", None),
        ),
        check_vma=False,
    )
```

```python
import functools

import jax
import jax.numpy as jnp
from jax import lax
from jax.experimental import pallas as pl
from jax.experimental.pallas import tpu as pltpu
from jax.sharding import PartitionSpec as P

BLOCK = 128
F32, BF16 = jnp.float32, jnp.bfloat16
VMEM = pl.BlockSpec(memory_space=pltpu.VMEM)
SMEM = pl.BlockSpec(memory_space=pltpu.SMEM)
ANY = pl.BlockSpec(memory_space=pl.ANY)
MIB = 1024 * 1024
LAST = ((1,), (1,))
NEAR_COST, SQUARE_COST, MAIN_COST = 0.2, 4, 10


def swap(x, n, offset):
    return lax.ppermute(x, "row", [(i, i ^ offset) for i in range(n)])


def gather_by_xor(x, own, n, call, pack):
    blocks = [x]
    bit = n // 2
    while bit >= 8:
        blocks = blocks + [swap(v, n, bit) for v in blocks]
        bit //= 2
    offsets = [0]
    bit = n // 2
    while bit >= 8:
        offsets = offsets + [o ^ bit for o in offsets]
        bit //= 2
    blocks = [v for _, v in sorted(zip(offsets, blocks), key=lambda pair: pair[0])]
    same = []
    for v in blocks:
        order = (2, 6, 4) if v is x else (6, 2, 4)
        square = (own if v is x else v, *[swap(v, n, offset) for offset in order])
        slots = (0, *[offset // 2 for offset in order])
        same.append(call(functools.partial(pack_kernel, slots), "pack_square", pack, square))
    return same, [swap(v, n, 1) for v in same]


def split_bf16(x):
    high = x.astype(BF16)
    return high, (x - high.astype(F32)).astype(BF16)


def dot(a, b, dims=((1,), (0,))):
    return lax.dot_general(a, b, (dims, ((), ())), preferred_element_type=F32)


def dot_wide(a, b, dims=((1,), (0,))):
    high, low = split_bf16(a)
    return dot(high, b, dims) + dot(low, b, dims)


def rows_to_lanes(row):
    return jnp.transpose(jnp.broadcast_to(row, (BLOCK, BLOCK)))


def rows_of(b):
    return pl.ds(b * BLOCK, BLOCK)


def pack_kernel(slots, *refs):
    for slot, ref in zip(slots, refs[:-1]):
        refs[-1][slot] = ref[...]


def stage_kernel(dumps, me_ref, trow_ref, tcol_ref, deg_ref, mask_ref, ws_ref, wn_ref, feat_ref, cot_ref,
                 tiles_ref, tiles_out, ws_out, wn_out, inverse_out, up_out, pre_out, featt_out,
                 own_out, index_out, sem):
    copy = pltpu.make_async_copy(tiles_ref, tiles_out, sem)
    copy.start()
    block_local = feat_ref.shape[0] // BLOCK
    tile_count = trow_ref.shape[0]
    me = me_ref[0]
    index_out[index_out.shape[0] - 1] = me

    def clear(i, carry):
        for section in range(2):
            index_out[3 * section * tile_count + i] = 0
            index_out[(3 * section + 1) * tile_count + i] = block_local
            index_out[(3 * section + 2) * tile_count + i] = dumps[section]
        return carry

    def place(t, counts):
        col = tcol_ref[t]
        live = col >= 0
        col = jnp.maximum(col, 0)
        chip_core = (col // block_local) ^ me
        far = chip_core >= 8
        position = jnp.where(far, chip_core - 8, chip_core) * block_local + col % block_local
        row = jnp.clip(trow_ref[t] - me * block_local, 0, block_local - 1)
        near_count, far_count = counts
        spot = jnp.where(far, 3 * tile_count + far_count, near_count)

        @pl.when(live)
        def _():
            index_out[spot] = t
            index_out[spot + tile_count] = row
            index_out[spot + 2 * tile_count] = position

        add = live.astype(jnp.int32)
        add_far = far.astype(jnp.int32) * add
        return near_count + add - add_far, far_count + add_far

    lax.fori_loop(0, tile_count, clear, 0)
    near_count, far_count = lax.fori_loop(0, tile_count, place, (jnp.int32(0), jnp.int32(0)))
    index_out[6 * tile_count] = near_count
    index_out[6 * tile_count + 1] = far_count
    own_out[...] = feat_ref[...]
    ws_out[...] = ws_ref[...]
    wn_out[...] = wn_ref[...]
    ws = ws_ref[...]
    for b in range(block_local):
        degree = rows_to_lanes(deg_ref[pl.ds(b, 1), :].astype(F32))
        mask = rows_to_lanes(mask_ref[pl.ds(b, 1), :].astype(F32))
        inverse_out[b] = 1.0 / degree
        feat = feat_ref[rows_of(b), :]
        featt_out[b] = jnp.transpose(feat.astype(F32)).astype(BF16)
        pre_out[rows_of(b), :] = dot(feat, ws)
        up_out[rows_of(b), :] = cot_ref[rows_of(b), :].astype(F32) * jnp.concatenate(
            [mask, mask], axis=1)
    copy.wait()


def over_tiles(section, group, index_ref, product, add):
    tile_count = (index_ref.shape[0] - 3) // 6
    start = 3 * section * tile_count

    def step(i, carry):
        spots = [start + i * group + u for u in range(group)]
        entries = [
            (index_ref[spot], index_ref[spot + tile_count], index_ref[spot + 2 * tile_count])
            for spot in spots
        ]
        products = [product(*entry) for entry in entries]
        for entry, value in zip(entries, products):
            add(*entry, value)
        return carry

    count = index_ref[6 * tile_count + section]
    lax.fori_loop(0, (count + group - 1) // group, step, 0)


def gathered_products(section, group, index_ref, tiles_ref, feat_refs, feats, raw):
    squares = len(feat_refs) // 2
    block_local = raw.shape[0] - 1
    for s in range(squares):
        for q in range(4):
            for core in range(2):
                for b in range(block_local):
                    spot = (8 * s + 2 * q + core) * block_local + b
                    feats[spot] = feat_refs[core * squares + s][q, rows_of(b), :]

    def add(t, row, position, value):
        raw[row] += value

    over_tiles(
        section, group, index_ref,
        lambda t, row, position: dot(tiles_ref[t], feats[jnp.minimum(position, feats.shape[0] - 1)]),
        add)


def forward_near_kernel(group, index_ref, tiles_ref, same_ref, other_ref, raw, feats):
    raw[...] = jnp.zeros_like(raw)
    gathered_products(0, group, index_ref, tiles_ref, (same_ref, other_ref), feats, raw)


def forward_kernel(group, far, index_ref, tiles_ref, wn_ref, inverse_ref, up_ref, pre_ref,
                   near_ref, *refs):
    feat_refs, refs = refs[:2 * far], refs[2 * far:]
    emb_ref, high_ref, low_ref, scaled_ref, gt_ref, raw, feats = refs
    block_local = inverse_ref.shape[0]
    raw[...] = near_ref[...]
    gathered_products(1, group, index_ref, tiles_ref, feat_refs, feats, raw)
    wn = wn_ref[...]
    for b in range(block_local):
        inverse = inverse_ref[b]
        pre = pre_ref[rows_of(b), :] + dot_wide(raw[b] * inverse, wn)
        sig = jax.nn.sigmoid(pre)
        emb_ref[rows_of(b), :] = (pre * sig).astype(BF16)
        grad_pre = up_ref[rows_of(b), :] * sig * (1.0 + pre * (1.0 - sig))
        scaled = (grad_pre * jnp.concatenate([inverse, inverse], axis=1)).astype(BF16)
        scaled_ref[rows_of(b), :] = scaled
        high_ref[rows_of(b), :], low_ref[rows_of(b), :] = split_bf16(grad_pre)
        high, low = split_bf16(dot(wn, scaled, LAST))
        gt_ref[b, :BLOCK, :] = high
        gt_ref[b, BLOCK:, :] = low


def weights_kernel(index_ref, high_ref, low_ref, scaled_ref, raw_ref, featt_ref, *refs):
    wkeep_ref, wsend_ref, wsum = refs[-3:]
    for b in range(featt_ref.shape[0]):
        feat_t = featt_ref[b]
        grad_self = dot(feat_t, high_ref[rows_of(b), :]) + dot(feat_t, low_ref[rows_of(b), :])
        grad_neigh = dot_wide(jnp.transpose(raw_ref[b]), scaled_ref[rows_of(b), :])
        if b == 0:
            wsum[0], wsum[1] = grad_self, grad_neigh
        else:
            wsum[0] += grad_self
            wsum[1] += grad_neigh
    core = index_ref[index_ref.shape[0] - 1] % 2
    wkeep_ref[...] = wsum[core]
    wsend_ref[...] = wsum[1 - core]


def backward_kernel(section, group, index_ref, tiles_ref, gt_ref, *refs):
    acc_ref = refs[-1]
    block_local = gt_ref.shape[0]
    acc_ref[...] = jnp.zeros_like(acc_ref)

    def product(t, row, position):
        both = dot(gt_ref[jnp.minimum(row, block_local - 1)], tiles_ref[t])
        return both[:BLOCK] + both[BLOCK:]

    def add(t, row, position, value):
        acc_ref[position] += value

    over_tiles(section, group, index_ref, product, add)


def send_kernel(square, acc_ref, *refs):
    send_ref = refs[-1]
    block_local = send_ref.shape[1] // BLOCK
    for q in range(4):
        for b in range(block_local):
            send_ref[q, rows_of(b), :] = acc_ref[(8 * square + 2 * q + 1) * block_local + b]


def cut_kernel(index_ref, wkeep_ref, wgot_ref, *parts):
    rows = parts[0].shape[0]
    chip = index_ref[index_ref.shape[0] - 1] // 2 % 4
    for p, ref in enumerate(parts):
        span = pl.ds(pl.multiple_of((chip ^ p) * rows, rows), rows)
        ref[...] = wkeep_ref[span, :] + wgot_ref[span, :]


def pair_kernel(square, chips, acc_ref, got_ref, *refs):
    refs = refs[-len(chips):]
    block_local = got_ref.shape[1] // BLOCK
    for q, ref in zip(chips, refs):
        for b in range(block_local):
            kept = acc_ref[(8 * square + 2 * q) * block_local + b]
            ref[rows_of(b), :] = (kept + got_ref[q, rows_of(b), :]).astype(ref.dtype)


def pair_weights_kernel(square, acc_ref, got_ref, w1, w2, w3, own_ref, *pieces):
    pair_kernel(square, range(4), acc_ref, got_ref, own_ref, *pieces)
    nodes, lanes = own_ref.shape
    for weight_ref, ref in zip((w1, w2, w3), pieces):
        rows, columns = weight_ref.shape
        start = nodes
        for part in split_bf16(weight_ref[...]):
            for column in range(0, columns, lanes):
                ref[pl.ds(start, rows), :] = part[:, column:column + lanes]
                start += rows


def add_two_kernel(own_ref, got_ref, out_ref):
    out_ref[...] = own_ref[...] + got_ref[...]


def add_kernel(own_ref, *refs):
    total = own_ref[...]
    for got_ref in refs[:-1]:
        total = total + got_ref[...].astype(F32)
    refs[-1][...] = total.astype(BF16)


def add_weights_kernel(weight_ref, own_ref, *refs):
    got_refs, (out_ref, weight_out) = refs[:-2], refs[-2:]
    nodes, lanes = own_ref.shape
    add_kernel(own_ref, *[ref.at[pl.ds(0, nodes), :] for ref in got_refs], out_ref)
    rows, columns = weight_ref.shape
    cuts = columns // lanes
    for cut in range(cuts):
        span = pl.ds(cut * lanes, lanes)
        total = weight_ref[:, span]
        for ref in got_refs[:3]:
            high = ref[pl.ds(nodes + cut * rows, rows), :]
            low = ref[pl.ds(nodes + (cuts + cut) * rows, rows), :]
            total = total + (high.astype(F32) + low.astype(F32))
        weight_out[:, span] = total


def near_kernel(high_ref, low_ref, ws_ref, own_ref, *refs):
    ws = ws_ref[...]
    for b in range(own_ref.shape[0] // BLOCK):
        total = own_ref[rows_of(b), :]
        for got_ref in refs[:-1]:
            total = total + got_ref[rows_of(b), :].astype(F32)
        base = dot(high_ref[rows_of(b), :], ws, LAST) + dot(low_ref[rows_of(b), :], ws, LAST)
        refs[-1][rows_of(b), :] = base + jnp.transpose(total)


def main_kernel(near_ref, *refs):
    for b in range(near_ref.shape[0] // BLOCK):
        total = refs[0][rows_of(b), :].astype(F32)
        for got_ref in refs[1:-1]:
            total = total + got_ref[rows_of(b), :].astype(F32)
        refs[-1][rows_of(b), :] = (near_ref[rows_of(b), :] + jnp.transpose(total)).astype(BF16)


def last_kernel(index_ref, weight_ref, other_ref, self_ref, neigh_ref):
    me = index_ref[index_ref.shape[0] - 1]
    first = me % 2 == 0
    chip = me // 2 % 4
    rows = weight_ref.shape[2]
    for p in range(4):
        span = pl.ds(pl.multiple_of((chip ^ p) * rows, rows), rows)
        mine, other = weight_ref[p % 2, p // 2], other_ref[p % 2, p // 2]
        self_ref[span, :] = jnp.where(first, mine, other)
        neigh_ref[span, :] = jnp.where(first, other, mine)


def body(features, tiles, tile_row, tile_col, degree, train_mask, w_self, w_neigh, cotangent):
    n = lax.axis_size("row")
    me = lax.axis_index("row").astype(jnp.int32).reshape(1)
    squares = n // 8
    nodes, feat_in = features.shape
    hidden = w_self.shape[1]
    block_local = nodes // BLOCK
    tile_count = tiles.shape[0]
    group = max(g for g in range(1, 11) if tile_count % g == 0)
    small = n * nodes * feat_in * 4 <= 4 * MIB
    limit = (24 if small else 56) * MIB

    def result(shape, dtype, stays=True):
        kind = pltpu.VMEM if small and stays else jax.ShapeDtypeStruct
        return kind(shape, dtype)

    def placed(x, spec):
        if spec is SMEM or not small:
            return x
        return pltpu.with_memory_space_constraint(x, pltpu.HBM if spec is ANY else pltpu.VMEM)

    def call(kernel, name, out_shape, operands, in_specs=None, out_specs=None, cost_us=0.2, **more):
        specs = in_specs or [VMEM] * len(operands)
        return pl.pallas_call(
            kernel,
            out_shape=out_shape,
            in_specs=specs,
            out_specs=out_specs or jax.tree.map(lambda _: VMEM, out_shape),
            compiler_params=pltpu.CompilerParams(vmem_limit_bytes=limit),
            cost_estimate=pl.CostEstimate(
                flops=int(cost_us * 1.1e9), bytes_accessed=int(cost_us * 3.6e6), transcendentals=0),
            name=name,
            **more,
        )(*[placed(x, spec) for x, spec in zip(operands, specs)])

    wide, piece = result((nodes, feat_in), F32), result((nodes, feat_in), BF16)
    weight = result((feat_in, hidden), F32)
    chunk = result((feat_in // 4, hidden), F32)
    by_block = (block_local, BLOCK, feat_in)

    own_arguments = (
        degree.reshape(block_local, BLOCK), train_mask.reshape(block_local, BLOCK),
        w_self, w_neigh, features, cotangent,
    )
    if small:
        own_arguments = [pltpu.with_memory_space_constraint(x, pltpu.HBM) for x in own_arguments]
    tiles_near, ws, wn, inverse, upstream, pre_self, feat_t, own, index = pl.pallas_call(
        functools.partial(stage_kernel, (8 * block_local, (n - 8) * block_local)),
        out_shape=(
            result(tiles.shape, BF16),
            result(w_self.shape, BF16),
            result(w_neigh.shape, BF16),
            result(by_block, F32),
            result((nodes, hidden), F32),
            result((nodes, hidden), F32),
            result(by_block, BF16),
            piece,
            pltpu.SMEM((6 * tile_count + 3,), jnp.int32),
        ),
        in_specs=[SMEM] * 3 + [VMEM] * 6 + [ANY],
        out_specs=(VMEM,) * 8 + (SMEM,),
        scratch_shapes=[pltpu.SemaphoreType.DMA],
        compiler_params=pltpu.CompilerParams(vmem_limit_bytes=limit),
        cost_estimate=pl.CostEstimate(flops=int(3 * 1.1e9), bytes_accessed=int(3 * 3.6e6), transcendentals=0),
        name="stage_arguments",
    )(me, tile_row, tile_col, *own_arguments, placed(tiles, ANY))

    same, other = gather_by_xor(features, own, n, call, result((4, nodes, feat_in), BF16))
    near_square = (8 * block_local, BLOCK, feat_in)
    far_squares = ((n - 8) * block_local, BLOCK, feat_in)
    raw_shape = (block_local + 1, BLOCK, feat_in)
    raw = call(
        functools.partial(forward_near_kernel, group), "forward_near", result(raw_shape, F32),
        (index, tiles_near, same[0], other[0]), [SMEM] + [VMEM] * 3, cost_us=0.1,
        scratch_shapes=[pltpu.VMEM(near_square, BF16)],
    )
    operands = (index, tiles_near, wn, inverse, upstream, pre_self, raw, *same[1:], *other[1:])
    wide_out = result((nodes, hidden), BF16)
    embedded, high, low, scaled, gt, raw = call(
        functools.partial(forward_kernel, group, squares - 1),
        "forward_layer",
        (
            result((nodes, hidden), BF16, False), wide_out, wide_out, wide_out,
            result((block_local, 2 * feat_in, BLOCK), BF16), result(raw_shape, F32),
        ),
        operands,
        [SMEM] + [VMEM] * (len(operands) - 1),
        cost_us=3,
        scratch_shapes=[pltpu.VMEM(far_squares, BF16)],
    )

    wkeep, wsend = call(
        weights_kernel, "weights", (weight, weight),
        (index, high, low, scaled, raw, feat_t), [SMEM] + [VMEM] * 5, cost_us=1,
        scratch_shapes=[pltpu.VMEM((2, feat_in, hidden), F32)])
    w0, w1, w2, w3 = call(
        cut_kernel, "cut_weights", (chunk,) * 4, (index, wkeep, swap(wsend, n, 1)),
        [SMEM, VMEM, VMEM])

    send_shape = result((4, nodes, feat_in), F32)
    sums, got = [], [None] * squares
    for section, shape in ((1, far_squares), (0, near_square)):
        acc = call(
            functools.partial(backward_kernel, section, group), "backward_tiles",
            result((shape[0] + 1,) + shape[1:], F32), (index, tiles_near, gt, wkeep),
            [SMEM] + [VMEM] * 3, cost_us=1.5 if section else 0.3)
        sums.insert(0, acc)
        for s in range(squares - 1, 0, -1) if section else (0,):
            operands = (acc, wkeep if section else w0)
            send = call(functools.partial(send_kernel, s - section), "send", send_shape, operands)
            got[s] = swap(send, n, 1)

    extra = result((nodes + 2 * chunk.shape[0] * (hidden // feat_in), feat_in), BF16)
    terms = [[]]
    for s in range(1, squares):
        operands = (sums[1], got[s])
        if s == squares - 1:
            own, *pieces = call(
                functools.partial(pair_weights_kernel, s - 1), "pair_sum_weights",
                (wide, extra, extra, extra), operands + (w1, w2, w3))
        else:
            own, *pieces = call(
                functools.partial(pair_kernel, s - 1, range(4)), "pair_sum",
                (wide, piece, piece, piece), operands)
        terms.append([own, *[swap(pieces[q - 1], n, 2 * q) for q in (1, 3, 2)]])
    near_operands = (sums[0], got[0])
    own, *pieces = call(
        functools.partial(pair_kernel, 0, (0, 3, 1)), "pair_sum", (wide, piece, piece),
        near_operands)
    near = [own, swap(pieces[0], n, 6), swap(pieces[1], n, 2)]
    distance = 1
    while distance < squares:
        for s in range(squares - distance, 0, -2 * distance):
            if s == squares - 1:
                total, wsum = call(
                    add_weights_kernel, "square_sum_weights", (piece, chunk), (w0, *terms[s]),
                    cost_us=SQUARE_COST)
            else:
                total = call(add_kernel, "square_sum", piece, terms[s], cost_us=SQUARE_COST)
            terms[s - distance].append(swap(total, n, 8 * distance))
        distance *= 2
    later = call(
        functools.partial(pair_kernel, 0, (2,)), "pair_sum_later", piece, near_operands + (total,))
    near.append(swap(later, n, 4))
    near_total = call(near_kernel, "near_sum", wide, (high, low, ws, *near), cost_us=NEAR_COST)
    terms[0].insert(0, near_total)
    bit = 8
    while bit < n:
        wsum = call(add_two_kernel, "weight_sum", chunk, (wsum, swap(wsum, n, bit)))
        bit *= 2
    rows = chunk.shape[0]
    two = call(functools.partial(pack_kernel, (0, 1)), "pack_weights", result((2, rows, hidden), F32), (wsum, swap(wsum, n, 4)))
    mine = call(
        functools.partial(pack_kernel, (0, 1)), "pack_weights", result((2, 2, rows, hidden), F32), (two, swap(two, n, 2), near_total))
    grad_input = call(
        main_kernel, "grad_input_sum", result((nodes, feat_in), BF16, False), terms[0],
        cost_us=MAIN_COST)
    full = result((feat_in, hidden), F32, False)
    grad_self, grad_neigh = call(
        last_kernel, "write_weights", (full, full), (index, mine, swap(mine, n, 1)),
        [SMEM] + [VMEM] * 2)
    return (embedded, grad_input, grad_self, grad_neigh)


def solution(mesh):
    placed = (
        P(("parts", "row"), None),
        P(("parts", "row"), None, None),
        P(("parts", "row")),
        P(("parts", "row")),
        P(("parts", "row")),
        P(("parts", "row")),
        P(),
        P(),
        P(("parts", "row"), None),
    )
    return jax.shard_map(
        body,
        mesh=mesh,
        in_specs=placed,
        out_specs=(
            P(("parts", "row"), None),
            P(("parts", "row"), None),
            P("parts", None),
            P("parts", None),
        ),
        check_vma=False,
    )
```
